512 devices in a mesh: leaf: 8 (over z_hi, y), row: 8 (over x, core), col: 8 (over z_lo).
Axes of the slice: x: 4, y: 4, z: 16 (z_hi: 2, z_lo: 8; z = z_hi * 8 + z_lo), core: 2. Of those that a mesh axis runs over, the one named last changes fastest.
Arguments:
- root_inverse: float32 [8192, 8192], P('row', ('leaf', 'col')), as said below
- root_row: int32 [8, 6144], replicated, may hold values from -1 to 8191, as said below
- coupling: float32 [8, 6144, 3072], P('leaf', 'row', 'col')
- pivot_variance: float32 [8, 3072], P('leaf', 'col'), may hold values from 0.5 to 2
Outputs:
- off_diagonal_inverse: float32 [8, 6144, 3072], P('leaf', 'row', 'col')
- pivot_marginal: float32 [8, 3072], P('leaf', 'col')
The draws below stay inside these ranges and needn't reach their ends.
Inputs may be any that keep to these rules, and one draw needn't show every extreme that they name: `root_row`: in each aligned block of 128 update rows of a child, the entries that are not -1 come first, increase, lie in one aligned block of 128 root rows, and number 128 // 2 to 128; the blocks of one child use distinct root blocks, increasing along the child; block b uses a root block within rows k * 1024 to (k + 1) * 1024 - 1, where k = b // 6. `root_inverse`: Symmetric.
All inputs are finite; a program needn't handle non-finite values.
Results may differ from the reference program's by a relative error of at most 0.0003.
Values sent between devices are 32-bit elements; how exact they have to be, the bound alone decides.
No kernel may reach another device: no remote copies, remote signals or barrier semaphores. Data moves between devices by JAX's collectives and lax.ppermute only.
A program may use at most 128 MiB of HBM per device.

```python
import math
import jax
import jax.numpy as jnp
from jax import lax

R = 8192
U = 6144
P_SIZE = 3072
BLK = 128
CHILDREN = 8
RANGE_BLOCKS = 8
TILE_BLOCKS = 6


def draw_root_inverse(key, part):
    key = jax.random.fold_in(key, 1)
    first_key, second_key = jax.random.split(key)
    noise = jax.random.normal(first_key, (R, R), jnp.float32)
    diagonal = jnp.exp(jax.random.uniform(second_key, (R,), jnp.float32, math.log(0.5), math.log(2.0)))
    coupled = (noise + noise.T) * (0.25 * math.sqrt(U) / math.sqrt(2.0))
    identity = jnp.arange(R)[:, None] == jnp.arange(R)[None, :]
    return jnp.where(identity, U * diagonal[:, None], coupled)


def draw_coupling(key, part):
    key = jax.random.fold_in(key, 2)
    location = jnp.arange(U, dtype=jnp.float32) / U
    noise = jax.random.normal(key, (CHILDREN, U, P_SIZE), jnp.float32)
    scaling = jnp.exp(math.log(3.0) * (location - 0.5)) / U
    return noise * scaling[None, :, None]


def draw_root_row(key, part):
    key = jax.random.fold_in(key, 3)
    block_key, count_key, offset_key = jax.random.split(key, 3)
    tiles = U // (BLK * TILE_BLOCKS)
    blocks_all = tiles * TILE_BLOCKS
    block_keys = jax.random.split(block_key, CHILDREN * tiles)
    chosen = jax.vmap(lambda sub_key: jax.random.permutation(sub_key, RANGE_BLOCKS)[:TILE_BLOCKS])(block_keys)
    chosen = jnp.sort(chosen, axis=1).reshape(CHILDREN, tiles, TILE_BLOCKS)
    forced = (jnp.arange(CHILDREN)[:, None, None] == 0) & (jnp.arange(tiles)[None, :, None] == tiles - 1) & (jnp.arange(TILE_BLOCKS)[None, None, :] == TILE_BLOCKS - 1)
    chosen = jnp.where(forced, RANGE_BLOCKS - 1, chosen)
    root_block = (chosen + jnp.arange(tiles)[None, :, None] * RANGE_BLOCKS).reshape(CHILDREN * blocks_all)
    counts = jax.random.randint(count_key, (CHILDREN, blocks_all), BLK // 2, BLK + 1)
    first_mark = (jnp.arange(CHILDREN)[:, None] == 0) & (jnp.arange(blocks_all)[None, :] == 0)
    last_mark = (jnp.arange(CHILDREN)[:, None] == 0) & (jnp.arange(blocks_all)[None, :] == blocks_all - 1)
    counts = jnp.where(first_mark, BLK // 2, jnp.where(last_mark, BLK, counts)).reshape(CHILDREN * blocks_all)
    offset_keys = jax.random.split(offset_key, CHILDREN * blocks_all)
    shuffled = jax.vmap(lambda sub_key: jax.random.permutation(sub_key, BLK))(offset_keys)
    ranking = jnp.argsort(shuffled, axis=1, stable=True)
    picked = ranking < counts[:, None]
    slot_of = jnp.cumsum(picked.astype(jnp.int32), axis=1) - 1
    slots = jnp.arange(BLK)
    matches = picked[:, :, None] & (slot_of[:, :, None] == slots[None, None, :])
    offsets = jnp.sum(jnp.where(matches, slots[None, :, None], 0), axis=1)
    result = jnp.where(slots[None, :] < counts[:, None], root_block[:, None] * BLK + offsets, -1)
    return result.reshape(CHILDREN, U).astype(jnp.int32)


def level_of(rng, extent, cuts, low, high):
    factor_of = 1.0
    for dim, shards_of in cuts:
        heights = jax.random.uniform(jax.random.fold_in(jax.random.fold_in(rng, 6), dim), (shards_of,), jnp.float32, low / len(cuts), high / len(cuts))
        factor_of = factor_of * jnp.repeat(jnp.exp(heights), extent[dim] // shards_of).reshape((-1,) + (1,) * (len(extent) - 1 - dim))
    return factor_of


def setup_inputs(seed: int = 0) -> dict:
    arg_keys = jax.random.split(jax.random.key(seed), 5)
    return {
        "root_inverse": draw_root_inverse(jax.random.fold_in(arg_keys[4], 71), 0),
        "root_row": draw_root_row(jax.random.fold_in(arg_keys[4], 71), 0),
        "coupling": draw_coupling(jax.random.fold_in(arg_keys[4], 71), 0),
        "pivot_variance": jnp.clip(jnp.exp(math.log(2.0) - 1.3862944 * jax.random.uniform(arg_keys[3], (CHILDREN, P_SIZE), jnp.float32) ** level_of(arg_keys[3], (CHILDREN, P_SIZE), ((0, 8), (1, 8)), -0.2, 0.2)), 0.5, 2.0),
    }


def reference(root_inverse, root_row, coupling, pivot_variance):
    def one_child(inputs):
        mapping, factor, variance = inputs
        usable = mapping >= 0
        position = jnp.where(usable, mapping, 0).astype(jnp.int32)
        picked = jnp.where(usable[:, None], jnp.take(root_inverse, position, axis=0), 0.0)
        adjoint = jnp.where(usable[None, :], jnp.take(picked, position, axis=1), 0.0)
        product = -jnp.dot(adjoint, factor, precision=lax.Precision.HIGHEST, preferred_element_type=jnp.float32)
        marginal = variance - jnp.sum(factor * product, axis=0)
        return product, marginal

    products, marginals = lax.map(one_child, (root_row, coupling, pivot_variance))
    return products, marginals
```

```python
import functools

import jax
import jax.numpy as jnp
from jax import lax
from jax.experimental import pallas as pl
from jax.experimental.pallas import tpu as pltpu
from jax.sharding import Mesh, PartitionSpec as P

BLOCK = 128
ORDER = (0, -1, 1, 2)
SPLIT_ROWS = 128


def shift(size, step):
    return [(i, (i + step) % size) for i in range(size)]


def split_into(high_ref, low_ref, value, index):
    high = value.astype(jnp.bfloat16)
    high_ref[index] = high
    low_ref[index] = (value - high.astype(jnp.float32)).astype(jnp.bfloat16)


def product_kernel(table, root_hbm, *rest):
    pieces = rest[:10]
    out_hbm = rest[10]
    (root_f, root_h, root_l, z_f, z_h, z_l, a_h, a_l, out_v, root_sem, z_sem, out_sem) = rest[11:]
    blocks = root_f.shape[0]
    rows = z_f.shape[2]
    half = rows // 2
    per_range = rows // BLOCK
    places = []
    for side in range(2):
        for slot in range(3):
            places.append((side, slot, 0, rows))
        places.append((side, 3, 0, half))
        places.append((side, 3, half, half))
    z_copies = [
        pltpu.make_async_copy(piece, z_f.at[side, slot, pl.ds(start, size)], z_sem.at[i])
        for i, (piece, (side, slot, start, size)) in enumerate(zip(pieces, places))
    ]
    root_copies = [
        pltpu.make_async_copy(root_hbm.at[b], root_f.at[b], root_sem.at[b]) for b in range(blocks)
    ]
    for copy in z_copies:
        copy.start()
    for copy in root_copies:
        copy.start()
    for copy, (side, slot, start, size) in zip(z_copies, places):
        copy.wait()

        def split_z(i, carry, side=side, slot=slot, start=start):
            at = pl.ds(pl.multiple_of(start + i * SPLIT_ROWS, SPLIT_ROWS), SPLIT_ROWS)
            value = z_f[side, slot, at, :]
            high = value.astype(jnp.bfloat16)
            z_h[slot, side, at, :] = high
            z_l[slot, side, at, :] = (value - high.astype(jnp.float32)).astype(jnp.bfloat16)
            return carry

        lax.fori_loop(0, size // SPLIT_ROWS, split_z, 0)
    for b, copy in enumerate(root_copies):
        copy.wait()

        def split_root(i, carry, b=b):
            at = pl.ds(pl.multiple_of(i * 256, 256), 256)
            value = root_f[b, at, :]
            high = value.astype(jnp.bfloat16)
            root_h[b, at, :] = high
            root_l[b, at, :] = (value - high.astype(jnp.float32)).astype(jnp.bfloat16)
            return carry

        lax.fori_loop(0, root_f.shape[1] // 256, split_root, 0)

    def child(t, carry):
        slot = table[t, 0]

        def select(k, inner):
            kb = table[t, 1 + per_range + k]
            for m in range(per_range):
                mb = pl.multiple_of(table[t, 1 + m] * BLOCK, BLOCK)
                at = pl.ds(m * BLOCK, BLOCK)
                a_h[k, at, :] = root_h[kb, pl.ds(mb, BLOCK), :]
                a_l[k, at, :] = root_l[kb, pl.ds(mb, BLOCK), :]
            return inner

        lax.fori_loop(0, 2 * per_range, select, 0)
        zh = z_h[slot].reshape(2 * rows, z_h.shape[3])
        zl = z_l[slot].reshape(2 * rows, z_h.shape[3])

        def part(m, inner):
            at = pl.ds(pl.multiple_of(m * 256, 256), 256)
            ah = jnp.concatenate([a_h[k, at, :] for k in range(2 * per_range)], axis=1)
            al = jnp.concatenate([a_l[k, at, :] for k in range(2 * per_range)], axis=1)
            total = jnp.dot(ah, zl, preferred_element_type=jnp.float32)
            total = total + jnp.dot(al, zh, preferred_element_type=jnp.float32)
            out_v[t, at, :] = total + jnp.dot(ah, zh, preferred_element_type=jnp.float32)
            return inner

        lax.fori_loop(0, rows // 256, part, 0)
        pltpu.make_async_copy(out_v.at[t], out_hbm.at[t], out_sem.at[t]).start()
        return carry

    lax.fori_loop(0, 4, child, 0)
    for t in range(4):
        pltpu.make_async_copy(out_v.at[t], out_hbm.at[t], out_sem.at[t]).wait()


def product(table, root, pieces):
    blocks, range_rows, _ = root.shape
    rows, cols = pieces[0].shape
    any_spec = pl.BlockSpec(memory_space=pl.ANY)
    return pl.pallas_call(
        product_kernel,
        out_shape=jax.ShapeDtypeStruct((4, rows, cols), jnp.float32),
        in_specs=[pl.BlockSpec(memory_space=pltpu.SMEM)] + [any_spec] * (1 + len(pieces)),
        out_specs=any_spec,
        scratch_shapes=[
            pltpu.VMEM((blocks, range_rows, BLOCK), jnp.float32),
            pltpu.VMEM((blocks, range_rows, BLOCK), jnp.bfloat16),
            pltpu.VMEM((blocks, range_rows, BLOCK), jnp.bfloat16),
            pltpu.VMEM((2, 4, rows, cols), jnp.float32),
            pltpu.VMEM((4, 2, rows, cols), jnp.bfloat16),
            pltpu.VMEM((4, 2, rows, cols), jnp.bfloat16),
            pltpu.VMEM((2 * rows // BLOCK, rows, BLOCK), jnp.bfloat16),
            pltpu.VMEM((2 * rows // BLOCK, rows, BLOCK), jnp.bfloat16),
            pltpu.VMEM((4, rows, cols), jnp.float32),
            pltpu.SemaphoreType.DMA((blocks,)),
            pltpu.SemaphoreType.DMA((len(pieces),)),
            pltpu.SemaphoreType.DMA((4,)),
        ],
        compiler_params=pltpu.CompilerParams(vmem_limit_bytes=60 * 1024 * 1024),
        cost_estimate=pl.CostEstimate(
            flops=4 * 3 * 2 * rows * 2 * rows * cols, bytes_accessed=24_000_000, transcendentals=0
        ),
    )(table, root, *pieces)


def per_device(root_inverse, root_row, coupling, pivot_variance):
    zh = lax.axis_index("zh")
    y = lax.axis_index("y")
    x = lax.axis_index("x")
    core = lax.axis_index("core")
    rows, cols = coupling.shape[1:]
    ranges = root_row.shape[1] // rows
    per_range = rows // BLOCK
    own_range = 2 * x + core

    first = root_row[:, ::BLOCK]
    block = (first // BLOCK).reshape(root_row.shape[0], ranges, per_range)
    place = lax.dynamic_slice(root_row, (zh * 4 + y, own_range * rows), (1, rows))
    place = place.reshape(per_range, BLOCK)
    own_block = block[zh * 4 + y, own_range]
    offsets = jnp.arange(BLOCK, dtype=jnp.int32)
    hot = (
        (place - own_block[:, None] * BLOCK)[:, :, None] == offsets[None, None, :]
    ).astype(jnp.float32)
    factor = coupling[0].reshape(per_range, BLOCK, cols)
    spread = jnp.einsum("iuo,iun->ion", hot, factor, precision=lax.Precision.HIGHEST)
    spread = spread.reshape(rows, cols)

    root = lax.all_gather(root_inverse, ("zh", "zl"), axis=0, tiled=False)

    swap = []
    for sy in range(4):
        for sx in range(4):
            for sc in range(2):
                r = 2 * sx + sc
                swap.append(((sy * 4 + sx) * 2 + sc, ((r % 4) * 4 + sy) * 2 + r // 4))
    own = lax.ppermute(spread, ("y", "x", "core"), swap)
    left = lax.ppermute(own, "x", shift(4, 1))
    right = lax.ppermute(own, "x", shift(4, -1))
    half = rows // 2
    far_a = lax.ppermute(left[:half], "x", shift(4, 1))
    far_b = lax.ppermute(right[half:], "x", shift(4, -1))
    mine = [own, left, right, far_a, far_b]
    other = [lax.ppermute(p, "core", [(0, 1), (1, 0)]) for p in mine]

    t = jnp.arange(4)
    child = (y + t) % 4
    slot_of_step = jnp.array([0, 2, 3, 1], jnp.int32)
    slot = slot_of_step[(child - x) % 4]
    row_blocks = block[zh * 4 + child, own_range] % 8
    sides = []
    for side in range(2):
        half_of = core if side == 0 else 1 - core
        column_blocks = block[zh * 4 + child, y + 4 * half_of] % 8
        sides.append(column_blocks + 8 * half_of)
    table = jnp.concatenate([slot[:, None], row_blocks, *sides], axis=1).astype(jnp.int32)

    partial = product(table, root.reshape(-1, *root_inverse.shape), mine + other)

    a = lax.ppermute(partial[2, :half], "y", shift(4, 1))
    b = lax.ppermute(partial[2, half:], "y", shift(4, -1))
    up = jnp.concatenate([partial[1, :half] + a, partial[1, half:]])
    down = jnp.concatenate([partial[3, :half], partial[3, half:] + b])
    summed = partial[0] + lax.ppermute(up, "y", shift(4, 1)) + lax.ppermute(down, "y", shift(4, -1))
    result = -jnp.einsum(
        "iuo,ion->iun", hot, summed.reshape(per_range, BLOCK, cols), precision=lax.Precision.HIGHEST
    )
    sums = jnp.sum(factor * result, axis=(0, 1))
    marginal = pivot_variance - lax.psum(sums, ("x", "core"))[None, :]
    return result.reshape(1, rows, cols), marginal


def solution(mesh):
    split = Mesh(mesh.devices.reshape(2, 4, 4, 2, 8), ("zh", "y", "x", "core", "zl"))
    leaf, row, col = ("zh", "y"), ("x", "core"), "zl"
    return jax.shard_map(
        per_device,
        mesh=split,
        in_specs=(P(row, ("zh", "y", "zl")), P(), P(leaf, row, col), P(leaf, col)),
        out_specs=(P(leaf, row, col), P(leaf, col)),
        check_vma=False,
    )
```

```python
import functools

import jax
import jax.numpy as jnp
from jax import lax
from jax.experimental import pallas as pl
from jax.experimental.pallas import tpu as pltpu
from jax.sharding import Mesh, PartitionSpec as P

BLOCK = 128
PART = 256
SPREAD_X = (
    (3, 1, 0, 0),
    (0, 3, 0, 1),
    (1, 2, 0, 1),
    (2, 0, 1, 1),
    (2, 2, 1, 3),
    (3, 1, 2, 2),
    (3, 0, 2, 3),
    (3, 2, 3, 0),
)


def shift(size, step):
    return [(i, (i + step) % size) for i in range(size)]


def spread_plan():
    pairs, holds, taken = [], {}, {}
    for y in range(4):
        for r in range(8):
            to = (SPREAD_X[r][y], r % 4)
            core = taken.get(to, 0)
            taken[to] = core + 1
            pairs.append(((y * 4 + r // 2) * 2 + r % 2, (to[1] * 4 + to[0]) * 2 + core))
            holds[(to[1], to[0], core)] = (r // 4) * 4 + y
    return pairs, [[[holds[(y, x, c)] for c in range(2)] for x in range(4)] for y in range(4)]


def spread_kernel(place, *rest):
    pieces = rest[:10]
    high_hbm, low_hbm, z_f, z_h, z_l, in_sem, out_sem = rest[10:]
    rows = z_f.shape[1]
    half = rows // 2
    spots = []
    for side in range(2):
        for slot in range(3):
            spots.append((side * 4 + slot, 0, rows))
        spots.append((side * 4 + 3, 0, half))
        spots.append((side * 4 + 3, half, half))
    copies = [
        pltpu.make_async_copy(piece, z_f.at[at, pl.ds(start, size)], in_sem.at[i])
        for i, (piece, (at, start, size)) in enumerate(zip(pieces, spots))
    ]
    for copy in copies:
        copy.start()
    row = lax.broadcasted_iota(jnp.int32, (BLOCK, BLOCK), 0)
    for copy, (at, start, size) in zip(copies, spots):
        copy.wait()

        def one(i, carry, at=at, start=start):
            block = start // BLOCK + i
            here = pl.ds(pl.multiple_of(start + i * BLOCK, BLOCK), BLOCK)
            value = z_f[at, here, :]
            high = value.astype(jnp.bfloat16)
            low = (value - high.astype(jnp.float32)).astype(jnp.bfloat16)
            hot = (place[at, pl.ds(block, 1), :] == row).astype(jnp.float32).astype(jnp.bfloat16)
            z_h[at, here, :] = jnp.dot(hot, high, preferred_element_type=jnp.float32).astype(
                jnp.bfloat16
            )
            z_l[at, here, :] = jnp.dot(hot, low, preferred_element_type=jnp.float32).astype(
                jnp.bfloat16
            )
            return carry

        lax.fori_loop(0, size // BLOCK, one, 0)
    outs = [
        pltpu.make_async_copy(z_h, high_hbm, out_sem.at[0]),
        pltpu.make_async_copy(z_l, low_hbm, out_sem.at[1]),
    ]
    for copy in outs:
        copy.start()
    for copy in outs:
        copy.wait()


def spread(place, pieces):
    rows, cols = pieces[0].shape
    any_spec = pl.BlockSpec(memory_space=pl.ANY)
    shape = (8, rows, cols)
    return pl.pallas_call(
        spread_kernel,
        out_shape=[jax.ShapeDtypeStruct(shape, jnp.bfloat16)] * 2,
        in_specs=[pl.BlockSpec(memory_space=pltpu.VMEM)] + [any_spec] * len(pieces),
        out_specs=[any_spec] * 2,
        scratch_shapes=[
            pltpu.VMEM(shape, jnp.float32),
            pltpu.VMEM(shape, jnp.bfloat16),
            pltpu.VMEM(shape, jnp.bfloat16),
            pltpu.SemaphoreType.DMA((len(pieces),)),
            pltpu.SemaphoreType.DMA((2,)),
        ],
        compiler_params=pltpu.CompilerParams(vmem_limit_bytes=48 * 1024 * 1024),
        cost_estimate=pl.CostEstimate(
            flops=8 * 4 * rows * BLOCK * cols, bytes_accessed=64 * rows * cols, transcendentals=0
        ),
    )(place, *pieces)


def product_kernel(steps, table, root_hbm, high_hbm, low_hbm, out_hbm, *rest):
    a_f, z_h, z_l, out_v, a_sem, z_sem, out_sem = rest
    rows = out_v.shape[1]
    per_range = rows // BLOCK
    parts = rows // PART
    per_part = PART // BLOCK

    def z_copies(i, t):
        found = []
        for side in range(2):
            spot = table[t, 3 * per_range + side]
            at = pl.ds(side * rows, rows)
            found.append(pltpu.make_async_copy(high_hbm.at[spot], z_h.at[i, at], z_sem.at[i, side]))
            found.append(
                pltpu.make_async_copy(low_hbm.at[spot], z_l.at[i, at], z_sem.at[i, 2 + side])
            )
        return found

    def a_start(i, t, part):
        def one(k, carry):
            kb = table[t, per_range + k]
            for m in range(per_part):
                mb = pl.multiple_of(table[t, part * per_part + m] * BLOCK, BLOCK)
                pltpu.make_async_copy(
                    root_hbm.at[kb, pl.ds(mb, BLOCK)],
                    a_f.at[i, part, k, pl.ds(m * BLOCK, BLOCK)],
                    a_sem.at[i, part],
                ).start()
            return carry

        lax.fori_loop(0, 2 * per_range, one, 0)

    for i, t in enumerate(steps):
        for copy in z_copies(i, t):
            copy.start()
        for part in range(parts):
            a_start(i, t, part)
    for i, t in enumerate(steps):
        for copy in z_copies(i, t):
            copy.wait()

        def one(part, carry, i=i):
            pltpu.make_async_copy(a_f.at[i, part], a_f.at[i, part], a_sem.at[i, part]).wait()
            values = [a_f[i, part, k] for k in range(2 * per_range)]
            highs = [v.astype(jnp.bfloat16) for v in values]
            lows = [
                (v - h.astype(jnp.float32)).astype(jnp.bfloat16) for v, h in zip(values, highs)
            ]
            ah = jnp.concatenate(highs, axis=1)
            al = jnp.concatenate(lows, axis=1)
            total = jnp.dot(ah, z_l[i], preferred_element_type=jnp.float32)
            total = total + jnp.dot(al, z_h[i], preferred_element_type=jnp.float32)
            at = pl.ds(pl.multiple_of(part * PART, PART), PART)
            out_v[i, at, :] = total + jnp.dot(ah, z_h[i], preferred_element_type=jnp.float32)
            return carry

        lax.fori_loop(0, parts, one, 0)
        pltpu.make_async_copy(out_v.at[i], out_hbm.at[i], out_sem.at[i]).start()
    for i in range(len(steps)):
        pltpu.make_async_copy(out_v.at[i], out_hbm.at[i], out_sem.at[i]).wait()


def product(steps, table, root, high, low):
    rows, cols = high.shape[1:]
    count = len(steps)
    any_spec = pl.BlockSpec(memory_space=pl.ANY)
    return pl.pallas_call(
        functools.partial(product_kernel, steps),
        out_shape=jax.ShapeDtypeStruct((count, rows, cols), jnp.float32),
        in_specs=[pl.BlockSpec(memory_space=pltpu.SMEM)] + [any_spec] * 3,
        out_specs=any_spec,
        scratch_shapes=[
            pltpu.VMEM((count, rows // PART, 2 * rows // BLOCK, PART, BLOCK), jnp.float32),
            pltpu.VMEM((count, 2 * rows, cols), jnp.bfloat16),
            pltpu.VMEM((count, 2 * rows, cols), jnp.bfloat16),
            pltpu.VMEM((count, rows, cols), jnp.float32),
            pltpu.SemaphoreType.DMA((count, rows // PART)),
            pltpu.SemaphoreType.DMA((count, 4)),
            pltpu.SemaphoreType.DMA((count,)),
        ],
        compiler_params=pltpu.CompilerParams(vmem_limit_bytes=48 * 1024 * 1024),
        cost_estimate=pl.CostEstimate(
            flops=count * 3 * 2 * rows * 2 * rows * cols,
            bytes_accessed=count * (8 * rows * rows + 12 * rows * cols),
            transcendentals=0,
        ),
    )(table, root, high, low)


def per_device(root_inverse, root_row, coupling, pivot_variance):
    zh = lax.axis_index("zh")
    y = lax.axis_index("y")
    x = lax.axis_index("x")
    core = lax.axis_index("core")
    rows, cols = coupling.shape[1:]
    ranges = root_row.shape[1] // rows
    per_range = rows // BLOCK
    half = rows // 2
    own_range = 2 * x + core

    root = lax.all_gather(root_inverse, ("zh", "zl"), axis=0, tiled=False)

    pairs, holds = spread_plan()
    own = lax.ppermute(coupling[0], ("y", "x", "core"), pairs)
    left = lax.ppermute(own, "x", shift(4, 1))
    right = lax.ppermute(own, "x", shift(4, -1))
    far_a = lax.ppermute(left[:half], "x", shift(4, 1))
    far_b = lax.ppermute(right[half:], "x", shift(4, -1))
    mine = [own, left, right, far_a, far_b]
    pieces = mine + [lax.ppermute(p, "core", [(0, 1), (1, 0)]) for p in mine]

    spots = jnp.array(holds, jnp.int32)[
        y, (x + jnp.array([0, -1, 1, 2] * 2)) % 4, jnp.array([0] * 4 + [1] * 4) ^ core
    ]
    by_range = root_row.reshape(root_row.shape[0], ranges, per_range, BLOCK)
    block = by_range[..., 0] // BLOCK
    place = by_range - block[..., None] * BLOCK
    piece_child, piece_range = zh * 4 + spots % 4, y + 4 * (spots // 4)
    high, low = spread(place[piece_child, piece_range], pieces)

    child = (y + jnp.arange(4)) % 4
    row_blocks = block[zh * 4 + child, own_range] % 8
    columns = [block[zh * 4 + child, y + 4 * side] % 8 + 8 * side for side in range(2)]
    found = [
        jnp.argmax(spots[None, :] == child[:, None] + 4 * side, axis=1)[:, None] for side in range(2)
    ]
    table = jnp.concatenate([row_blocks, *columns, *found], axis=1).astype(jnp.int32)

    far = product((2,), table, root, high, low)[0]
    a = lax.ppermute(far[:half], "y", shift(4, 1))
    b = lax.ppermute(far[half:], "y", shift(4, -1))
    near = product((1, 3), table, root, high, low)
    up = lax.ppermute(near[0, half:], "y", shift(4, 1))
    down = lax.ppermute(near[1, :half], "y", shift(4, -1))
    up_far = lax.ppermute(near[0, :half] + a, "y", shift(4, 1))
    down_far = lax.ppermute(near[1, half:] + b, "y", shift(4, -1))
    home = product((0,), table, root, high, low)[0]
    summed = jnp.concatenate([home[:half] + up_far + down, home[half:] + up + down_far])

    own_place = place[zh * 4 + y, own_range]
    hot = (own_place[:, :, None] == jnp.arange(BLOCK, dtype=jnp.int32)).astype(jnp.float32)
    result = -jnp.einsum(
        "iuo,ion->iun", hot, summed.reshape(per_range, BLOCK, cols), precision=lax.Precision.HIGHEST
    )
    sums = jnp.sum(coupling[0] * result.reshape(rows, cols), axis=0, keepdims=True)
    sums = sums + lax.ppermute(sums, "core", [(0, 1), (1, 0)])
    sums = sums + lax.ppermute(sums, "x", [(0, 1), (1, 0), (2, 3), (3, 2)])
    sums = sums + lax.ppermute(sums, "x", [(0, 2), (2, 0), (1, 3), (3, 1)])
    return result.reshape(1, rows, cols), pivot_variance - sums


def solution(mesh):
    split = Mesh(mesh.devices.reshape(2, 4, 4, 2, 8), ("zh", "y", "x", "core", "zl"))
    leaf, row, col = ("zh", "y"), ("x", "core"), "zl"
    return jax.shard_map(
        per_device,
        mesh=split,
        in_specs=(P(row, ("zh", "y", "zl")), P(), P(leaf, row, col), P(leaf, col)),
        out_specs=(P(leaf, row, col), P(leaf, col)),
        check_vma=False,
    )
```

```python
import functools

import jax
import jax.numpy as jnp
from jax import lax
from jax.experimental import pallas as pl
from jax.experimental.pallas import tpu as pltpu
from jax.sharding import Mesh, PartitionSpec as P

BLOCK = 128
PART = 256
VMEM_BYTES = 60 * 1024 * 1024
CORES = [(0, 1), (1, 0)]
SPREAD_X = (
    (3, 1, 0, 0),
    (0, 3, 0, 1),
    (1, 2, 0, 1),
    (2, 0, 1, 1),
    (2, 2, 1, 3),
    (3, 1, 2, 2),
    (3, 0, 2, 3),
    (3, 2, 3, 0),
)


def shift(size, step):
    return [(i, (i + step) % size) for i in range(size)]


def opposite(size):
    return [(2 * i + c, (i + 1 - 2 * c) % size * 2 + c) for i in range(size) for c in range(2)]


def spread_plan():
    pairs, holds, taken = [], {}, {}
    for y in range(4):
        for r in range(8):
            to = (SPREAD_X[r][y], r % 4)
            core = taken.get(to, 0)
            taken[to] = core + 1
            pairs.append(((y * 4 + r // 2) * 2 + r % 2, (to[1] * 4 + to[0]) * 2 + core))
            holds[(to[1], to[0], core)] = (r // 4, y)
    return pairs, holds


def piece_plan(holds):
    halves, own, found = [], [], []
    for y in range(4):
        for x in range(4):
            for c in range(2):
                d = 2 * c - 1
                at = [
                    (x, c),
                    (x, 1 - c),
                    (x + d, c),
                    (x + d, 1 - c),
                    (x + 2, c),
                    (x - d, 1 - c),
                    (x - d, c),
                    (x + 2, 1 - c),
                ]
                has = [holds[(y, px % 4, pc)] for px, pc in at]
                mine = [y, (y + d) % 4, (y + 2) % 4, (y - d) % 4]
                halves.append([h * 4 + k for h, k in has])
                own.append(mine)
                found.append(
                    [[has.index((0, k)), has.index((1, k)), 8 + mine.index(k)] for k in range(4)]
                )
    return [jnp.array(v, jnp.int32) for v in (halves, own, found)]


def spread_kernel(start_row, rows_ref, *rest):
    pieces = rest[:12]
    high_hbm, low_hbm, z_f, z_h, z_l, in_sem, out_sem = rest[12:]
    rows = z_f.shape[1]
    copies = [
        pltpu.make_async_copy(piece, z_f.at[i], in_sem.at[i]) for i, piece in enumerate(pieces)
    ]
    outs = []
    for i in range(12):
        outs.append(pltpu.make_async_copy(z_h.at[i], high_hbm.at[i], out_sem.at[2 * i]))
        outs.append(pltpu.make_async_copy(z_l.at[i], low_hbm.at[i], out_sem.at[2 * i + 1]))
    for copy in copies:
        copy.start()
    row = lax.broadcasted_iota(jnp.int32, (BLOCK, BLOCK), 0)
    for at, copy in enumerate(copies):
        copy.wait()

        def one(i, carry, at=at):
            here = pl.ds(pl.multiple_of(i * BLOCK, BLOCK), BLOCK)
            value = z_f[at, here, :]
            high = value.astype(jnp.bfloat16)
            low = (value - high.astype(jnp.float32)).astype(jnp.bfloat16)
            place = rows_ref[pl.ds(start_row[at] + i, 1), :]
            place = jnp.where(place >= 0, place & (BLOCK - 1), -1)
            hot = (place == row).astype(jnp.float32).astype(jnp.bfloat16)
            z_h[at, here, :] = jnp.dot(hot, high, preferred_element_type=jnp.float32).astype(
                jnp.bfloat16
            )
            z_l[at, here, :] = jnp.dot(hot, low, preferred_element_type=jnp.float32).astype(
                jnp.bfloat16
            )
            return carry

        lax.fori_loop(0, rows // BLOCK, one, 0, unroll=2)
        outs[2 * at].start()
        outs[2 * at + 1].start()
    for copy in outs:
        copy.wait()


def spread(start_row, root_row, pieces):
    rows, cols = pieces[0].shape
    any_spec = pl.BlockSpec(memory_space=pl.ANY)
    shape = (len(pieces), rows, cols)
    return pl.pallas_call(
        spread_kernel,
        out_shape=[jax.ShapeDtypeStruct(shape, jnp.bfloat16)] * 2,
        in_specs=[
            pl.BlockSpec(memory_space=pltpu.SMEM),
            pl.BlockSpec(memory_space=pltpu.VMEM),
        ]
        + [any_spec] * len(pieces),
        out_specs=[any_spec] * 2,
        scratch_shapes=[
            pltpu.VMEM(shape, jnp.float32),
            pltpu.VMEM(shape, jnp.bfloat16),
            pltpu.VMEM(shape, jnp.bfloat16),
            pltpu.SemaphoreType.DMA((len(pieces),)),
            pltpu.SemaphoreType.DMA((2 * len(pieces),)),
        ],
        compiler_params=pltpu.CompilerParams(vmem_limit_bytes=VMEM_BYTES),
        cost_estimate=pl.CostEstimate(
            flops=12 * 4 * rows * BLOCK * cols, bytes_accessed=96 * rows * cols, transcendentals=0
        ),
    )(start_row, root_row, *pieces)


def product_kernel(steps, table, root_hbm, high_hbm, low_hbm, out_hbm, sums_hbm, *rest):
    a_f, z_h, z_l, b_h, b_l, out_v, sums_v, a_sem, z_sem, out_sem = rest
    rows = out_v.shape[1]
    per_range = rows // BLOCK
    per_part = PART // BLOCK

    def child(t):
        return (table[0, 3 * per_range + 3] + t) & 3

    def z_copies(i, t):
        c = child(t)
        found = []
        for side in range(2):
            spot = table[c, 3 * per_range + side]
            at = pl.ds(side * rows, rows)
            found.append(pltpu.make_async_copy(high_hbm.at[spot], z_h.at[i, at], z_sem.at[i, side]))
            found.append(
                pltpu.make_async_copy(low_hbm.at[spot], z_l.at[i, at], z_sem.at[i, 2 + side])
            )
        spot = table[c, 3 * per_range + 2]
        found.append(pltpu.make_async_copy(high_hbm.at[spot], b_h.at[i], z_sem.at[i, 4]))
        found.append(pltpu.make_async_copy(low_hbm.at[spot], b_l.at[i], z_sem.at[i, 5]))
        return found

    def a_copy(i, t, m):
        mb = pl.multiple_of(table[child(t), m] * BLOCK, BLOCK)
        return pltpu.make_async_copy(
            root_hbm.at[:, pl.ds(mb, BLOCK)], a_f.at[i, m], a_sem.at[i, m]
        )

    for i, t in enumerate(steps):
        for copy in z_copies(i, t):
            copy.start()
        for m in range(per_range):
            a_copy(i, t, m).start()
    for i, t in enumerate(steps):
        for copy in z_copies(i, t):
            copy.wait()
        c = child(t)

        def one(part, total, i=i, t=t, c=c):
            for m in range(per_part):
                a_copy(i, t, part * per_part + m).wait()
            highs, lows = [], []
            for k in range(2 * per_range):
                kb = table[c, per_range + k]
                value = jnp.concatenate(
                    [a_f[i, part * per_part + m, kb] for m in range(per_part)], axis=0
                )
                high = value.astype(jnp.bfloat16)
                highs.append(high)
                lows.append((value - high.astype(jnp.float32)).astype(jnp.bfloat16))
            high = jnp.concatenate(highs, axis=1)
            both = jnp.concatenate([high, jnp.concatenate(lows, axis=1)], axis=0)
            first = jnp.dot(both, z_h[i], preferred_element_type=jnp.float32)
            second = jnp.dot(high, z_l[i], preferred_element_type=jnp.float32)
            value = first[:PART] + (first[PART:] + second)
            at = pl.ds(pl.multiple_of(part * PART, PART), PART)
            out_v[i, at, :] = value
            factor = b_h[i, at, :].astype(jnp.float32) + b_l[i, at, :].astype(jnp.float32)
            return total + jnp.sum((factor * value).reshape(PART // 8, 8, -1), axis=0)

        sums_v[i] = lax.fori_loop(
            0, rows // PART, one, jnp.zeros(sums_v.shape[1:], jnp.float32)
        )
        pltpu.make_async_copy(out_v.at[i], out_hbm.at[i], out_sem.at[i, 0]).start()
        pltpu.make_async_copy(sums_v.at[i], sums_hbm.at[i], out_sem.at[i, 1]).start()
    for i in range(len(steps)):
        pltpu.make_async_copy(out_v.at[i], out_hbm.at[i], out_sem.at[i, 0]).wait()
        pltpu.make_async_copy(sums_v.at[i], sums_hbm.at[i], out_sem.at[i, 1]).wait()


def product(steps, table, root, high, low):
    rows, cols = high.shape[1:]
    count = len(steps)
    per_range = rows // BLOCK
    any_spec = pl.BlockSpec(memory_space=pl.ANY)
    return pl.pallas_call(
        functools.partial(product_kernel, steps),
        out_shape=[
            jax.ShapeDtypeStruct((count, rows, cols), jnp.float32),
            jax.ShapeDtypeStruct((count, 8, cols), jnp.float32),
        ],
        in_specs=[pl.BlockSpec(memory_space=pltpu.SMEM)] + [any_spec] * 3,
        out_specs=[any_spec] * 2,
        scratch_shapes=[
            pltpu.VMEM((count, per_range, root.shape[0], BLOCK, BLOCK), jnp.float32),
            pltpu.VMEM((count, 2 * rows, cols), jnp.bfloat16),
            pltpu.VMEM((count, 2 * rows, cols), jnp.bfloat16),
            pltpu.VMEM((count, rows, cols), jnp.bfloat16),
            pltpu.VMEM((count, rows, cols), jnp.bfloat16),
            pltpu.VMEM((count, rows, cols), jnp.float32),
            pltpu.VMEM((count, 8, cols), jnp.float32),
            pltpu.SemaphoreType.DMA((count, per_range)),
            pltpu.SemaphoreType.DMA((count, 6)),
            pltpu.SemaphoreType.DMA((count, 2)),
        ],
        compiler_params=pltpu.CompilerParams(vmem_limit_bytes=VMEM_BYTES),
        cost_estimate=pl.CostEstimate(
            flops=count * 3 * 2 * rows * 2 * rows * cols,
            bytes_accessed=count * (12 * rows * rows + 16 * rows * cols),
            transcendentals=0,
        ),
    )(table, root, high, low)


def per_device(root_inverse, root_row, coupling, pivot_variance):
    zh = lax.axis_index("zh")
    y = lax.axis_index("y")
    x = lax.axis_index("x")
    core = lax.axis_index("core")
    rows, cols = coupling.shape[1:]
    ranges = root_row.shape[1] // rows
    per_range = rows // BLOCK
    half = rows // 2
    own_range = 2 * x + core
    device = (y * 4 + x) * 2 + core

    root = lax.all_gather(root_inverse, ("zh", "zl"), axis=0, tiled=False)

    pairs, holds = spread_plan()
    own = lax.ppermute(coupling[0], ("y", "x", "core"), pairs)
    along_x, along_y = opposite(4), opposite(4)
    beside = lax.ppermute(own, "core", CORES)
    near = lax.ppermute(own, ("x", "core"), along_x)
    near_beside = lax.ppermute(beside, ("x", "core"), along_x)
    far = lax.ppermute(near, ("x", "core"), along_x)
    pieces = [own, beside, near, near_beside, far]
    pieces += [lax.ppermute(p, "core", CORES) for p in (near, near_beside, far)]

    y_beside = lax.ppermute(coupling[0], "core", CORES)
    y_near = lax.ppermute(coupling[0], ("y", "core"), along_y)
    y_near_beside = lax.ppermute(y_beside, ("y", "core"), along_y)
    y_far = lax.ppermute(y_near, ("y", "core"), along_y)
    pieces += [coupling[0], y_near, y_far, lax.ppermute(y_near_beside, "core", CORES)]

    halves, own_children, found = piece_plan(holds)
    spots = lax.dynamic_slice(halves, (device, 0), (1, 8))[0]
    own_spots = lax.dynamic_slice(own_children, (device, 0), (1, 4))[0]
    child = zh * 4 + jnp.concatenate([spots & 3, own_spots])
    ranged = jnp.concatenate([y + 4 * (spots >> 2), jnp.full((4,), own_range, jnp.int32)])
    start_row = (child * ranges + ranged) * per_range
    high, low = spread(start_row, root_row.reshape(-1, BLOCK), pieces)

    block = (root_row[:, ::BLOCK] >> 7).reshape(-1, ranges, per_range)

    def blocks_of(r):
        return lax.dynamic_slice(block, (zh * 4, r, 0), (4, 1, per_range))[:, 0] & 7

    table = jnp.concatenate(
        [
            blocks_of(own_range),
            blocks_of(y),
            blocks_of(y + 4) + 8,
            lax.dynamic_slice(found, (device, 0, 0), (1, 4, 3))[0],
            jnp.broadcast_to(y, (4, 1)),
        ],
        axis=1,
    ).astype(jnp.int32)

    far, far_sums = product((2,), table, root, high, low)
    a = lax.ppermute(far[0, :half], "y", shift(4, 1))
    b = lax.ppermute(far[0, half:], "y", shift(4, -1))
    near, near_sums = product((1, 3), table, root, high, low)
    up = lax.ppermute(near[0, half:], "y", shift(4, 1))
    down = lax.ppermute(near[1, :half], "y", shift(4, -1))
    up_far = lax.ppermute(near[0, :half] + a, "y", shift(4, 1))
    down_far = lax.ppermute(near[1, half:] + b, "y", shift(4, -1))
    home, home_sums = product((0,), table, root, high, low)
    summed = jnp.concatenate([home[0, :half] + up_far + down, home[0, half:] + up + down_far])

    own_place = lax.dynamic_slice(root_row, (zh * 4 + y, own_range * rows), (1, rows))[0]
    own_place = jnp.where(own_place >= 0, own_place & (BLOCK - 1), -1).reshape(per_range, BLOCK)
    hot = (own_place[:, :, None] == jnp.arange(BLOCK, dtype=jnp.int32)).astype(jnp.float32)
    result = -jnp.einsum(
        "iuo,ion->iun", hot, summed.reshape(per_range, BLOCK, cols), precision=lax.Precision.HIGHEST
    )

    sums = jnp.concatenate([home_sums, near_sums[:1], far_sums, near_sums[1:]]).sum(axis=1)
    steps = (jnp.arange(4)[:, None] - y) % 4 == jnp.arange(4)[None, :]
    sums = jnp.sum(jnp.where(steps[:, :, None], sums[None], 0.0), axis=1)
    sums = lax.psum(sums, ("y", "x", "core"))
    marginal = pivot_variance + lax.dynamic_slice(sums, (y, 0), (1, cols))
    return result.reshape(1, rows, cols), marginal


def solution(mesh):
    split = Mesh(mesh.devices.reshape(2, 4, 4, 2, 8), ("zh", "y", "x", "core", "zl"))
    leaf, row, col = ("zh", "y"), ("x", "core"), "zl"
    return jax.shard_map(
        per_device,
        mesh=split,
        in_specs=(P(row, ("zh", "y", "zl")), P(), P(leaf, row, col), P(leaf, col)),
        out_specs=(P(leaf, row, col), P(leaf, col)),
        check_vma=False,
    )
```

```python
import functools

import jax
import jax.numpy as jnp
from jax import lax
from jax.experimental import pallas as pl
from jax.experimental.pallas import tpu as pltpu
from jax.sharding import Mesh, PartitionSpec as P

BLOCK = 128
PART = 256
SLOTS = 4
SPREAD_VMEM = 16 * 1024 * 1024
PRODUCT_VMEM = 42 * 1024 * 1024
CORES = [(0, 1), (1, 0)]
SPREAD_X = (
    (3, 1, 0, 0),
    (0, 3, 0, 1),
    (1, 2, 0, 1),
    (2, 0, 1, 1),
    (2, 2, 1, 3),
    (3, 1, 2, 2),
    (3, 0, 2, 3),
    (3, 2, 3, 0),
)


def shift(size, step):
    return [(i, (i + step) % size) for i in range(size)]


def opposite(size):
    return [(2 * i + c, (i + 1 - 2 * c) % size * 2 + c) for i in range(size) for c in range(2)]


def spread_plan():
    pairs, holds, taken = [], {}, {}
    for y in range(4):
        for r in range(8):
            to = (SPREAD_X[r][y], r % 4)
            core = taken.get(to, 0)
            taken[to] = core + 1
            pairs.append(((y * 4 + r // 2) * 2 + r % 2, (to[1] * 4 + to[0]) * 2 + core))
            holds[(to[1], to[0], core)] = (r // 4, y)
    return pairs, holds


def piece_plan(holds):
    halves, own, found = [], [], []
    for y in range(4):
        for x in range(4):
            for c in range(2):
                d = 2 * c - 1
                at = [
                    (x, c),
                    (x, 1 - c),
                    (x + d, c),
                    (x + d, 1 - c),
                    (x + 2, c),
                    (x - d, 1 - c),
                    (x - d, c),
                    (x + 2, 1 - c),
                ]
                has = [holds[(y, px % 4, pc)] for px, pc in at]
                mine = [y, (y + d) % 4, (y + 2) % 4, (y - d) % 4]
                halves.append([h * 4 + k for h, k in has])
                own.append(mine)
                found.append(
                    [[has.index((0, k)), has.index((1, k)), 8 + mine.index(k)] for k in range(4)]
                )
    return [jnp.array(v, jnp.int32) for v in (halves, own, found)]


def spread_kernel(start_row, rows_ref, *rest):
    pieces = rest[:12]
    high_hbm, low_hbm, z_f, z_h, z_l, in_sem, out_sem = rest[12:]
    slots, rows = z_f.shape[:2]

    def fetch(i):
        return pltpu.make_async_copy(pieces[i], z_f.at[i % slots], in_sem.at[i])

    def store(i):
        return [
            pltpu.make_async_copy(z_h.at[i % slots], high_hbm.at[i], out_sem.at[2 * i]),
            pltpu.make_async_copy(z_l.at[i % slots], low_hbm.at[i], out_sem.at[2 * i + 1]),
        ]

    for i in range(slots):
        fetch(i).start()
    row = lax.broadcasted_iota(jnp.int32, (BLOCK, BLOCK), 0)
    for at in range(len(pieces)):
        fetch(at).wait()
        if at >= slots:
            for copy in store(at - slots):
                copy.wait()

        def one(i, carry, at=at):
            here = pl.ds(pl.multiple_of(i * BLOCK, BLOCK), BLOCK)
            value = z_f[at % slots, here, :]
            high = value.astype(jnp.bfloat16)
            low = (value - high.astype(jnp.float32)).astype(jnp.bfloat16)
            place = rows_ref[pl.ds(start_row[at] + i, 1), :]
            place = jnp.where(place >= 0, place & (BLOCK - 1), -1)
            hot = (place == row).astype(jnp.float32).astype(jnp.bfloat16)
            z_h[at % slots, here, :] = jnp.dot(
                hot, high, preferred_element_type=jnp.float32
            ).astype(jnp.bfloat16)
            z_l[at % slots, here, :] = jnp.dot(
                hot, low, preferred_element_type=jnp.float32
            ).astype(jnp.bfloat16)
            return carry

        lax.fori_loop(0, rows // BLOCK, one, 0, unroll=2)
        for copy in store(at):
            copy.start()
        if at + slots < len(pieces):
            fetch(at + slots).start()
    for at in range(len(pieces) - slots, len(pieces)):
        for copy in store(at):
            copy.wait()


def spread(start_row, root_row, pieces):
    rows, cols = pieces[0].shape
    any_spec = pl.BlockSpec(memory_space=pl.ANY)
    shape = (len(pieces), rows, cols)
    held = (SLOTS, rows, cols)
    return pl.pallas_call(
        spread_kernel,
        out_shape=[jax.ShapeDtypeStruct(shape, jnp.bfloat16)] * 2,
        in_specs=[
            pl.BlockSpec(memory_space=pltpu.SMEM),
            pl.BlockSpec(memory_space=pltpu.VMEM),
        ]
        + [any_spec] * len(pieces),
        out_specs=[any_spec] * 2,
        scratch_shapes=[
            pltpu.VMEM(held, jnp.float32),
            pltpu.VMEM(held, jnp.bfloat16),
            pltpu.VMEM(held, jnp.bfloat16),
            pltpu.SemaphoreType.DMA((len(pieces),)),
            pltpu.SemaphoreType.DMA((2 * len(pieces),)),
        ],
        compiler_params=pltpu.CompilerParams(vmem_limit_bytes=SPREAD_VMEM),
        cost_estimate=pl.CostEstimate(
            flops=12 * 4 * rows * BLOCK * cols, bytes_accessed=96 * rows * cols, transcendentals=0
        ),
    )(start_row, root_row, *pieces)


def product_kernel(steps, table, root_hbm, high_hbm, low_hbm, out_hbm, sums_hbm, *rest):
    a_f, z_h, z_l, b_h, b_l, out_v, sums_v, a_sem, z_sem, out_sem = rest
    rows = out_v.shape[1]
    per_range = rows // BLOCK
    per_part = PART // BLOCK
    parts = rows // PART

    def child(t):
        return (table[0, 3 * per_range + 3] + t) & 3

    def factor_copies(source, target, i, t, sem):
        found = []
        for side in range(2):
            spot = table[child(t), 3 * per_range + side]
            at = pl.ds(side * rows, rows)
            found.append(
                pltpu.make_async_copy(source.at[spot], target.at[i, at], z_sem.at[i, sem + side])
            )
        return found

    def high_copies(i, t):
        return factor_copies(high_hbm, z_h, i, t, 0)

    def low_copies(i, t):
        return factor_copies(low_hbm, z_l, i, t, 2)

    def own_copies(i, t):
        spot = table[child(t), 3 * per_range + 2]
        return [
            pltpu.make_async_copy(high_hbm.at[spot], b_h.at[i], z_sem.at[i, 4]),
            pltpu.make_async_copy(low_hbm.at[spot], b_l.at[i], z_sem.at[i, 5]),
        ]

    def start_root(i, t, part):
        for m in range(per_part):
            mb = pl.multiple_of(table[child(t), part * per_part + m] * BLOCK, BLOCK)
            pltpu.make_async_copy(
                root_hbm.at[:, pl.ds(mb, BLOCK)],
                a_f.at[i, part, :, pl.ds(m * BLOCK, BLOCK)],
                a_sem.at[i, part],
            ).start()

    def out_copy(i, part):
        at = pl.ds(part * PART, PART)
        return pltpu.make_async_copy(out_v.at[i, at], out_hbm.at[i, at], out_sem.at[i, part])

    def sums_copy(i):
        return pltpu.make_async_copy(sums_v.at[i], sums_hbm.at[i], out_sem.at[i, parts])

    for i, t in enumerate(steps):
        for copy in high_copies(i, t):
            copy.start()
        start_root(i, t, 0)
        for copy in low_copies(i, t):
            copy.start()
        for part in range(1, parts):
            start_root(i, t, part)
        for copy in own_copies(i, t):
            copy.start()
    for i, t in enumerate(steps):
        c = child(t)
        for copy in high_copies(i, t):
            copy.wait()
        for part in range(parts):
            pltpu.make_async_copy(a_f.at[i, part], a_f.at[i, part], a_sem.at[i, part]).wait()
            if part == 0:
                for copy in low_copies(i, t):
                    copy.wait()
            highs, lows = [], []
            for k in range(2 * per_range):
                value = a_f[i, part, table[c, per_range + k]]
                high = value.astype(jnp.bfloat16)
                highs.append(high)
                lows.append((value - high.astype(jnp.float32)).astype(jnp.bfloat16))
            high = jnp.concatenate(highs, axis=1)
            low = jnp.concatenate(lows, axis=1)
            total = jnp.dot(high, z_l[i], preferred_element_type=jnp.float32)
            total = total + jnp.dot(low, z_h[i], preferred_element_type=jnp.float32)
            total = total + jnp.dot(high, z_h[i], preferred_element_type=jnp.float32)
            out_v[i, pl.ds(part * PART, PART), :] = total
            out_copy(i, part).start()
        for copy in own_copies(i, t):
            copy.wait()

        def add(p, total, i=i):
            at = pl.ds(pl.multiple_of(p * 64, 64), 64)
            factor = b_h[i, at, :].astype(jnp.float32) + b_l[i, at, :].astype(jnp.float32)
            return total + jnp.sum((factor * out_v[i, at, :]).reshape(8, 8, -1), axis=0)

        sums_v[i] = lax.fori_loop(0, rows // 64, add, jnp.zeros(sums_v.shape[1:], jnp.float32))
        sums_copy(i).start()
    for i in range(len(steps)):
        for part in range(parts):
            out_copy(i, part).wait()
        sums_copy(i).wait()


def product(steps, table, root, high, low):
    rows, cols = high.shape[1:]
    count = len(steps)
    any_spec = pl.BlockSpec(memory_space=pl.ANY)
    return pl.pallas_call(
        functools.partial(product_kernel, steps),
        out_shape=[
            jax.ShapeDtypeStruct((count, rows, cols), jnp.float32),
            jax.ShapeDtypeStruct((count, 8, cols), jnp.float32),
        ],
        in_specs=[pl.BlockSpec(memory_space=pltpu.SMEM)] + [any_spec] * 3,
        out_specs=[any_spec] * 2,
        scratch_shapes=[
            pltpu.VMEM((count, rows // PART, root.shape[0], PART, BLOCK), jnp.float32),
            pltpu.VMEM((count, 2 * rows, cols), jnp.bfloat16),
            pltpu.VMEM((count, 2 * rows, cols), jnp.bfloat16),
            pltpu.VMEM((count, rows, cols), jnp.bfloat16),
            pltpu.VMEM((count, rows, cols), jnp.bfloat16),
            pltpu.VMEM((count, rows, cols), jnp.float32),
            pltpu.VMEM((count, 8, cols), jnp.float32),
            pltpu.SemaphoreType.DMA((count, rows // PART)),
            pltpu.SemaphoreType.DMA((count, 6)),
            pltpu.SemaphoreType.DMA((count, rows // PART + 1)),
        ],
        compiler_params=pltpu.CompilerParams(vmem_limit_bytes=PRODUCT_VMEM),
        cost_estimate=pl.CostEstimate(
            flops=count * 3 * 2 * rows * 2 * rows * cols,
            bytes_accessed=count * (12 * rows * rows + 16 * rows * cols),
            transcendentals=0,
        ),
    )(table, root, high, low)


def per_device(root_inverse, root_row, coupling, pivot_variance):
    zh = lax.axis_index("zh")
    y = lax.axis_index("y")
    x = lax.axis_index("x")
    core = lax.axis_index("core")
    rows, cols = coupling.shape[1:]
    ranges = root_row.shape[1] // rows
    per_range = rows // BLOCK
    half = rows // 2
    own_range = 2 * x + core
    device = (y * 4 + x) * 2 + core

    root = lax.all_gather(root_inverse, ("zh", "zl"), axis=0, tiled=False)

    pairs, holds = spread_plan()
    own = lax.ppermute(coupling[0], ("y", "x", "core"), pairs)
    along_x, along_y = opposite(4), opposite(4)
    beside = lax.ppermute(own, "core", CORES)
    near = lax.ppermute(own, ("x", "core"), along_x)
    near_beside = lax.ppermute(beside, ("x", "core"), along_x)
    far = lax.ppermute(near, ("x", "core"), along_x)
    pieces = [own, beside, near, near_beside, far]
    pieces += [lax.ppermute(p, "core", CORES) for p in (near, near_beside, far)]

    y_beside = lax.ppermute(coupling[0], "core", CORES)
    y_near = lax.ppermute(coupling[0], ("y", "core"), along_y)
    y_near_beside = lax.ppermute(y_beside, ("y", "core"), along_y)
    y_far = lax.ppermute(y_near, ("y", "core"), along_y)
    pieces += [coupling[0], y_near, y_far, lax.ppermute(y_near_beside, "core", CORES)]

    halves, own_children, found = piece_plan(holds)
    spots = lax.dynamic_slice(halves, (device, 0), (1, 8))[0]
    own_spots = lax.dynamic_slice(own_children, (device, 0), (1, 4))[0]
    child = zh * 4 + jnp.concatenate([spots & 3, own_spots])
    ranged = jnp.concatenate([y + 4 * (spots >> 2), jnp.full((4,), own_range, jnp.int32)])
    start_row = (child * ranges + ranged) * per_range
    high, low = spread(start_row, root_row.reshape(-1, BLOCK), pieces)

    block = (root_row[:, ::BLOCK] >> 7).reshape(-1, ranges, per_range)

    def blocks_of(r):
        return lax.dynamic_slice(block, (zh * 4, r, 0), (4, 1, per_range))[:, 0] & 7

    table = jnp.concatenate(
        [
            blocks_of(own_range),
            blocks_of(y),
            blocks_of(y + 4) + 8,
            lax.dynamic_slice(found, (device, 0, 0), (1, 4, 3))[0],
            jnp.broadcast_to(y, (4, 1)),
        ],
        axis=1,
    ).astype(jnp.int32)

    far, far_sums = product((2,), table, root, high, low)
    a = lax.ppermute(far[0, :half], "y", shift(4, 1))
    b = lax.ppermute(far[0, half:], "y", shift(4, -1))
    near, near_sums = product((1, 3), table, root, high, low)
    up = lax.ppermute(near[0, half:], "y", shift(4, 1))
    down = lax.ppermute(near[1, :half], "y", shift(4, -1))
    up_far = lax.ppermute(near[0, :half] + a, "y", shift(4, 1))
    down_far = lax.ppermute(near[1, half:] + b, "y", shift(4, -1))
    home, home_sums = product((0,), table, root, high, low)
    summed = jnp.concatenate([home[0, :half] + up_far + down, home[0, half:] + up + down_far])

    own_place = lax.dynamic_slice(root_row, (zh * 4 + y, own_range * rows), (1, rows))[0]
    own_place = jnp.where(own_place >= 0, own_place & (BLOCK - 1), -1).reshape(per_range, BLOCK)
    hot = (own_place[:, :, None] == jnp.arange(BLOCK, dtype=jnp.int32)).astype(jnp.float32)
    result = -jnp.einsum(
        "iuo,ion->iun", hot, summed.reshape(per_range, BLOCK, cols), precision=lax.Precision.HIGHEST
    )

    sums = (
        home_sums[0]
        + lax.ppermute(far_sums[0], "y", shift(4, 2))
        + lax.ppermute(near_sums[0], "y", shift(4, 1))
        + lax.ppermute(near_sums[1], "y", shift(4, -1))
    )
    marginal = pivot_variance + lax.psum(jnp.sum(sums, axis=0, keepdims=True), ("x", "core"))
    return result.reshape(1, rows, cols), marginal


def solution(mesh):
    split = Mesh(mesh.devices.reshape(2, 4, 4, 2, 8), ("zh", "y", "x", "core", "zl"))
    leaf, row, col = ("zh", "y"), ("x", "core"), "zl"
    return jax.shard_map(
        per_device,
        mesh=split,
        in_specs=(P(row, ("zh", "y", "zl")), P(), P(leaf, row, col), P(leaf, col)),
        out_specs=(P(leaf, row, col), P(leaf, col)),
        check_vma=False,
    )
```

```python
import functools

import jax
import jax.numpy as jnp
from jax import lax
from jax.experimental import pallas as pl
from jax.experimental.pallas import tpu as pltpu
from jax.sharding import Mesh, PartitionSpec as P

BLOCK = 128
PART = 256
SLOTS = 4
VMEM_BYTES = 20 * 1024 * 1024
CORES = [(0, 1), (1, 0)]
SPREAD_X = (
    (3, 1, 0, 0),
    (0, 3, 0, 1),
    (1, 2, 0, 1),
    (2, 0, 1, 1),
    (2, 2, 1, 3),
    (3, 1, 2, 2),
    (3, 0, 2, 3),
    (3, 2, 3, 0),
)


def shift(size, step):
    return [(i, (i + step) % size) for i in range(size)]


def opposite(size, way=1):
    return [
        (2 * i + c, (i + way * (1 - 2 * c)) % size * 2 + c) for i in range(size) for c in range(2)
    ]


def spread_plan():
    pairs, holds, taken = [], {}, {}
    for y in range(4):
        for r in range(8):
            to = (SPREAD_X[r][y], r % 4)
            core = taken.get(to, 0)
            taken[to] = core + 1
            pairs.append(((y * 4 + r // 2) * 2 + r % 2, (to[1] * 4 + to[0]) * 2 + core))
            holds[(to[1], to[0], core)] = (r // 4, y)
    return pairs, holds


def piece_plan(holds):
    halves, own, found = [], [], []
    for y in range(4):
        for x in range(4):
            for c in range(2):
                d = 2 * c - 1
                at = [
                    (x, c),
                    (x, 1 - c),
                    (x + d, c),
                    (x + d, 1 - c),
                    (x + 2, c),
                    (x - d, 1 - c),
                    (x - d, c),
                    (x + 2, 1 - c),
                ]
                has = [holds[(y, px % 4, pc)] for px, pc in at]
                mine = [y, (y + d) % 4, (y + 2) % 4, (y - d) % 4]
                halves.append([h * 4 + k for h, k in has])
                own.append(mine)
                found.append(
                    [[has.index((0, k)), has.index((1, k)), 8 + mine.index(k)] for k in range(4)]
                )
    return [jnp.array(v, jnp.int32) for v in (halves, own, found)]


def spread_kernel(start_row, rows_ref, *rest):
    pieces = rest[:12]
    high_ref, low_ref, z_f, in_sem = rest[12:]
    slots, rows = z_f.shape[:2]

    def fetch(i):
        return pltpu.make_async_copy(pieces[i], z_f.at[i % slots], in_sem.at[i])

    for i in range(slots):
        fetch(i).start()
    row = lax.broadcasted_iota(jnp.int32, (BLOCK, BLOCK), 0)
    for at in range(len(pieces)):
        fetch(at).wait()

        def one(i, carry, at=at):
            here = pl.ds(pl.multiple_of(i * BLOCK, BLOCK), BLOCK)
            value = z_f[at % slots, here, :]
            high = value.astype(jnp.bfloat16)
            low = (value - high.astype(jnp.float32)).astype(jnp.bfloat16)
            place = rows_ref[pl.ds(start_row[at] + i, 1), :]
            place = jnp.where(place >= 0, place & (BLOCK - 1), -1)
            hot = (place == row).astype(jnp.float32).astype(jnp.bfloat16)
            high_ref[at, here, :] = jnp.dot(
                hot, high, preferred_element_type=jnp.float32
            ).astype(jnp.bfloat16)
            low_ref[at, here, :] = jnp.dot(
                hot, low, preferred_element_type=jnp.float32
            ).astype(jnp.bfloat16)
            return carry

        lax.fori_loop(0, rows // BLOCK, one, 0, unroll=3)
        if at + slots < len(pieces):
            fetch(at + slots).start()


def spread(start_row, root_row, pieces):
    rows, cols = pieces[0].shape
    any_spec = pl.BlockSpec(memory_space=pl.ANY)
    vmem = pl.BlockSpec(memory_space=pltpu.VMEM)
    shape = (len(pieces), rows, cols)
    return pl.pallas_call(
        spread_kernel,
        out_shape=[pltpu.VMEM(shape, jnp.bfloat16)] * 2,
        in_specs=[pl.BlockSpec(memory_space=pltpu.SMEM), vmem] + [any_spec] * len(pieces),
        out_specs=[vmem] * 2,
        scratch_shapes=[
            pltpu.VMEM((SLOTS, rows, cols), jnp.float32),
            pltpu.SemaphoreType.DMA((len(pieces),)),
        ],
        compiler_params=pltpu.CompilerParams(vmem_limit_bytes=VMEM_BYTES),
        cost_estimate=pl.CostEstimate(
            flops=12 * 4 * rows * BLOCK * cols, bytes_accessed=48 * rows * cols, transcendentals=0
        ),
    )(start_row, root_row, *pieces)


def product_kernel(call, table, root, high_ref, low_ref, out, sums):
    rows = out.shape[0]
    per_range = rows // BLOCK
    per_part = PART // BLOCK
    c = table[call, 3 * per_range + 3]
    spots = [table[c, 3 * per_range + i] for i in range(3)]
    high_z = jnp.concatenate([high_ref[spots[0]], high_ref[spots[1]]], axis=0)
    low_z = jnp.concatenate([low_ref[spots[0]], low_ref[spots[1]]], axis=0)

    def one(part, total):
        at = [
            pl.ds(pl.multiple_of(table[c, part * per_part + m] * BLOCK, BLOCK), BLOCK)
            for m in range(per_part)
        ]
        highs, lows = [], []
        for k in range(2 * per_range):
            kb = table[c, per_range + k]
            value = jnp.concatenate([root[kb, here, :] for here in at], axis=0)
            high = value.astype(jnp.bfloat16)
            highs.append(high)
            lows.append((value - high.astype(jnp.float32)).astype(jnp.bfloat16))
        high = jnp.concatenate(highs, axis=1)
        low = jnp.concatenate(lows, axis=1)
        value = jnp.dot(high, low_z, preferred_element_type=jnp.float32)
        value = value + jnp.dot(low, high_z, preferred_element_type=jnp.float32)
        value = value + jnp.dot(high, high_z, preferred_element_type=jnp.float32)
        here = pl.ds(pl.multiple_of(part * PART, PART), PART)
        out[here, :] = value
        factor = high_ref[spots[2], here, :].astype(jnp.float32) + low_ref[
            spots[2], here, :
        ].astype(jnp.float32)
        return total + jnp.sum((factor * value).reshape(PART // 8, 8, -1), axis=0)

    sums[...] = lax.fori_loop(0, rows // PART, one, jnp.zeros(sums.shape, jnp.float32))


def product(call, table, root, high, low):
    rows, cols = high.shape[1:]
    vmem = pl.BlockSpec(memory_space=pltpu.VMEM)
    return pl.pallas_call(
        functools.partial(product_kernel, call),
        out_shape=[
            jax.ShapeDtypeStruct((rows, cols), jnp.float32),
            jax.ShapeDtypeStruct((8, cols), jnp.float32),
        ],
        in_specs=[pl.BlockSpec(memory_space=pltpu.SMEM)] + [vmem] * 3,
        out_specs=[vmem] * 2,
        compiler_params=pltpu.CompilerParams(vmem_limit_bytes=VMEM_BYTES),
        cost_estimate=pl.CostEstimate(
            flops=3 * 2 * rows * 2 * rows * cols, bytes_accessed=4 * rows * cols, transcendentals=0
        ),
    )(table, root, high, low)


def per_device(root_inverse, root_row, coupling, pivot_variance):
    zh = lax.axis_index("zh")
    y = lax.axis_index("y")
    x = lax.axis_index("x")
    core = lax.axis_index("core")
    rows, cols = coupling.shape[1:]
    ranges = root_row.shape[1] // rows
    per_range = rows // BLOCK
    half = rows // 2
    own_range = 2 * x + core
    device = (y * 4 + x) * 2 + core

    root = lax.all_gather(root_inverse, ("zh", "zl"), axis=0, tiled=False)

    pairs, holds = spread_plan()
    own = lax.ppermute(coupling[0], ("y", "x", "core"), pairs)
    along_x, along_y = opposite(4), opposite(4)
    beside = lax.ppermute(own, "core", CORES)
    near = lax.ppermute(own, ("x", "core"), along_x)
    near_beside = lax.ppermute(beside, ("x", "core"), along_x)
    far = lax.ppermute(near, ("x", "core"), along_x)
    pieces = [own, beside, near, near_beside, far]
    pieces += [lax.ppermute(p, "core", CORES) for p in (near, near_beside, far)]

    y_beside = lax.ppermute(coupling[0], "core", CORES)
    y_near = lax.ppermute(coupling[0], ("y", "core"), along_y)
    y_near_beside = lax.ppermute(y_beside, ("y", "core"), along_y)
    y_far = lax.ppermute(y_near, ("y", "core"), along_y)
    pieces += [coupling[0], y_near, y_far, lax.ppermute(y_near_beside, "core", CORES)]

    halves, own_children, found = piece_plan(holds)
    spots = lax.dynamic_slice(halves, (device, 0), (1, 8))[0]
    own_spots = lax.dynamic_slice(own_children, (device, 0), (1, 4))[0]
    child = zh * 4 + jnp.concatenate([spots & 3, own_spots])
    ranged = jnp.concatenate([y + 4 * (spots >> 2), jnp.full((4,), own_range, jnp.int32)])
    start_row = (child * ranges + ranged) * per_range
    high, low = spread(start_row, root_row.reshape(-1, BLOCK), pieces)

    block = (root_row[:, ::BLOCK] >> 7).reshape(-1, ranges, per_range)

    def blocks_of(r):
        return lax.dynamic_slice(block, (zh * 4, r, 0), (4, 1, per_range))[:, 0] & 7

    order = (y + jnp.stack([2, 3 - 2 * core, 1 + 2 * core, 0])) & 3
    table = jnp.concatenate(
        [
            blocks_of(own_range),
            blocks_of(y),
            blocks_of(y + 4) + 8,
            lax.dynamic_slice(found, (device, 0, 0), (1, 4, 3))[0],
            order[:, None],
        ],
        axis=1,
    ).astype(jnp.int32)

    root = pltpu.with_memory_space_constraint(root.reshape(-1, *root_inverse.shape), pltpu.VMEM)
    high = pltpu.with_memory_space_constraint(high, pltpu.VMEM)
    low = pltpu.with_memory_space_constraint(low, pltpu.VMEM)
    far, far_sums = product(0, table, root, high, low)
    passed = lax.ppermute(far, ("y", "core"), opposite(4))
    first, first_sums = product(1, table, root, high, low)
    back = lax.ppermute(first, ("y", "core"), opposite(4, -1))
    second, second_sums = product(2, table, root, high, low)
    forth = lax.ppermute(second + passed, ("y", "core"), opposite(4))
    home, home_sums = product(3, table, root, high, low)
    summed = home + forth + back

    own_place = lax.dynamic_slice(root_row, (zh * 4 + y, own_range * rows), (1, rows))[0]
    own_place = jnp.where(own_place >= 0, own_place & (BLOCK - 1), -1).reshape(per_range, BLOCK)
    hot = (own_place[:, :, None] == jnp.arange(BLOCK, dtype=jnp.int32)).astype(jnp.float32)
    result = -jnp.einsum(
        "iuo,ion->iun", hot, summed.reshape(per_range, BLOCK, cols), precision=lax.Precision.HIGHEST
    )

    sums = jnp.stack(
        [
            home_sums,
            jnp.where(core == 0, second_sums, first_sums),
            far_sums,
            jnp.where(core == 0, first_sums, second_sums),
        ]
    )
    sums = lax.psum(jnp.sum(sums, axis=1), ("x", "core"))
    marginal = pivot_variance + sums[:1]
    for step in range(1, 4):
        marginal = marginal + lax.ppermute(sums[step : step + 1], "y", shift(4, step))
    return result.reshape(1, rows, cols), marginal


def solution(mesh):
    split = Mesh(mesh.devices.reshape(2, 4, 4, 2, 8), ("zh", "y", "x", "core", "zl"))
    leaf, row, col = ("zh", "y"), ("x", "core"), "zl"
    return jax.shard_map(
        per_device,
        mesh=split,
        in_specs=(P(row, ("zh", "y", "zl")), P(), P(leaf, row, col), P(leaf, col)),
        out_specs=(P(leaf, row, col), P(leaf, col)),
        check_vma=False,
    )
```

```python
import functools

import jax
import jax.numpy as jnp
from jax import lax
from jax.experimental import pallas as pl
from jax.experimental.pallas import tpu as pltpu
from jax.sharding import Mesh, PartitionSpec as P

BLOCK = 128
PART = 256
SLOTS = 4
VMEM_BYTES = 24 * 1024 * 1024
CORES = [(0, 1), (1, 0)]
SPREAD_X = (
    (3, 1, 0, 0),
    (0, 3, 0, 1),
    (1, 2, 0, 1),
    (2, 0, 1, 1),
    (2, 2, 1, 3),
    (3, 1, 2, 2),
    (3, 0, 2, 3),
    (3, 2, 3, 0),
)


def shift(size, step):
    return [(i, (i + step) % size) for i in range(size)]


def opposite(size, way=1):
    return [
        (2 * i + c, (i + way * (1 - 2 * c)) % size * 2 + c) for i in range(size) for c in range(2)
    ]


def spread_plan():
    pairs, holds, taken = [], {}, {}
    for y in range(4):
        for r in range(8):
            to = (SPREAD_X[r][y], r % 4)
            core = taken.get(to, 0)
            taken[to] = core + 1
            pairs.append(((y * 4 + r // 2) * 2 + r % 2, (to[1] * 4 + to[0]) * 2 + core))
            holds[(to[1], to[0], core)] = (r // 4, y)
    return pairs, holds


def piece_plan(holds):
    halves, found = [], []
    for y in range(4):
        for x in range(4):
            for c in range(2):
                d = 2 * c - 1
                at = [
                    (x, c),
                    (x, 1 - c),
                    (x + d, c),
                    (x + d, 1 - c),
                    (x + 2, c),
                    (x - d, 1 - c),
                    (x - d, c),
                    (x + 2, 1 - c),
                ]
                has = [holds[(y, px % 4, pc)] for px, pc in at]
                halves.append([h * 4 + k for h, k in has])
                found.append([[has.index((0, k)), has.index((1, k))] for k in range(4)])
    return [jnp.array(v, jnp.int32) for v in (halves, found)]


def spread_kernel(start_row, rows_ref, *rest):
    pieces = rest[:8]
    high_hbm, low_hbm, z_f, z_h, z_l, in_sem, out_sem = rest[8:]
    slots, rows = z_f.shape[:2]

    def fetch(i):
        return pltpu.make_async_copy(pieces[i], z_f.at[i % slots], in_sem.at[i])

    def store(i):
        return [
            pltpu.make_async_copy(z_h.at[i % slots], high_hbm.at[i], out_sem.at[2 * i]),
            pltpu.make_async_copy(z_l.at[i % slots], low_hbm.at[i], out_sem.at[2 * i + 1]),
        ]

    for i in range(slots):
        fetch(i).start()
    row = lax.broadcasted_iota(jnp.int32, (BLOCK, BLOCK), 0)
    for at in range(len(pieces)):
        fetch(at).wait()
        if at >= slots:
            for copy in store(at - slots):
                copy.wait()

        def one(i, carry, at=at):
            here = pl.ds(pl.multiple_of(i * BLOCK, BLOCK), BLOCK)
            value = z_f[at % slots, here, :]
            high = value.astype(jnp.bfloat16)
            low = (value - high.astype(jnp.float32)).astype(jnp.bfloat16)
            place = rows_ref[pl.ds(start_row[at] + i, 1), :]
            place = jnp.where(place >= 0, place & (BLOCK - 1), -1)
            hot = (place == row).astype(jnp.float32).astype(jnp.bfloat16)
            z_h[at % slots, here, :] = jnp.dot(
                hot, high, preferred_element_type=jnp.float32
            ).astype(jnp.bfloat16)
            z_l[at % slots, here, :] = jnp.dot(
                hot, low, preferred_element_type=jnp.float32
            ).astype(jnp.bfloat16)
            return carry

        lax.fori_loop(0, rows // BLOCK, one, 0, unroll=3)
        for copy in store(at):
            copy.start()
        if at + slots < len(pieces):
            fetch(at + slots).start()
    for at in range(len(pieces) - slots, len(pieces)):
        for copy in store(at):
            copy.wait()


def spread(start_row, root_row, pieces):
    rows, cols = pieces[0].shape
    any_spec = pl.BlockSpec(memory_space=pl.ANY)
    shape = (len(pieces), rows, cols)
    held = (SLOTS, rows, cols)
    return pl.pallas_call(
        spread_kernel,
        out_shape=[jax.ShapeDtypeStruct(shape, jnp.bfloat16)] * 2,
        in_specs=[
            pl.BlockSpec(memory_space=pltpu.SMEM),
            pl.BlockSpec(memory_space=pltpu.VMEM),
        ]
        + [any_spec] * len(pieces),
        out_specs=[any_spec] * 2,
        scratch_shapes=[
            pltpu.VMEM(held, jnp.float32),
            pltpu.VMEM(held, jnp.bfloat16),
            pltpu.VMEM(held, jnp.bfloat16),
            pltpu.SemaphoreType.DMA((len(pieces),)),
            pltpu.SemaphoreType.DMA((2 * len(pieces),)),
        ],
        compiler_params=pltpu.CompilerParams(vmem_limit_bytes=VMEM_BYTES),
        cost_estimate=pl.CostEstimate(
            flops=8 * 4 * rows * BLOCK * cols, bytes_accessed=64 * rows * cols, transcendentals=0
        ),
    )(start_row, root_row, *pieces)


def product_kernel(call, table, root_hbm, high_hbm, low_hbm, out, a_f, z_h, z_l, a_sem, z_sem):
    rows = out.shape[0]
    per_range = rows // BLOCK
    per_part = PART // BLOCK
    parts = rows // PART
    c = table[call, 3 * per_range + 2]

    def factor_copies(source, target, first):
        return [
            pltpu.make_async_copy(
                source.at[table[c, 3 * per_range + side]],
                target.at[pl.ds(side * rows, rows)],
                z_sem.at[first + side],
            )
            for side in range(2)
        ]

    def start_root(part):
        for m in range(per_part):
            mb = pl.multiple_of(table[c, part * per_part + m] * BLOCK, BLOCK)
            pltpu.make_async_copy(
                root_hbm.at[:, pl.ds(mb, BLOCK)],
                a_f.at[part, :, pl.ds(m * BLOCK, BLOCK)],
                a_sem.at[part],
            ).start()

    highs_in = factor_copies(high_hbm, z_h, 0)
    lows_in = factor_copies(low_hbm, z_l, 2)
    start_root(0)
    for copy in highs_in + lows_in:
        copy.start()
    start_root(1)
    for part in range(parts):
        pltpu.make_async_copy(a_f.at[part], a_f.at[part], a_sem.at[part]).wait()
        if part == 0:
            for copy in highs_in:
                copy.wait()
        if part + 2 < parts:
            start_root(part + 2)
        highs, lows = [], []
        for k in range(2 * per_range):
            value = a_f[part, table[c, per_range + k]]
            high = value.astype(jnp.bfloat16)
            highs.append(high)
            lows.append((value - high.astype(jnp.float32)).astype(jnp.bfloat16))
        high = jnp.concatenate(highs, axis=1)
        low = jnp.concatenate(lows, axis=1)
        value = jnp.dot(high, z_h[...], preferred_element_type=jnp.float32)
        value = value + jnp.dot(low, z_h[...], preferred_element_type=jnp.float32)
        if part == 0:
            for copy in lows_in:
                copy.wait()
        value = value + jnp.dot(high, z_l[...], preferred_element_type=jnp.float32)
        out[part * PART : (part + 1) * PART, :] = value


def product(call, table, root, high, low):
    rows, cols = high.shape[1:]
    any_spec = pl.BlockSpec(memory_space=pl.ANY)
    root, high, low = [pltpu.with_memory_space_constraint(v, pltpu.HBM) for v in (root, high, low)]
    return pl.pallas_call(
        functools.partial(product_kernel, call),
        out_shape=jax.ShapeDtypeStruct((rows, cols), jnp.float32),
        in_specs=[pl.BlockSpec(memory_space=pltpu.SMEM)] + [any_spec] * 3,
        out_specs=pl.BlockSpec(memory_space=pltpu.VMEM),
        scratch_shapes=[
            pltpu.VMEM((rows // PART, root.shape[0], PART, BLOCK), jnp.float32),
            pltpu.VMEM((2 * rows, cols), jnp.bfloat16),
            pltpu.VMEM((2 * rows, cols), jnp.bfloat16),
            pltpu.SemaphoreType.DMA((rows // PART,)),
            pltpu.SemaphoreType.DMA((4,)),
        ],
        compiler_params=pltpu.CompilerParams(vmem_limit_bytes=VMEM_BYTES),
        cost_estimate=pl.CostEstimate(
            flops=3 * 2 * rows * 2 * rows * cols, bytes_accessed=12 * rows * rows, transcendentals=0
        ),
    )(table, root, high, low)


def per_device(root_inverse, root_row, coupling, pivot_variance):
    zh = lax.axis_index("zh")
    y = lax.axis_index("y")
    x = lax.axis_index("x")
    core = lax.axis_index("core")
    rows, cols = coupling.shape[1:]
    ranges = root_row.shape[1] // rows
    per_range = rows // BLOCK
    own_range = 2 * x + core
    device = (y * 4 + x) * 2 + core

    root = lax.all_gather(root_inverse, ("zh", "zl"), axis=0, tiled=False)

    pairs, holds = spread_plan()
    own = lax.ppermute(coupling[0], ("y", "x", "core"), pairs)
    along_x = opposite(4)
    beside = lax.ppermute(own, "core", CORES)
    near = lax.ppermute(own, ("x", "core"), along_x)
    near_beside = lax.ppermute(beside, ("x", "core"), along_x)
    far = lax.ppermute(near, ("x", "core"), along_x)
    pieces = [own, beside, near, near_beside, far]
    pieces += [lax.ppermute(p, "core", CORES) for p in (near, near_beside, far)]

    halves, found = piece_plan(holds)
    spots = lax.dynamic_slice(halves, (device, 0), (1, 8))[0]
    start_row = ((zh * 4 + (spots & 3)) * ranges + y + 4 * (spots >> 2)) * per_range
    high, low = spread(start_row, root_row.reshape(-1, BLOCK), pieces)

    block = (root_row[:, ::BLOCK] >> 7).reshape(-1, ranges, per_range)

    def blocks_of(r):
        return lax.dynamic_slice(block, (zh * 4, r, 0), (4, 1, per_range))[:, 0] & 7

    order = (y + jnp.stack([2, 3 - 2 * core, 1 + 2 * core, 0])) & 3
    table = jnp.concatenate(
        [
            blocks_of(own_range),
            blocks_of(y),
            blocks_of(y + 4) + 8,
            lax.dynamic_slice(found, (device, 0, 0), (1, 4, 2))[0],
            order[:, None],
        ],
        axis=1,
    ).astype(jnp.int32)

    root = root.reshape(-1, *root_inverse.shape)
    far = product(0, table, root, high, low)
    passed = lax.ppermute(far, ("y", "core"), opposite(4))
    first = product(1, table, root, high, low)
    back = lax.ppermute(first, ("y", "core"), opposite(4, -1))
    second = product(2, table, root, high, low)
    forth = lax.ppermute(second + passed, ("y", "core"), opposite(4))
    home = product(3, table, root, high, low)
    summed = home + forth + back

    own_place = lax.dynamic_slice(root_row, (zh * 4 + y, own_range * rows), (1, rows))[0]
    own_place = jnp.where(own_place >= 0, own_place & (BLOCK - 1), -1).reshape(per_range, BLOCK)
    hot = (own_place[:, :, None] == jnp.arange(BLOCK, dtype=jnp.int32)).astype(jnp.float32)
    result = -jnp.einsum(
        "iuo,ion->iun", hot, summed.reshape(per_range, BLOCK, cols), precision=lax.Precision.HIGHEST
    )

    result = result.reshape(1, rows, cols)
    sums = jnp.sum(coupling * result, axis=1)
    sums = lax.all_to_all(
        jnp.broadcast_to(sums, (8, cols)), ("x", "core"), split_axis=0, concat_axis=0, tiled=True
    )
    return result, pivot_variance - jnp.sum(sums, axis=0, keepdims=True)


def solution(mesh):
    split = Mesh(mesh.devices.reshape(2, 4, 4, 2, 8), ("zh", "y", "x", "core", "zl"))
    leaf, row, col = ("zh", "y"), ("x", "core"), "zl"
    return jax.shard_map(
        per_device,
        mesh=split,
        in_specs=(P(row, ("zh", "y", "zl")), P(), P(leaf, row, col), P(leaf, col)),
        out_specs=(P(leaf, row, col), P(leaf, col)),
        check_vma=False,
    )
```

```python
import functools

import jax
import jax.numpy as jnp
from jax import lax
from jax.experimental import pallas as pl
from jax.experimental.pallas import tpu as pltpu
from jax.sharding import Mesh, PartitionSpec as P

BLOCK = 128
PART = 256
SLOTS = 4
VMEM_BYTES = 24 * 1024 * 1024
CORES = [(0, 1), (1, 0)]
SPREAD_X = (
    (3, 1, 0, 0),
    (0, 3, 0, 1),
    (1, 2, 0, 1),
    (2, 0, 1, 1),
    (2, 2, 1, 3),
    (3, 1, 2, 2),
    (3, 0, 2, 3),
    (3, 2, 3, 0),
)


def shift(size, step):
    return [(i, (i + step) % size) for i in range(size)]


def opposite(size, way=1):
    return [
        (2 * i + c, (i + way * (1 - 2 * c)) % size * 2 + c) for i in range(size) for c in range(2)
    ]


def spread_plan():
    pairs, holds, taken = [], {}, {}
    for y in range(4):
        for r in range(8):
            to = (SPREAD_X[r][y], r % 4)
            core = taken.get(to, 0)
            taken[to] = core + 1
            pairs.append(((y * 4 + r // 2) * 2 + r % 2, (to[1] * 4 + to[0]) * 2 + core))
            holds[(to[1], to[0], core)] = (r // 4, y)
    return pairs, holds


def piece_plan(holds):
    halves, found = [], []
    for y in range(4):
        for x in range(4):
            for c in range(2):
                d = 2 * c - 1
                at = [
                    (x, c),
                    (x, 1 - c),
                    (x + d, c),
                    (x + d, 1 - c),
                    (x + 2, c),
                    (x - d, 1 - c),
                    (x - d, c),
                    (x + 2, 1 - c),
                ]
                has = [holds[(y, px % 4, pc)] for px, pc in at]
                halves.append([h * 4 + k for h, k in has])
                found.append([[has.index((0, k)), has.index((1, k))] for k in range(4)])
    return [jnp.array(v, jnp.int32) for v in (halves, found)]


def spread_kernel(start_row, rows_ref, *rest):
    pieces = rest[:-7]
    high_hbm, low_hbm, z_f, z_h, z_l, in_sem, out_sem = rest[-7:]
    slots, rows = z_f.shape[:2]

    def fetch(i):
        return pltpu.make_async_copy(pieces[i], z_f.at[i % slots], in_sem.at[i])

    def store(i):
        return [
            pltpu.make_async_copy(z_h.at[i % slots], high_hbm.at[i], out_sem.at[2 * i]),
            pltpu.make_async_copy(z_l.at[i % slots], low_hbm.at[i], out_sem.at[2 * i + 1]),
        ]

    for i in range(slots):
        fetch(i).start()
    row = lax.broadcasted_iota(jnp.int32, (BLOCK, BLOCK), 0)
    for at in range(len(pieces)):
        fetch(at).wait()
        if at >= slots:
            for copy in store(at - slots):
                copy.wait()

        def one(i, carry, at=at):
            here = pl.ds(pl.multiple_of(i * BLOCK, BLOCK), BLOCK)
            value = z_f[at % slots, here, :]
            high = value.astype(jnp.bfloat16)
            low = (value - high.astype(jnp.float32)).astype(jnp.bfloat16)
            place = rows_ref[pl.ds(start_row[at] + i, 1), :]
            place = jnp.where(place >= 0, place & (BLOCK - 1), -1)
            hot = (place == row).astype(jnp.float32).astype(jnp.bfloat16)
            z_h[at % slots, here, :] = jnp.dot(
                hot, high, preferred_element_type=jnp.float32
            ).astype(jnp.bfloat16)
            z_l[at % slots, here, :] = jnp.dot(
                hot, low, preferred_element_type=jnp.float32
            ).astype(jnp.bfloat16)
            return carry

        lax.fori_loop(0, rows // BLOCK, one, 0, unroll=3)
        for copy in store(at):
            copy.start()
        if at + slots < len(pieces):
            fetch(at + slots).start()
    for at in range(len(pieces) - slots, len(pieces)):
        for copy in store(at):
            copy.wait()


def spread(start_row, root_row, pieces):
    rows, cols = pieces[0].shape
    any_spec = pl.BlockSpec(memory_space=pl.ANY)
    shape = (len(pieces), rows, cols)
    held = (SLOTS, rows, cols)
    return pl.pallas_call(
        spread_kernel,
        out_shape=[jax.ShapeDtypeStruct(shape, jnp.bfloat16)] * 2,
        in_specs=[
            pl.BlockSpec(memory_space=pltpu.SMEM),
            pl.BlockSpec(memory_space=pltpu.VMEM),
        ]
        + [any_spec] * len(pieces),
        out_specs=[any_spec] * 2,
        scratch_shapes=[
            pltpu.VMEM(held, jnp.float32),
            pltpu.VMEM(held, jnp.bfloat16),
            pltpu.VMEM(held, jnp.bfloat16),
            pltpu.SemaphoreType.DMA((len(pieces),)),
            pltpu.SemaphoreType.DMA((2 * len(pieces),)),
        ],
        compiler_params=pltpu.CompilerParams(vmem_limit_bytes=VMEM_BYTES),
        cost_estimate=pl.CostEstimate(
            flops=10 * 4 * rows * BLOCK * cols, bytes_accessed=80 * rows * cols, transcendentals=0
        ),
    )(start_row, root_row, *pieces)


def product_kernel(call, table, root_hbm, high_hbm, low_hbm, out, a_f, z_h, z_l, a_sem, z_sem):
    rows = out.shape[0]
    per_range = rows // BLOCK
    per_part = PART // BLOCK
    parts = rows // PART
    c = table[call, 3 * per_range + 2]

    def factor_copies(source, target, first):
        return [
            pltpu.make_async_copy(
                source.at[table[c, 3 * per_range + side]],
                target.at[pl.ds(side * rows, rows)],
                z_sem.at[first + side],
            )
            for side in range(2)
        ]

    def start_root(part):
        for m in range(per_part):
            mb = pl.multiple_of(table[c, part * per_part + m] * BLOCK, BLOCK)
            pltpu.make_async_copy(
                root_hbm.at[:, pl.ds(mb, BLOCK)],
                a_f.at[part, :, pl.ds(m * BLOCK, BLOCK)],
                a_sem.at[part],
            ).start()

    highs_in = factor_copies(high_hbm, z_h, 0)
    lows_in = factor_copies(low_hbm, z_l, 2)
    start_root(0)
    for copy in highs_in + lows_in:
        copy.start()
    start_root(1)
    for part in range(parts):
        pltpu.make_async_copy(a_f.at[part], a_f.at[part], a_sem.at[part]).wait()
        if part == 0:
            for copy in highs_in:
                copy.wait()
        if part + 2 < parts:
            start_root(part + 2)
        highs, lows = [], []
        for k in range(2 * per_range):
            value = a_f[part, table[c, per_range + k]]
            high = value.astype(jnp.bfloat16)
            highs.append(high)
            lows.append((value - high.astype(jnp.float32)).astype(jnp.bfloat16))
        high = jnp.concatenate(highs, axis=1)
        low = jnp.concatenate(lows, axis=1)
        value = jnp.dot(high, z_h[...], preferred_element_type=jnp.float32)
        value = value + jnp.dot(low, z_h[...], preferred_element_type=jnp.float32)
        if part == 0:
            for copy in lows_in:
                copy.wait()
        value = value + jnp.dot(high, z_l[...], preferred_element_type=jnp.float32)
        out[part * PART : (part + 1) * PART, :] = value


def product(call, table, root, high, low):
    rows, cols = high.shape[1:]
    any_spec = pl.BlockSpec(memory_space=pl.ANY)
    root, high, low = [pltpu.with_memory_space_constraint(v, pltpu.HBM) for v in (root, high, low)]
    return pl.pallas_call(
        functools.partial(product_kernel, call),
        out_shape=jax.ShapeDtypeStruct((rows, cols), jnp.float32),
        in_specs=[pl.BlockSpec(memory_space=pltpu.SMEM)] + [any_spec] * 3,
        out_specs=pl.BlockSpec(memory_space=pltpu.VMEM),
        scratch_shapes=[
            pltpu.VMEM((rows // PART, root.shape[0], PART, BLOCK), jnp.float32),
            pltpu.VMEM((2 * rows, cols), jnp.bfloat16),
            pltpu.VMEM((2 * rows, cols), jnp.bfloat16),
            pltpu.SemaphoreType.DMA((rows // PART,)),
            pltpu.SemaphoreType.DMA((4,)),
        ],
        compiler_params=pltpu.CompilerParams(vmem_limit_bytes=VMEM_BYTES),
        cost_estimate=pl.CostEstimate(
            flops=3 * 2 * rows * 2 * rows * cols, bytes_accessed=12 * rows * rows, transcendentals=0
        ),
    )(table, root, high, low)


def weigh_kernel(piece, first, second, high_hbm, low_hbm, total, sums, high, low, sem):
    rows, cols = total.shape
    copies = [
        pltpu.make_async_copy(high_hbm.at[piece], high, sem.at[0]),
        pltpu.make_async_copy(low_hbm.at[piece], low, sem.at[1]),
    ]
    for copy in copies:
        copy.start()
    for copy in copies:
        copy.wait()

    def one(i, found):
        at = pl.ds(pl.multiple_of(i * 64, 64), 64)
        value = first[at, :] + second[at, :]
        total[at, :] = value
        factor = high[at, :].astype(jnp.float32) + low[at, :].astype(jnp.float32)
        return found + jnp.sum((factor * value).reshape(8, 8, cols), axis=0)

    found = lax.fori_loop(0, rows // 64, one, jnp.zeros((8, cols), jnp.float32))
    sums[...] = jnp.sum(found, axis=0, keepdims=True)


def weigh(piece, first, second, high, low):
    rows, cols = first.shape
    any_spec = pl.BlockSpec(memory_space=pl.ANY)
    vmem = pl.BlockSpec(memory_space=pltpu.VMEM)
    high, low = [pltpu.with_memory_space_constraint(v, pltpu.HBM) for v in (high, low)]
    return pl.pallas_call(
        functools.partial(weigh_kernel, piece),
        out_shape=[
            jax.ShapeDtypeStruct((rows, cols), jnp.float32),
            jax.ShapeDtypeStruct((1, cols), jnp.float32),
        ],
        in_specs=[vmem, vmem, any_spec, any_spec],
        out_specs=[vmem, vmem],
        scratch_shapes=[
            pltpu.VMEM((rows, cols), jnp.bfloat16),
            pltpu.VMEM((rows, cols), jnp.bfloat16),
            pltpu.SemaphoreType.DMA((2,)),
        ],
        compiler_params=pltpu.CompilerParams(vmem_limit_bytes=VMEM_BYTES),
        cost_estimate=pl.CostEstimate(
            flops=4 * rows * cols, bytes_accessed=16 * rows * cols, transcendentals=0
        ),
    )(first, second, high, low)


def per_device(root_inverse, root_row, coupling, pivot_variance):
    zh = lax.axis_index("zh")
    y = lax.axis_index("y")
    x = lax.axis_index("x")
    core = lax.axis_index("core")
    rows, cols = coupling.shape[1:]
    ranges = root_row.shape[1] // rows
    per_range = rows // BLOCK
    own_range = 2 * x + core
    device = (y * 4 + x) * 2 + core

    root = lax.all_gather(root_inverse, ("zh", "zl"), axis=0, tiled=False)

    pairs, holds = spread_plan()
    own = lax.ppermute(coupling[0], ("y", "x", "core"), pairs)
    along_x = opposite(4)
    beside = lax.ppermute(own, "core", CORES)
    near = lax.ppermute(own, ("x", "core"), along_x)
    near_beside = lax.ppermute(beside, ("x", "core"), along_x)
    far = lax.ppermute(near, ("x", "core"), along_x)
    pieces = [own, beside, near, near_beside, far]
    pieces += [lax.ppermute(p, "core", CORES) for p in (near, near_beside, far)]

    halves, found = piece_plan(holds)
    spots = lax.dynamic_slice(halves, (device, 0), (1, 8))[0]
    pieces += [coupling[0], lax.ppermute(coupling[0], ("y", "core"), opposite(4, -1))]
    child = zh * 4 + jnp.concatenate([spots & 3, jnp.stack([y, (y + 1 - 2 * core) & 3])])
    ranged = jnp.concatenate([y + 4 * (spots >> 2), jnp.stack([own_range, own_range])])
    start_row = (child * ranges + ranged) * per_range
    high, low = spread(start_row, root_row.reshape(-1, BLOCK), pieces)

    block = (root_row[:, ::BLOCK] >> 7).reshape(-1, ranges, per_range)

    def blocks_of(r):
        return lax.dynamic_slice(block, (zh * 4, r, 0), (4, 1, per_range))[:, 0] & 7

    order = (y + jnp.stack([2, 3 - 2 * core, 1 + 2 * core, 0])) & 3
    table = jnp.concatenate(
        [
            blocks_of(own_range),
            blocks_of(y),
            blocks_of(y + 4) + 8,
            lax.dynamic_slice(found, (device, 0, 0), (1, 4, 2))[0],
            order[:, None],
        ],
        axis=1,
    ).astype(jnp.int32)

    root = root.reshape(-1, *root_inverse.shape)
    far = product(0, table, root, high, low)
    passed = lax.ppermute(far, ("y", "core"), opposite(4))
    first = product(1, table, root, high, low)
    back = lax.ppermute(first, ("y", "core"), opposite(4, -1))
    second = product(2, table, root, high, low)
    last, last_sums = weigh(9, second, passed, high, low)
    table, last, last_sums = lax.optimization_barrier((table, last, last_sums))
    last_sums = lax.ppermute(last_sums, ("y", "core"), opposite(4))
    home = product(3, table, root, high, low)
    last, home, last_sums = lax.optimization_barrier((last, home, last_sums))
    forth = lax.ppermute(last, ("y", "core"), opposite(4))
    kept, sums = weigh(8, home, back, high, low)
    sums = lax.all_to_all(
        jnp.broadcast_to(sums + last_sums, (8, cols)),
        ("x", "core"),
        split_axis=0,
        concat_axis=0,
        tiled=True,
    )
    marginal = pivot_variance + jnp.sum(sums, axis=0, keepdims=True)
    kept, marginal = lax.optimization_barrier((kept, marginal))
    summed = kept + forth

    own_place = lax.dynamic_slice(root_row, (zh * 4 + y, own_range * rows), (1, rows))[0]
    own_place = jnp.where(own_place >= 0, own_place & (BLOCK - 1), -1).reshape(per_range, BLOCK)
    hot = (own_place[:, :, None] == jnp.arange(BLOCK, dtype=jnp.int32)).astype(jnp.float32)
    result = -jnp.einsum(
        "iuo,ion->iun", hot, summed.reshape(per_range, BLOCK, cols), precision=lax.Precision.HIGHEST
    )

    return result.reshape(1, rows, cols), marginal


def solution(mesh):
    split = Mesh(mesh.devices.reshape(2, 4, 4, 2, 8), ("zh", "y", "x", "core", "zl"))
    leaf, row, col = ("zh", "y"), ("x", "core"), "zl"
    return jax.shard_map(
        per_device,
        mesh=split,
        in_specs=(P(row, ("zh", "y", "zl")), P(), P(leaf, row, col), P(leaf, col)),
        out_specs=(P(leaf, row, col), P(leaf, col)),
        check_vma=False,
    )
```

```python
import functools

import jax
import jax.numpy as jnp
from jax import lax
from jax.experimental import pallas as pl
from jax.experimental.pallas import tpu as pltpu
from jax.sharding import Mesh, PartitionSpec as P

BLOCK = 128
PART = 256
SLOTS = 4
VMEM_BYTES = 24 * 1024 * 1024
CORES = [(0, 1), (1, 0)]
SPREAD_X = (
    (3, 1, 0, 0),
    (0, 3, 0, 1),
    (1, 2, 0, 1),
    (2, 0, 1, 1),
    (2, 2, 1, 3),
    (3, 1, 2, 2),
    (3, 0, 2, 3),
    (3, 2, 3, 0),
)


def shift(size, step):
    return [(i, (i + step) % size) for i in range(size)]


def opposite(size, way=1):
    return [
        (2 * i + c, (i + way * (1 - 2 * c)) % size * 2 + c) for i in range(size) for c in range(2)
    ]


def spread_plan():
    pairs, holds, taken = [], {}, {}
    for y in range(4):
        for r in range(8):
            to = (SPREAD_X[r][y], r % 4)
            core = taken.get(to, 0)
            taken[to] = core + 1
            pairs.append(((y * 4 + r // 2) * 2 + r % 2, (to[1] * 4 + to[0]) * 2 + core))
            holds[(to[1], to[0], core)] = (r // 4, y)
    return pairs, holds


def piece_plan(holds):
    halves, found = [], []
    for y in range(4):
        for x in range(4):
            for c in range(2):
                d = 2 * c - 1
                at = [
                    (x, c),
                    (x, 1 - c),
                    (x + d, c),
                    (x + d, 1 - c),
                    (x + 2, c),
                    (x - d, 1 - c),
                    (x - d, c),
                    (x + 2, 1 - c),
                ]
                has = [holds[(y, px % 4, pc)] for px, pc in at]
                halves.append([h * 4 + k for h, k in has])
                found.append([[has.index((0, k)), has.index((1, k))] for k in range(4)])
    return [jnp.array(v, jnp.int32) for v in (halves, found)]


def spread_kernel(start_row, rows_ref, *rest):
    pieces = rest[:-7]
    high_hbm, low_hbm, z_f, z_h, z_l, in_sem, out_sem = rest[-7:]
    slots, rows = z_f.shape[:2]

    def fetch(i):
        return pltpu.make_async_copy(pieces[i], z_f.at[i % slots], in_sem.at[i])

    def store(i):
        return [
            pltpu.make_async_copy(z_h.at[i % slots], high_hbm.at[i], out_sem.at[2 * i]),
            pltpu.make_async_copy(z_l.at[i % slots], low_hbm.at[i], out_sem.at[2 * i + 1]),
        ]

    for i in range(slots):
        fetch(i).start()
    row = lax.broadcasted_iota(jnp.int32, (BLOCK, BLOCK), 0)
    for at in range(len(pieces)):
        fetch(at).wait()
        if at >= slots:
            for copy in store(at - slots):
                copy.wait()

        def one(i, carry, at=at):
            here = pl.ds(pl.multiple_of(i * BLOCK, BLOCK), BLOCK)
            value = z_f[at % slots, here, :]
            high = value.astype(jnp.bfloat16)
            low = (value - high.astype(jnp.float32)).astype(jnp.bfloat16)
            place = rows_ref[pl.ds(start_row[at] + i, 1), :]
            place = jnp.where(place >= 0, place & (BLOCK - 1), -1)
            hot = (place == row).astype(jnp.float32).astype(jnp.bfloat16)
            z_h[at % slots, here, :] = jnp.dot(
                hot, high, preferred_element_type=jnp.float32
            ).astype(jnp.bfloat16)
            z_l[at % slots, here, :] = jnp.dot(
                hot, low, preferred_element_type=jnp.float32
            ).astype(jnp.bfloat16)
            return carry

        lax.fori_loop(0, rows // BLOCK, one, 0, unroll=3)
        for copy in store(at):
            copy.start()
        if at + slots < len(pieces):
            fetch(at + slots).start()
    for at in range(len(pieces) - slots, len(pieces)):
        for copy in store(at):
            copy.wait()


def spread(start_row, root_row, pieces):
    rows, cols = pieces[0].shape
    any_spec = pl.BlockSpec(memory_space=pl.ANY)
    shape = (len(pieces), rows, cols)
    held = (SLOTS, rows, cols)
    return pl.pallas_call(
        spread_kernel,
        out_shape=[pltpu.HBM(shape, jnp.bfloat16)] * 2,
        in_specs=[
            pl.BlockSpec(memory_space=pltpu.SMEM),
            pl.BlockSpec(memory_space=pltpu.VMEM),
        ]
        + [any_spec] * len(pieces),
        out_specs=[pl.BlockSpec(memory_space=pltpu.HBM)] * 2,
        scratch_shapes=[
            pltpu.VMEM(held, jnp.float32),
            pltpu.VMEM(held, jnp.bfloat16),
            pltpu.VMEM(held, jnp.bfloat16),
            pltpu.SemaphoreType.DMA((len(pieces),)),
            pltpu.SemaphoreType.DMA((2 * len(pieces),)),
        ],
        compiler_params=pltpu.CompilerParams(vmem_limit_bytes=VMEM_BYTES),
        cost_estimate=pl.CostEstimate(
            flops=10 * 4 * rows * BLOCK * cols, bytes_accessed=80 * rows * cols, transcendentals=0
        ),
    )(start_row, root_row, *pieces)


def product_kernel(calls, table, root_hbm, high_hbm, low_hbm, *rest):
    outs = rest[: len(calls)]
    a_f, z_h, z_l, a_sem, z_sem = rest[len(calls) :]
    rows = outs[0].shape[0]
    per_range = rows // BLOCK
    per_part = PART // BLOCK
    parts = rows // PART
    children = [table[call, 3 * per_range + 2] for call in calls]

    def factor_copies(i, source, target, first):
        return [
            pltpu.make_async_copy(
                source.at[table[children[i], 3 * per_range + side]],
                target.at[i, pl.ds(side * rows, rows)],
                z_sem.at[i, first + side],
            )
            for side in range(2)
        ]

    def start_root(i, part):
        for m in range(per_part):
            mb = pl.multiple_of(table[children[i], part * per_part + m] * BLOCK, BLOCK)
            pltpu.make_async_copy(
                root_hbm.at[:, pl.ds(mb, BLOCK)],
                a_f.at[i, part, :, pl.ds(m * BLOCK, BLOCK)],
                a_sem.at[i, part],
            ).start()

    highs_in = [factor_copies(i, high_hbm, z_h, 0) for i in range(len(calls))]
    lows_in = [factor_copies(i, low_hbm, z_l, 2) for i in range(len(calls))]

    def begin(i):
        start_root(i, 0)
        for copy in highs_in[i] + lows_in[i]:
            copy.start()
        start_root(i, 1)

    begin(0)
    for i, out in enumerate(outs):
        for part in range(parts):
            pltpu.make_async_copy(a_f.at[i, part], a_f.at[i, part], a_sem.at[i, part]).wait()
            if part == 0:
                for copy in highs_in[i]:
                    copy.wait()
            if part + 2 < parts:
                start_root(i, part + 2)
            elif part + 2 == parts and i + 1 < len(calls):
                begin(i + 1)
            highs, lows = [], []
            for k in range(2 * per_range):
                value = a_f[i, part, table[children[i], per_range + k]]
                high = value.astype(jnp.bfloat16)
                highs.append(high)
                lows.append((value - high.astype(jnp.float32)).astype(jnp.bfloat16))
            high = jnp.concatenate(highs, axis=1)
            low = jnp.concatenate(lows, axis=1)
            value = jnp.dot(high, z_h[i], preferred_element_type=jnp.float32)
            value = value + jnp.dot(low, z_h[i], preferred_element_type=jnp.float32)
            if part == 0:
                for copy in lows_in[i]:
                    copy.wait()
            value = value + jnp.dot(high, z_l[i], preferred_element_type=jnp.float32)
            out[part * PART : (part + 1) * PART, :] = value


def product(calls, table, root, high, low):
    rows, cols = high.shape[1:]
    n = len(calls)
    any_spec = pl.BlockSpec(memory_space=pl.ANY)
    root, high, low = [pltpu.with_memory_space_constraint(v, pltpu.HBM) for v in (root, high, low)]
    return pl.pallas_call(
        functools.partial(product_kernel, calls),
        out_shape=[jax.ShapeDtypeStruct((rows, cols), jnp.float32)] * n,
        in_specs=[pl.BlockSpec(memory_space=pltpu.SMEM)] + [any_spec] * 3,
        out_specs=[pl.BlockSpec(memory_space=pltpu.VMEM)] * n,
        scratch_shapes=[
            pltpu.VMEM((n, rows // PART, root.shape[0], PART, BLOCK), jnp.float32),
            pltpu.VMEM((n, 2 * rows, cols), jnp.bfloat16),
            pltpu.VMEM((n, 2 * rows, cols), jnp.bfloat16),
            pltpu.SemaphoreType.DMA((n, rows // PART)),
            pltpu.SemaphoreType.DMA((n, 4)),
        ],
        compiler_params=pltpu.CompilerParams(vmem_limit_bytes=(12 + 14 * n) * 1024 * 1024),
        cost_estimate=pl.CostEstimate(
            flops=n * 3 * 2 * rows * 2 * rows * cols,
            bytes_accessed=n * 12 * rows * rows,
            transcendentals=0,
        ),
    )(table, root, high, low)


def weigh_kernel(piece, first, second, high_hbm, low_hbm, total, sums, high, low, sem):
    rows, cols = total.shape
    copies = [
        pltpu.make_async_copy(high_hbm.at[piece], high, sem.at[0]),
        pltpu.make_async_copy(low_hbm.at[piece], low, sem.at[1]),
    ]
    for copy in copies:
        copy.start()
    for copy in copies:
        copy.wait()

    def one(i, found):
        at = pl.ds(pl.multiple_of(i * 64, 64), 64)
        value = first[at, :] + second[at, :]
        total[at, :] = value
        factor = high[at, :].astype(jnp.float32) + low[at, :].astype(jnp.float32)
        return found + jnp.sum((factor * value).reshape(8, 8, cols), axis=0)

    found = lax.fori_loop(0, rows // 64, one, jnp.zeros((8, cols), jnp.float32))
    sums[...] = jnp.sum(found, axis=0, keepdims=True)


def weigh(piece, first, second, high, low):
    rows, cols = first.shape
    any_spec = pl.BlockSpec(memory_space=pl.ANY)
    vmem = pl.BlockSpec(memory_space=pltpu.VMEM)
    high, low = [pltpu.with_memory_space_constraint(v, pltpu.HBM) for v in (high, low)]
    return pl.pallas_call(
        functools.partial(weigh_kernel, piece),
        out_shape=[
            jax.ShapeDtypeStruct((rows, cols), jnp.float32),
            jax.ShapeDtypeStruct((1, cols), jnp.float32),
        ],
        in_specs=[vmem, vmem, any_spec, any_spec],
        out_specs=[vmem, vmem],
        scratch_shapes=[
            pltpu.VMEM((rows, cols), jnp.bfloat16),
            pltpu.VMEM((rows, cols), jnp.bfloat16),
            pltpu.SemaphoreType.DMA((2,)),
        ],
        compiler_params=pltpu.CompilerParams(vmem_limit_bytes=VMEM_BYTES),
        cost_estimate=pl.CostEstimate(
            flops=4 * rows * cols, bytes_accessed=16 * rows * cols, transcendentals=0
        ),
    )(first, second, high, low)


def per_device(root_inverse, root_row, coupling, pivot_variance):
    zh = lax.axis_index("zh")
    y = lax.axis_index("y")
    x = lax.axis_index("x")
    core = lax.axis_index("core")
    rows, cols = coupling.shape[1:]
    ranges = root_row.shape[1] // rows
    per_range = rows // BLOCK
    own_range = 2 * x + core
    device = (y * 4 + x) * 2 + core

    root = lax.all_gather(root_inverse, ("zh", "zl"), axis=0, tiled=False)

    pairs, holds = spread_plan()
    halves, found = piece_plan(holds)
    spots = lax.dynamic_slice(halves, (device, 0), (1, 8))[0]
    child = zh * 4 + jnp.concatenate([spots & 3, jnp.stack([y, (y + 1 - 2 * core) & 3])])
    ranged = jnp.concatenate([y + 4 * (spots >> 2), jnp.stack([own_range, own_range])])
    start_row = (child * ranges + ranged) * per_range
    block = (root_row[:, ::BLOCK] >> 7).reshape(-1, ranges, per_range)

    def blocks_of(r):
        return lax.dynamic_slice(block, (zh * 4, r, 0), (4, 1, per_range))[:, 0] & 7

    order = (y + jnp.stack([2, 3 - 2 * core, 1 + 2 * core, 0])) & 3
    table = jnp.concatenate(
        [
            blocks_of(own_range),
            blocks_of(y),
            blocks_of(y + 4) + 8,
            lax.dynamic_slice(found, (device, 0, 0), (1, 4, 2))[0],
            order[:, None],
        ],
        axis=1,
    ).astype(jnp.int32)
    own = lax.ppermute(coupling[0], ("y", "x", "core"), pairs)
    rows_of = root_row.reshape(-1, BLOCK)
    own, table, start_row, rows_of = lax.optimization_barrier((own, table, start_row, rows_of))
    along_x = opposite(4)
    beside = lax.ppermute(own, "core", CORES)
    near = lax.ppermute(own, ("x", "core"), along_x)
    near_beside = lax.ppermute(beside, ("x", "core"), along_x)
    far = lax.ppermute(near, ("x", "core"), along_x)
    pieces = [own, beside, near, near_beside, far]
    pieces += [lax.ppermute(p, "core", CORES) for p in (near, near_beside, far)]
    pieces += [coupling[0], lax.ppermute(coupling[0], ("y", "core"), opposite(4, -1))]
    high, low = spread(start_row, rows_of, pieces)

    root = root.reshape(-1, *root_inverse.shape)
    (far,) = product((0,), table, root, high, low)
    passed = lax.ppermute(far, ("y", "core"), opposite(4))
    (first,) = product((1,), table, root, high, low)
    back = lax.ppermute(first, ("y", "core"), opposite(4, -1))
    second, home = product((2, 3), table, root, high, low)
    last, last_sums = weigh(9, second, passed, high, low)
    last_sums = lax.ppermute(last_sums, ("y", "core"), opposite(4))
    last, last_sums = lax.optimization_barrier((last, last_sums))
    forth = lax.ppermute(last, ("y", "core"), opposite(4))
    kept, sums = weigh(8, home, back, high, low)
    sums = lax.all_to_all(
        jnp.broadcast_to(sums + last_sums, (8, cols)),
        ("x", "core"),
        split_axis=0,
        concat_axis=0,
        tiled=True,
    )
    marginal = pivot_variance + jnp.sum(sums, axis=0, keepdims=True)
    kept, marginal = lax.optimization_barrier((kept, marginal))
    summed = kept + forth

    own_place = lax.dynamic_slice(root_row, (zh * 4 + y, own_range * rows), (1, rows))[0]
    own_place = jnp.where(own_place >= 0, own_place & (BLOCK - 1), -1).reshape(per_range, BLOCK)
    hot = (own_place[:, :, None] == jnp.arange(BLOCK, dtype=jnp.int32)).astype(jnp.float32)
    result = -jnp.einsum(
        "iuo,ion->iun", hot, summed.reshape(per_range, BLOCK, cols), precision=lax.Precision.HIGHEST
    )

    return result.reshape(1, rows, cols), marginal


def solution(mesh):
    split = Mesh(mesh.devices.reshape(2, 4, 4, 2, 8), ("zh", "y", "x", "core", "zl"))
    leaf, row, col = ("zh", "y"), ("x", "core"), "zl"
    return jax.shard_map(
        per_device,
        mesh=split,
        in_specs=(P(row, ("zh", "y", "zl")), P(), P(leaf, row, col), P(leaf, col)),
        out_specs=(P(leaf, row, col), P(leaf, col)),
        check_vma=False,
    )
```

```python
import functools

import jax
import jax.numpy as jnp
from jax import lax
from jax.experimental import pallas as pl
from jax.experimental.pallas import tpu as pltpu
from jax.sharding import Mesh, PartitionSpec as P

BLOCK = 128
PART = 256
SLOTS = 4
VMEM_BYTES = 24 * 1024 * 1024
CORES = [(0, 1), (1, 0)]
SPREAD_X = (
    (3, 1, 0, 0),
    (0, 3, 0, 1),
    (1, 2, 0, 1),
    (2, 0, 1, 1),
    (2, 2, 1, 3),
    (3, 1, 2, 2),
    (3, 0, 2, 3),
    (3, 2, 3, 0),
)


def shift(size, step):
    return [(i, (i + step) % size) for i in range(size)]


def opposite(size, way=1):
    return [
        (2 * i + c, (i + way * (1 - 2 * c)) % size * 2 + c) for i in range(size) for c in range(2)
    ]


def spread_plan():
    pairs, holds, taken = [], {}, {}
    for y in range(4):
        for r in range(8):
            to = (SPREAD_X[r][y], r % 4)
            core = taken.get(to, 0)
            taken[to] = core + 1
            pairs.append(((y * 4 + r // 2) * 2 + r % 2, (to[1] * 4 + to[0]) * 2 + core))
            holds[(to[1], to[0], core)] = (r // 4, y)
    return pairs, holds


def piece_plan(holds):
    halves, found = [], []
    for y in range(4):
        for x in range(4):
            for c in range(2):
                d = 2 * c - 1
                at = [
                    (x, c),
                    (x, 1 - c),
                    (x + d, c),
                    (x + d, 1 - c),
                    (x + 2, c),
                    (x - d, 1 - c),
                    (x - d, c),
                    (x + 2, 1 - c),
                ]
                has = [holds[(y, px % 4, pc)] for px, pc in at]
                halves.append([h * 4 + k for h, k in has])
                found.append([[has.index((0, k)), has.index((1, k))] for k in range(4)])
    return [jnp.array(v, jnp.int32) for v in (halves, found)]


def spread_kernel(start_row, rows_ref, *rest):
    pieces = rest[:-7]
    high_hbm, low_hbm, z_f, z_h, z_l, in_sem, out_sem = rest[-7:]
    slots, rows = z_f.shape[:2]

    def fetch(i):
        return pltpu.make_async_copy(pieces[i], z_f.at[i % slots], in_sem.at[i])

    def store(i):
        return [
            pltpu.make_async_copy(z_h.at[i % slots], high_hbm.at[i], out_sem.at[2 * i]),
            pltpu.make_async_copy(z_l.at[i % slots], low_hbm.at[i], out_sem.at[2 * i + 1]),
        ]

    for i in range(slots):
        fetch(i).start()
    row = lax.broadcasted_iota(jnp.int32, (BLOCK, BLOCK), 0)
    for at in range(len(pieces)):
        fetch(at).wait()
        if at >= slots:
            for copy in store(at - slots):
                copy.wait()

        def one(i, carry, at=at):
            here = pl.ds(pl.multiple_of(i * BLOCK, BLOCK), BLOCK)
            value = z_f[at % slots, here, :]
            high = value.astype(jnp.bfloat16)
            low = (value - high.astype(jnp.float32)).astype(jnp.bfloat16)
            place = rows_ref[pl.ds(start_row[at] + i, 1), :]
            place = jnp.where(place >= 0, place & (BLOCK - 1), -1)
            hot = (place == row).astype(jnp.float32).astype(jnp.bfloat16)
            z_h[at % slots, here, :] = jnp.dot(
                hot, high, preferred_element_type=jnp.float32
            ).astype(jnp.bfloat16)
            z_l[at % slots, here, :] = jnp.dot(
                hot, low, preferred_element_type=jnp.float32
            ).astype(jnp.bfloat16)
            return carry

        lax.fori_loop(0, rows // BLOCK, one, 0, unroll=3)
        for copy in store(at):
            copy.start()
        if at + slots < len(pieces):
            fetch(at + slots).start()
    for at in range(len(pieces) - slots, len(pieces)):
        for copy in store(at):
            copy.wait()


def spread(start_row, root_row, pieces):
    rows, cols = pieces[0].shape
    any_spec = pl.BlockSpec(memory_space=pl.ANY)
    shape = (len(pieces), rows, cols)
    held = (SLOTS, rows, cols)
    return pl.pallas_call(
        spread_kernel,
        out_shape=[pltpu.HBM(shape, jnp.bfloat16)] * 2,
        in_specs=[
            pl.BlockSpec(memory_space=pltpu.SMEM),
            pl.BlockSpec(memory_space=pltpu.VMEM),
        ]
        + [any_spec] * len(pieces),
        out_specs=[pl.BlockSpec(memory_space=pltpu.HBM)] * 2,
        scratch_shapes=[
            pltpu.VMEM(held, jnp.float32),
            pltpu.VMEM(held, jnp.bfloat16),
            pltpu.VMEM(held, jnp.bfloat16),
            pltpu.SemaphoreType.DMA((len(pieces),)),
            pltpu.SemaphoreType.DMA((2 * len(pieces),)),
        ],
        compiler_params=pltpu.CompilerParams(vmem_limit_bytes=VMEM_BYTES),
        cost_estimate=pl.CostEstimate(
            flops=10 * 4 * rows * BLOCK * cols, bytes_accessed=80 * rows * cols, transcendentals=0
        ),
    )(start_row, root_row, *pieces)


def product_kernel(calls, table, root_hbm, high_hbm, low_hbm, *rest):
    outs = rest[: len(calls)]
    a_f, z_h, z_l, a_sem, z_sem = rest[len(calls) :]
    rows = outs[0].shape[0]
    per_range = rows // BLOCK
    per_part = PART // BLOCK
    parts = rows // PART
    children = [table[call, 3 * per_range + 2] for call in calls]

    def factor_copies(i, source, target, first):
        return [
            pltpu.make_async_copy(
                source.at[table[children[i], 3 * per_range + side]],
                target.at[i, pl.ds(side * rows, rows)],
                z_sem.at[i, first + side],
            )
            for side in range(2)
        ]

    def start_root(i, part):
        for m in range(per_part):
            mb = pl.multiple_of(table[children[i], part * per_part + m] * BLOCK, BLOCK)
            pltpu.make_async_copy(
                root_hbm.at[:, pl.ds(mb, BLOCK)],
                a_f.at[i, part, :, pl.ds(m * BLOCK, BLOCK)],
                a_sem.at[i, part],
            ).start()

    highs_in = [factor_copies(i, high_hbm, z_h, 0) for i in range(len(calls))]
    lows_in = [factor_copies(i, low_hbm, z_l, 2) for i in range(len(calls))]

    def begin(i):
        start_root(i, 0)
        for copy in highs_in[i] + lows_in[i]:
            copy.start()
        start_root(i, 1)

    begin(0)
    for i, out in enumerate(outs):
        for part in range(parts):
            pltpu.make_async_copy(a_f.at[i, part], a_f.at[i, part], a_sem.at[i, part]).wait()
            if part == 0:
                for copy in highs_in[i]:
                    copy.wait()
            if part + 2 < parts:
                start_root(i, part + 2)
            elif part + 2 == parts and i + 1 < len(calls):
                begin(i + 1)
            highs, lows = [], []
            for k in range(2 * per_range):
                value = a_f[i, part, table[children[i], per_range + k]]
                high = value.astype(jnp.bfloat16)
                highs.append(high)
                lows.append((value - high.astype(jnp.float32)).astype(jnp.bfloat16))
            high = jnp.concatenate(highs, axis=1)
            low = jnp.concatenate(lows, axis=1)
            value = jnp.dot(high, z_h[i], preferred_element_type=jnp.float32)
            value = value + jnp.dot(low, z_h[i], preferred_element_type=jnp.float32)
            if part == 0:
                for copy in lows_in[i]:
                    copy.wait()
            value = value + jnp.dot(high, z_l[i], preferred_element_type=jnp.float32)
            out[part * PART : (part + 1) * PART, :] = value


def product(calls, table, root, high, low):
    rows, cols = high.shape[1:]
    n = len(calls)
    any_spec = pl.BlockSpec(memory_space=pl.ANY)
    root, high, low = [pltpu.with_memory_space_constraint(v, pltpu.HBM) for v in (root, high, low)]
    return pl.pallas_call(
        functools.partial(product_kernel, calls),
        out_shape=[jax.ShapeDtypeStruct((rows, cols), jnp.float32)] * n,
        in_specs=[pl.BlockSpec(memory_space=pltpu.SMEM)] + [any_spec] * 3,
        out_specs=[pl.BlockSpec(memory_space=pltpu.VMEM)] * n,
        scratch_shapes=[
            pltpu.VMEM((n, rows // PART, root.shape[0], PART, BLOCK), jnp.float32),
            pltpu.VMEM((n, 2 * rows, cols), jnp.bfloat16),
            pltpu.VMEM((n, 2 * rows, cols), jnp.bfloat16),
            pltpu.SemaphoreType.DMA((n, rows // PART)),
            pltpu.SemaphoreType.DMA((n, 4)),
        ],
        compiler_params=pltpu.CompilerParams(vmem_limit_bytes=(12 + 14 * n) * 1024 * 1024),
        cost_estimate=pl.CostEstimate(
            flops=n * 3 * 2 * rows * 2 * rows * cols,
            bytes_accessed=n * 12 * rows * rows,
            transcendentals=0,
        ),
    )(table, root, high, low)


def weigh_kernel(piece, first, second, high_hbm, low_hbm, total, sums, high, low, sem):
    rows, cols = total.shape
    copies = [
        pltpu.make_async_copy(high_hbm.at[piece], high, sem.at[0]),
        pltpu.make_async_copy(low_hbm.at[piece], low, sem.at[1]),
    ]
    for copy in copies:
        copy.start()
    for copy in copies:
        copy.wait()

    def one(i, found):
        at = pl.ds(pl.multiple_of(i * 64, 64), 64)
        value = first[at, :] + second[at, :]
        total[at, :] = value
        factor = high[at, :].astype(jnp.float32) + low[at, :].astype(jnp.float32)
        return found + jnp.sum((factor * value).reshape(8, 8, cols), axis=0)

    found = lax.fori_loop(0, rows // 64, one, jnp.zeros((8, cols), jnp.float32))
    sums[...] = jnp.sum(found, axis=0, keepdims=True)


def weigh(piece, first, second, high, low):
    rows, cols = first.shape
    any_spec = pl.BlockSpec(memory_space=pl.ANY)
    vmem = pl.BlockSpec(memory_space=pltpu.VMEM)
    high, low = [pltpu.with_memory_space_constraint(v, pltpu.HBM) for v in (high, low)]
    return pl.pallas_call(
        functools.partial(weigh_kernel, piece),
        out_shape=[
            jax.ShapeDtypeStruct((rows, cols), jnp.float32),
            jax.ShapeDtypeStruct((1, cols), jnp.float32),
        ],
        in_specs=[vmem, vmem, any_spec, any_spec],
        out_specs=[vmem, vmem],
        scratch_shapes=[
            pltpu.VMEM((rows, cols), jnp.bfloat16),
            pltpu.VMEM((rows, cols), jnp.bfloat16),
            pltpu.SemaphoreType.DMA((2,)),
        ],
        compiler_params=pltpu.CompilerParams(vmem_limit_bytes=VMEM_BYTES),
        cost_estimate=pl.CostEstimate(
            flops=4 * rows * cols, bytes_accessed=16 * rows * cols, transcendentals=0
        ),
    )(first, second, high, low)


def per_device(root_inverse, root_row, coupling, pivot_variance):
    zh = lax.axis_index("zh")
    y = lax.axis_index("y")
    x = lax.axis_index("x")
    core = lax.axis_index("core")
    rows, cols = coupling.shape[1:]
    ranges = root_row.shape[1] // rows
    per_range = rows // BLOCK
    own_range = 2 * x + core
    device = (y * 4 + x) * 2 + core

    root = lax.all_gather(root_inverse, ("zh", "zl"), axis=0, tiled=False)

    pairs, holds = spread_plan()
    halves, found = piece_plan(holds)
    spots = lax.dynamic_slice(halves, (device, 0), (1, 8))[0]
    child = zh * 4 + jnp.concatenate([spots & 3, jnp.stack([y, (y + 1 - 2 * core) & 3])])
    ranged = jnp.concatenate([y + 4 * (spots >> 2), jnp.stack([own_range, own_range])])
    start_row = (child * ranges + ranged) * per_range
    block = (root_row[:, ::BLOCK] >> 7).reshape(-1, ranges, per_range)

    def blocks_of(r):
        return lax.dynamic_slice(block, (zh * 4, r, 0), (4, 1, per_range))[:, 0] & 7

    order = (y + jnp.stack([2, 3 - 2 * core, 1 + 2 * core, 0])) & 3
    table = jnp.concatenate(
        [
            blocks_of(own_range),
            blocks_of(y),
            blocks_of(y + 4) + 8,
            lax.dynamic_slice(found, (device, 0, 0), (1, 4, 2))[0],
            order[:, None],
        ],
        axis=1,
    ).astype(jnp.int32)
    own = lax.ppermute(coupling[0], ("y", "x", "core"), pairs)
    rows_of = root_row.reshape(-1, BLOCK)
    own, table, start_row, rows_of = lax.optimization_barrier((own, table, start_row, rows_of))
    along_x = opposite(4)
    beside = lax.ppermute(own, "core", CORES)
    near = lax.ppermute(own, ("x", "core"), along_x)
    near_beside = lax.ppermute(beside, ("x", "core"), along_x)
    far = lax.ppermute(near, ("x", "core"), along_x)
    pieces = [own, beside, near, near_beside, far]
    pieces += [lax.ppermute(p, "core", CORES) for p in (near, near_beside, far)]
    pieces += [coupling[0], lax.ppermute(coupling[0], ("y", "core"), opposite(4, -1))]
    high, low = spread(start_row, rows_of, pieces)

    root = root.reshape(-1, *root_inverse.shape)
    far, first = product((0, 1), table, root, high, low)
    passed = lax.ppermute(far, ("y", "core"), opposite(4))
    second, home = product((2, 3), table, root, high, low)
    first, second = lax.optimization_barrier((first, second))
    back = lax.ppermute(first, ("y", "core"), opposite(4, -1))
    last, last_sums = weigh(9, second, passed, high, low)
    last_sums = lax.ppermute(last_sums, ("y", "core"), opposite(4))
    last, last_sums = lax.optimization_barrier((last, last_sums))
    forth = lax.ppermute(last, ("y", "core"), opposite(4))
    kept, sums = weigh(8, home, back, high, low)
    sums = lax.all_to_all(
        jnp.broadcast_to(sums + last_sums, (8, cols)),
        ("x", "core"),
        split_axis=0,
        concat_axis=0,
        tiled=True,
    )
    marginal = pivot_variance + jnp.sum(sums, axis=0, keepdims=True)
    kept, marginal = lax.optimization_barrier((kept, marginal))
    summed = kept + forth

    own_place = lax.dynamic_slice(root_row, (zh * 4 + y, own_range * rows), (1, rows))[0]
    own_place = jnp.where(own_place >= 0, own_place & (BLOCK - 1), -1).reshape(per_range, BLOCK)
    hot = (own_place[:, :, None] == jnp.arange(BLOCK, dtype=jnp.int32)).astype(jnp.float32)
    result = -jnp.einsum(
        "iuo,ion->iun", hot, summed.reshape(per_range, BLOCK, cols), precision=lax.Precision.HIGHEST
    )

    return result.reshape(1, rows, cols), marginal


def solution(mesh):
    split = Mesh(mesh.devices.reshape(2, 4, 4, 2, 8), ("zh", "y", "x", "core", "zl"))
    leaf, row, col = ("zh", "y"), ("x", "core"), "zl"
    return jax.shard_map(
        per_device,
        mesh=split,
        in_specs=(P(row, ("zh", "y", "zl")), P(), P(leaf, row, col), P(leaf, col)),
        out_specs=(P(leaf, row, col), P(leaf, col)),
        check_vma=False,
    )
```

```python
import functools

import jax
import jax.numpy as jnp
from jax import lax
from jax.experimental import pallas as pl
from jax.experimental.pallas import tpu as pltpu
from jax.sharding import Mesh, PartitionSpec as P

BLOCK = 128
PART = 256
SLOTS = 4
VMEM_BYTES = 24 * 1024 * 1024
CORES = [(0, 1), (1, 0)]
SPREAD_X = (
    (3, 1, 0, 0),
    (0, 3, 0, 1),
    (1, 2, 0, 1),
    (2, 0, 1, 1),
    (2, 2, 1, 3),
    (3, 1, 2, 2),
    (3, 0, 2, 3),
    (3, 2, 3, 0),
)


def shift(size, step):
    return [(i, (i + step) % size) for i in range(size)]


def opposite(size, way=1):
    return [
        (2 * i + c, (i + way * (1 - 2 * c)) % size * 2 + c) for i in range(size) for c in range(2)
    ]


def spread_plan():
    pairs, holds, taken = [], {}, {}
    for y in range(4):
        for r in range(8):
            to = (SPREAD_X[r][y], r % 4)
            core = taken.get(to, 0)
            taken[to] = core + 1
            pairs.append(((y * 4 + r // 2) * 2 + r % 2, (to[1] * 4 + to[0]) * 2 + core))
            holds[(to[1], to[0], core)] = (r // 4, y)
    return pairs, holds


def piece_plan(holds):
    halves, found = [], []
    for y in range(4):
        for x in range(4):
            for c in range(2):
                d = 2 * c - 1
                at = [
                    (x, c),
                    (x, 1 - c),
                    (x + d, c),
                    (x + d, 1 - c),
                    (x + 2, c),
                    (x - d, 1 - c),
                    (x - d, c),
                    (x + 2, 1 - c),
                ]
                has = [holds[(y, px % 4, pc)] for px, pc in at]
                halves.append([h * 4 + k for h, k in has])
                found.append([[has.index((0, k)), has.index((1, k))] for k in range(4)])
    return [jnp.array(v, jnp.int32) for v in (halves, found)]


def spread_kernel(start_row, rows_ref, *rest):
    pieces = rest[:-7]
    high_hbm, low_hbm, z_f, z_h, z_l, in_sem, out_sem = rest[-7:]
    slots, rows = z_f.shape[:2]

    def fetch(i):
        return pltpu.make_async_copy(pieces[i], z_f.at[i % slots], in_sem.at[i])

    def store(i):
        return [
            pltpu.make_async_copy(z_h.at[i % slots], high_hbm.at[i], out_sem.at[2 * i]),
            pltpu.make_async_copy(z_l.at[i % slots], low_hbm.at[i], out_sem.at[2 * i + 1]),
        ]

    for i in range(slots):
        fetch(i).start()
    row = lax.broadcasted_iota(jnp.int32, (BLOCK, BLOCK), 0)
    for at in range(len(pieces)):
        fetch(at).wait()
        if at >= slots:
            for copy in store(at - slots):
                copy.wait()

        def one(i, carry, at=at):
            here = pl.ds(pl.multiple_of(i * BLOCK, BLOCK), BLOCK)
            value = z_f[at % slots, here, :]
            high = value.astype(jnp.bfloat16)
            low = (value - high.astype(jnp.float32)).astype(jnp.bfloat16)
            place = rows_ref[pl.ds(start_row[at] + i, 1), :]
            place = jnp.where(place >= 0, place & (BLOCK - 1), -1)
            hot = (place == row).astype(jnp.float32).astype(jnp.bfloat16)
            z_h[at % slots, here, :] = jnp.dot(
                hot, high, preferred_element_type=jnp.float32
            ).astype(jnp.bfloat16)
            z_l[at % slots, here, :] = jnp.dot(
                hot, low, preferred_element_type=jnp.float32
            ).astype(jnp.bfloat16)
            return carry

        lax.fori_loop(0, rows // BLOCK, one, 0, unroll=3)
        for copy in store(at):
            copy.start()
        if at + slots < len(pieces):
            fetch(at + slots).start()
    for at in range(len(pieces) - slots, len(pieces)):
        for copy in store(at):
            copy.wait()


def spread(start_row, root_row, pieces):
    rows, cols = pieces[0].shape
    any_spec = pl.BlockSpec(memory_space=pl.ANY)
    shape = (len(pieces), rows, cols)
    held = (SLOTS, rows, cols)
    return pl.pallas_call(
        spread_kernel,
        out_shape=[pltpu.HBM(shape, jnp.bfloat16)] * 2,
        in_specs=[
            pl.BlockSpec(memory_space=pltpu.SMEM),
            pl.BlockSpec(memory_space=pltpu.VMEM),
        ]
        + [any_spec] * len(pieces),
        out_specs=[pl.BlockSpec(memory_space=pltpu.HBM)] * 2,
        scratch_shapes=[
            pltpu.VMEM(held, jnp.float32),
            pltpu.VMEM(held, jnp.bfloat16),
            pltpu.VMEM(held, jnp.bfloat16),
            pltpu.SemaphoreType.DMA((len(pieces),)),
            pltpu.SemaphoreType.DMA((2 * len(pieces),)),
        ],
        compiler_params=pltpu.CompilerParams(vmem_limit_bytes=VMEM_BYTES),
        cost_estimate=pl.CostEstimate(
            flops=10 * 4 * rows * BLOCK * cols, bytes_accessed=80 * rows * cols, transcendentals=0
        ),
    )(start_row, root_row, *pieces)


def product_kernel(calls, ahead, given, table, root_hbm, high_hbm, low_hbm, *rest):
    fetched = len(calls) - given
    slots, rest = ([rest[:3]], rest[3:]) if given else ([], rest)
    outs, rest = rest[: len(calls)], rest[len(calls) :]
    if ahead is not None:
        next_slot, rest = rest[:3], rest[3:]
    if fetched:
        slots = slots + [[ref.at[i] for ref in rest[:3]] for i in range(fetched)]
        rest = rest[3:]
    a_sem, z_sem = rest
    rows = outs[0].shape[0]
    per_range = rows // BLOCK
    per_part = PART // BLOCK
    parts = rows // PART
    wanted = list(calls)
    if ahead is not None:
        slots = slots + [next_slot]
        wanted.append(ahead)
    children = [table[call, 3 * per_range + 2] for call in wanted]

    def factor_copies(i, source, which):
        return [
            pltpu.make_async_copy(
                source.at[table[children[i], 3 * per_range + side]],
                slots[i][which].at[pl.ds(side * rows, rows)],
                z_sem.at[i, 2 * (which - 1) + side],
            )
            for side in range(2)
        ]

    def start_root(i, part):
        for m in range(per_part):
            mb = pl.multiple_of(table[children[i], part * per_part + m] * BLOCK, BLOCK)
            pltpu.make_async_copy(
                root_hbm.at[:, pl.ds(mb, BLOCK)],
                slots[i][0].at[part, :, pl.ds(m * BLOCK, BLOCK)],
                a_sem.at[i, part],
            ).start()

    def wait_root(i, part):
        whole = slots[i][0].at[part]
        pltpu.make_async_copy(whole, whole, a_sem.at[i, part]).wait()

    def begin(i):
        start_root(i, 0)
        for copy in factor_copies(i, high_hbm, 1) + factor_copies(i, low_hbm, 2):
            copy.start()
        for part in range(1, parts):
            start_root(i, part)

    begin(0 if not given else 1)
    for i, out in enumerate(outs):
        here = i >= given
        for part in range(parts):
            if here:
                wait_root(i, part)
            if here and part == 0:
                for copy in factor_copies(i, high_hbm, 1):
                    copy.wait()
            if part == 1 and (i + 1 if here else i + 2) < len(wanted):
                begin(i + 1 if here else i + 2)
            highs, lows = [], []
            for k in range(2 * per_range):
                value = slots[i][0][part, table[children[i], per_range + k]]
                high = value.astype(jnp.bfloat16)
                highs.append(high)
                lows.append((value - high.astype(jnp.float32)).astype(jnp.bfloat16))
            high = jnp.concatenate(highs, axis=1)
            low = jnp.concatenate(lows, axis=1)
            value = jnp.dot(high, slots[i][1][...], preferred_element_type=jnp.float32)
            value = value + jnp.dot(low, slots[i][1][...], preferred_element_type=jnp.float32)
            if here and part == 0:
                for copy in factor_copies(i, low_hbm, 2):
                    copy.wait()
            value = value + jnp.dot(high, slots[i][2][...], preferred_element_type=jnp.float32)
            out[part * PART : (part + 1) * PART, :] = value
    if ahead is not None:
        i = len(wanted) - 1
        for part in range(parts):
            wait_root(i, part)
        for copy in factor_copies(i, high_hbm, 1) + factor_copies(i, low_hbm, 2):
            copy.wait()


def product(calls, ahead, given, table, root, high, low):
    rows, cols = high.shape[1:]
    n = len(calls)
    total = n + (ahead is not None)
    fetched = n - (given is not None)
    any_spec = pl.BlockSpec(memory_space=pl.ANY)
    vmem = pl.BlockSpec(memory_space=pltpu.VMEM)
    slot = [
        ((rows // PART, root.shape[0], PART, BLOCK), jnp.float32),
        ((2 * rows, cols), jnp.bfloat16),
        ((2 * rows, cols), jnp.bfloat16),
    ]
    args = [pltpu.with_memory_space_constraint(v, pltpu.HBM) for v in (root, high, low)]
    if given is not None:
        args += [pltpu.with_memory_space_constraint(v, pltpu.VMEM) for v in given]
    out_shape = [jax.ShapeDtypeStruct((rows, cols), jnp.float32)] * n
    if ahead is not None:
        out_shape += [pltpu.VMEM(shape, dtype) for shape, dtype in slot]
    scratch = [pltpu.VMEM((fetched, *shape), dtype) for shape, dtype in slot if fetched]
    found = pl.pallas_call(
        functools.partial(product_kernel, calls, ahead, int(given is not None)),
        out_shape=out_shape,
        in_specs=[pl.BlockSpec(memory_space=pltpu.SMEM)]
        + [any_spec] * 3
        + [vmem] * (len(args) - 3),
        out_specs=[vmem] * len(out_shape),
        scratch_shapes=scratch
        + [
            pltpu.SemaphoreType.DMA((total, rows // PART)),
            pltpu.SemaphoreType.DMA((total, 4)),
        ],
        compiler_params=pltpu.CompilerParams(vmem_limit_bytes=28 * 1024 * 1024),
        cost_estimate=pl.CostEstimate(
            flops=n * 3 * 2 * rows * 2 * rows * cols,
            bytes_accessed=n * 12 * rows * rows,
            transcendentals=0,
        ),
    )(table, *args)
    return found[:n], found[n:]


def weigh_kernel(piece, first, second, high_hbm, low_hbm, total, sums, high, low, sem):
    rows, cols = total.shape
    copies = [
        pltpu.make_async_copy(high_hbm.at[piece], high, sem.at[0]),
        pltpu.make_async_copy(low_hbm.at[piece], low, sem.at[1]),
    ]
    for copy in copies:
        copy.start()
    for copy in copies:
        copy.wait()

    def one(i, found):
        at = pl.ds(pl.multiple_of(i * 64, 64), 64)
        value = first[at, :] + second[at, :]
        total[at, :] = value
        factor = high[at, :].astype(jnp.float32) + low[at, :].astype(jnp.float32)
        return found + jnp.sum((factor * value).reshape(8, 8, cols), axis=0)

    found = lax.fori_loop(0, rows // 64, one, jnp.zeros((8, cols), jnp.float32))
    sums[...] = jnp.sum(found, axis=0, keepdims=True)


def weigh(piece, first, second, high, low):
    rows, cols = first.shape
    any_spec = pl.BlockSpec(memory_space=pl.ANY)
    vmem = pl.BlockSpec(memory_space=pltpu.VMEM)
    high, low = [pltpu.with_memory_space_constraint(v, pltpu.HBM) for v in (high, low)]
    return pl.pallas_call(
        functools.partial(weigh_kernel, piece),
        out_shape=[
            jax.ShapeDtypeStruct((rows, cols), jnp.float32),
            jax.ShapeDtypeStruct((1, cols), jnp.float32),
        ],
        in_specs=[vmem, vmem, any_spec, any_spec],
        out_specs=[vmem, vmem],
        scratch_shapes=[
            pltpu.VMEM((rows, cols), jnp.bfloat16),
            pltpu.VMEM((rows, cols), jnp.bfloat16),
            pltpu.SemaphoreType.DMA((2,)),
        ],
        compiler_params=pltpu.CompilerParams(vmem_limit_bytes=VMEM_BYTES),
        cost_estimate=pl.CostEstimate(
            flops=4 * rows * cols, bytes_accessed=16 * rows * cols, transcendentals=0
        ),
    )(first, second, high, low)


def per_device(root_inverse, root_row, coupling, pivot_variance):
    zh = lax.axis_index("zh")
    y = lax.axis_index("y")
    x = lax.axis_index("x")
    core = lax.axis_index("core")
    rows, cols = coupling.shape[1:]
    ranges = root_row.shape[1] // rows
    per_range = rows // BLOCK
    own_range = 2 * x + core
    device = (y * 4 + x) * 2 + core

    root = lax.all_gather(root_inverse, ("zh", "zl"), axis=0, tiled=False)

    pairs, holds = spread_plan()
    halves, found = piece_plan(holds)
    spots = lax.dynamic_slice(halves, (device, 0), (1, 8))[0]
    child = zh * 4 + jnp.concatenate([spots & 3, jnp.stack([y, (y + 1 - 2 * core) & 3])])
    ranged = jnp.concatenate([y + 4 * (spots >> 2), jnp.stack([own_range, own_range])])
    start_row = (child * ranges + ranged) * per_range
    block = (root_row[:, ::BLOCK] >> 7).reshape(-1, ranges, per_range)

    def blocks_of(r):
        return lax.dynamic_slice(block, (zh * 4, r, 0), (4, 1, per_range))[:, 0] & 7

    order = (y + jnp.stack([2, 3 - 2 * core, 1 + 2 * core, 0])) & 3
    table = jnp.concatenate(
        [
            blocks_of(own_range),
            blocks_of(y),
            blocks_of(y + 4) + 8,
            lax.dynamic_slice(found, (device, 0, 0), (1, 4, 2))[0],
            order[:, None],
        ],
        axis=1,
    ).astype(jnp.int32)
    own = lax.ppermute(coupling[0], ("y", "x", "core"), pairs)
    rows_of = root_row.reshape(-1, BLOCK)
    own, table, start_row, rows_of = lax.optimization_barrier((own, table, start_row, rows_of))
    along_x = opposite(4)
    beside = lax.ppermute(own, "core", CORES)
    near = lax.ppermute(own, ("x", "core"), along_x)
    near_beside = lax.ppermute(beside, ("x", "core"), along_x)
    far = lax.ppermute(near, ("x", "core"), along_x)
    pieces = [own, beside, near, near_beside, far]
    pieces += [lax.ppermute(p, "core", CORES) for p in (near, near_beside, far)]
    pieces += [coupling[0], lax.ppermute(coupling[0], ("y", "core"), opposite(4, -1))]
    high, low = spread(start_row, rows_of, pieces)

    root = root.reshape(-1, *root_inverse.shape)
    (far,), given = product((0,), 1, None, table, root, high, low)
    passed = lax.ppermute(far, ("y", "core"), opposite(4))
    (first,), given = product((1,), 2, given, table, root, high, low)
    back = lax.ppermute(first, ("y", "core"), opposite(4, -1))
    (second, home), _ = product((2, 3), None, given, table, root, high, low)
    last, last_sums = weigh(9, second, passed, high, low)
    last_sums = lax.ppermute(last_sums, ("y", "core"), opposite(4))
    last, last_sums = lax.optimization_barrier((last, last_sums))
    forth = lax.ppermute(last, ("y", "core"), opposite(4))
    kept, sums = weigh(8, home, back, high, low)
    sums = lax.all_to_all(
        jnp.broadcast_to(sums + last_sums, (8, cols)),
        ("x", "core"),
        split_axis=0,
        concat_axis=0,
        tiled=True,
    )
    marginal = pivot_variance + jnp.sum(sums, axis=0, keepdims=True)
    kept, marginal = lax.optimization_barrier((kept, marginal))
    summed = kept + forth

    own_place = lax.dynamic_slice(root_row, (zh * 4 + y, own_range * rows), (1, rows))[0]
    own_place = jnp.where(own_place >= 0, own_place & (BLOCK - 1), -1).reshape(per_range, BLOCK)
    hot = (own_place[:, :, None] == jnp.arange(BLOCK, dtype=jnp.int32)).astype(jnp.float32)
    result = -jnp.einsum(
        "iuo,ion->iun", hot, summed.reshape(per_range, BLOCK, cols), precision=lax.Precision.HIGHEST
    )

    return result.reshape(1, rows, cols), marginal


def solution(mesh):
    split = Mesh(mesh.devices.reshape(2, 4, 4, 2, 8), ("zh", "y", "x", "core", "zl"))
    leaf, row, col = ("zh", "y"), ("x", "core"), "zl"
    return jax.shard_map(
        per_device,
        mesh=split,
        in_specs=(P(row, ("zh", "y", "zl")), P(), P(leaf, row, col), P(leaf, col)),
        out_specs=(P(leaf, row, col), P(leaf, col)),
        check_vma=False,
    )
```

```python
import functools

import jax
import jax.numpy as jnp
from jax import lax
from jax.experimental import pallas as pl
from jax.experimental.pallas import tpu as pltpu
from jax.sharding import Mesh, PartitionSpec as P

BLOCK = 128
PART = 256
SLOTS = 4
VMEM_BYTES = 24 * 1024 * 1024
CORES = [(0, 1), (1, 0)]
SPREAD_X = (
    (3, 1, 0, 0),
    (0, 3, 0, 1),
    (1, 2, 0, 1),
    (2, 0, 1, 1),
    (2, 2, 1, 3),
    (3, 1, 2, 2),
    (3, 0, 2, 3),
    (3, 2, 3, 0),
)


def shift(size, step):
    return [(i, (i + step) % size) for i in range(size)]


def opposite(size, way=1):
    return [
        (2 * i + c, (i + way * (1 - 2 * c)) % size * 2 + c) for i in range(size) for c in range(2)
    ]


def spread_plan():
    pairs, holds, taken = [], {}, {}
    for y in range(4):
        for r in range(8):
            to = (SPREAD_X[r][y], r % 4)
            core = taken.get(to, 0)
            taken[to] = core + 1
            pairs.append(((y * 4 + r // 2) * 2 + r % 2, (to[1] * 4 + to[0]) * 2 + core))
            holds[(to[1], to[0], core)] = (r // 4, y)
    return pairs, holds


def piece_plan(holds):
    halves, found = [], []
    for y in range(4):
        for x in range(4):
            for c in range(2):
                d = 2 * c - 1
                at = [
                    (x, c),
                    (x, 1 - c),
                    (x + d, c),
                    (x + d, 1 - c),
                    (x + 2, c),
                    (x - d, 1 - c),
                    (x - d, c),
                    (x + 2, 1 - c),
                ]
                has = [holds[(y, px % 4, pc)] for px, pc in at]
                halves.append([h * 4 + k for h, k in has])
                found.append([[has.index((0, k)), has.index((1, k))] for k in range(4)])
    return [jnp.array(v, jnp.int32) for v in (halves, found)]


def spread_kernel(start_row, rows_ref, *rest):
    pieces = rest[:-7]
    high_hbm, low_hbm, z_f, z_h, z_l, in_sem, out_sem = rest[-7:]
    slots, rows = z_f.shape[:2]

    def fetch(i):
        return pltpu.make_async_copy(pieces[i], z_f.at[i % slots], in_sem.at[i])

    def store(i):
        return [
            pltpu.make_async_copy(z_h.at[i % slots], high_hbm.at[i], out_sem.at[2 * i]),
            pltpu.make_async_copy(z_l.at[i % slots], low_hbm.at[i], out_sem.at[2 * i + 1]),
        ]

    for i in range(slots):
        fetch(i).start()
    row = lax.broadcasted_iota(jnp.int32, (BLOCK, BLOCK), 0)
    for at in range(len(pieces)):
        fetch(at).wait()
        if at >= slots:
            for copy in store(at - slots):
                copy.wait()

        def one(i, carry, at=at):
            here = pl.ds(pl.multiple_of(i * BLOCK, BLOCK), BLOCK)
            value = z_f[at % slots, here, :]
            high = value.astype(jnp.bfloat16)
            low = (value - high.astype(jnp.float32)).astype(jnp.bfloat16)
            place = rows_ref[pl.ds(start_row[at] + i, 1), :]
            place = jnp.where(place >= 0, place & (BLOCK - 1), -1)
            hot = (place == row).astype(jnp.float32).astype(jnp.bfloat16)
            z_h[at % slots, here, :] = jnp.dot(
                hot, high, preferred_element_type=jnp.float32
            ).astype(jnp.bfloat16)
            z_l[at % slots, here, :] = jnp.dot(
                hot, low, preferred_element_type=jnp.float32
            ).astype(jnp.bfloat16)
            return carry

        lax.fori_loop(0, rows // BLOCK, one, 0, unroll=3)
        for copy in store(at):
            copy.start()
        if at + slots < len(pieces):
            fetch(at + slots).start()
    for at in range(len(pieces) - slots, len(pieces)):
        for copy in store(at):
            copy.wait()


def spread(start_row, root_row, pieces):
    rows, cols = pieces[0].shape
    any_spec = pl.BlockSpec(memory_space=pl.ANY)
    shape = (len(pieces), rows, cols)
    held = (SLOTS, rows, cols)
    return pl.pallas_call(
        spread_kernel,
        out_shape=[pltpu.HBM(shape, jnp.bfloat16)] * 2,
        in_specs=[
            pl.BlockSpec(memory_space=pltpu.SMEM),
            pl.BlockSpec(memory_space=pltpu.VMEM),
        ]
        + [any_spec] * len(pieces),
        out_specs=[pl.BlockSpec(memory_space=pltpu.HBM)] * 2,
        scratch_shapes=[
            pltpu.VMEM(held, jnp.float32),
            pltpu.VMEM(held, jnp.bfloat16),
            pltpu.VMEM(held, jnp.bfloat16),
            pltpu.SemaphoreType.DMA((len(pieces),)),
            pltpu.SemaphoreType.DMA((2 * len(pieces),)),
        ],
        compiler_params=pltpu.CompilerParams(vmem_limit_bytes=VMEM_BYTES),
        cost_estimate=pl.CostEstimate(
            flops=10 * 4 * rows * BLOCK * cols, bytes_accessed=80 * rows * cols, transcendentals=0
        ),
    )(start_row, root_row, *pieces)


def product_kernel(calls, table, root_hbm, high_hbm, low_hbm, *rest):
    outs = rest[: len(calls)]
    a_f, z_h, z_l, a_sem, z_sem = rest[len(calls) :]
    rows = outs[0].shape[0]
    per_range = rows // BLOCK
    per_part = PART // BLOCK
    parts = rows // PART
    children = [table[call, 3 * per_range + 2] for call in calls]

    def factor_copies(i, source, target, first):
        return [
            pltpu.make_async_copy(
                source.at[table[children[i], 3 * per_range + side]],
                target.at[i, pl.ds(side * rows, rows)],
                z_sem.at[i, first + side],
            )
            for side in range(2)
        ]

    def start_root(i, part):
        for m in range(per_part):
            mb = pl.multiple_of(table[children[i], part * per_part + m] * BLOCK, BLOCK)
            pltpu.make_async_copy(
                root_hbm.at[:, pl.ds(mb, BLOCK)],
                a_f.at[i, part, :, pl.ds(m * BLOCK, BLOCK)],
                a_sem.at[i, part],
            ).start()

    highs_in = [factor_copies(i, high_hbm, z_h, 0) for i in range(len(calls))]
    lows_in = [factor_copies(i, low_hbm, z_l, 2) for i in range(len(calls))]

    def begin(i):
        start_root(i, 0)
        for copy in highs_in[i] + lows_in[i]:
            copy.start()
        start_root(i, 1)

    begin(0)
    for i, out in enumerate(outs):
        for part in range(parts):
            pltpu.make_async_copy(a_f.at[i, part], a_f.at[i, part], a_sem.at[i, part]).wait()
            if part == 0:
                for copy in highs_in[i]:
                    copy.wait()
            if part + 2 < parts:
                start_root(i, part + 2)
            elif part + 2 == parts and i + 1 < len(calls):
                begin(i + 1)
            highs, lows = [], []
            for k in range(2 * per_range):
                value = a_f[i, part, table[children[i], per_range + k]]
                high = value.astype(jnp.bfloat16)
                highs.append(high)
                lows.append((value - high.astype(jnp.float32)).astype(jnp.bfloat16))
            high = jnp.concatenate(highs, axis=1)
            low = jnp.concatenate(lows, axis=1)
            value = jnp.dot(high, z_h[i], preferred_element_type=jnp.float32)
            value = value + jnp.dot(low, z_h[i], preferred_element_type=jnp.float32)
            if part == 0:
                for copy in lows_in[i]:
                    copy.wait()
            value = value + jnp.dot(high, z_l[i], preferred_element_type=jnp.float32)
            out[part * PART : (part + 1) * PART, :] = value


def product(calls, table, root, high, low):
    rows, cols = high.shape[1:]
    n = len(calls)
    any_spec = pl.BlockSpec(memory_space=pl.ANY)
    root, high, low = [pltpu.with_memory_space_constraint(v, pltpu.HBM) for v in (root, high, low)]
    return pl.pallas_call(
        functools.partial(product_kernel, calls),
        out_shape=[jax.ShapeDtypeStruct((rows, cols), jnp.float32)] * n,
        in_specs=[pl.BlockSpec(memory_space=pltpu.SMEM)] + [any_spec] * 3,
        out_specs=[pl.BlockSpec(memory_space=pltpu.VMEM)] * n,
        scratch_shapes=[
            pltpu.VMEM((n, rows // PART, root.shape[0], PART, BLOCK), jnp.float32),
            pltpu.VMEM((n, 2 * rows, cols), jnp.bfloat16),
            pltpu.VMEM((n, 2 * rows, cols), jnp.bfloat16),
            pltpu.SemaphoreType.DMA((n, rows // PART)),
            pltpu.SemaphoreType.DMA((n, 4)),
        ],
        compiler_params=pltpu.CompilerParams(vmem_limit_bytes=(12 + 14 * n) * 1024 * 1024),
        cost_estimate=pl.CostEstimate(
            flops=n * 3 * 2 * rows * 2 * rows * cols,
            bytes_accessed=n * 12 * rows * rows,
            transcendentals=0,
        ),
    )(table, root, high, low)


def weigh_kernel(piece, first, second, high_hbm, low_hbm, total, sums, high, low, sem):
    rows, cols = total.shape
    copies = [
        pltpu.make_async_copy(high_hbm.at[piece], high, sem.at[0]),
        pltpu.make_async_copy(low_hbm.at[piece], low, sem.at[1]),
    ]
    for copy in copies:
        copy.start()
    for copy in copies:
        copy.wait()

    def one(i, found):
        at = pl.ds(pl.multiple_of(i * 64, 64), 64)
        value = first[at, :] + second[at, :]
        total[at, :] = value
        factor = high[at, :].astype(jnp.float32) + low[at, :].astype(jnp.float32)
        return found + jnp.sum((factor * value).reshape(8, 8, cols), axis=0)

    found = lax.fori_loop(0, rows // 64, one, jnp.zeros((8, cols), jnp.float32))
    sums[...] = jnp.sum(found, axis=0, keepdims=True)


def weigh(piece, first, second, high, low):
    rows, cols = first.shape
    any_spec = pl.BlockSpec(memory_space=pl.ANY)
    vmem = pl.BlockSpec(memory_space=pltpu.VMEM)
    high, low = [pltpu.with_memory_space_constraint(v, pltpu.HBM) for v in (high, low)]
    return pl.pallas_call(
        functools.partial(weigh_kernel, piece),
        out_shape=[
            jax.ShapeDtypeStruct((rows, cols), jnp.float32),
            jax.ShapeDtypeStruct((1, cols), jnp.float32),
        ],
        in_specs=[vmem, vmem, any_spec, any_spec],
        out_specs=[vmem, vmem],
        scratch_shapes=[
            pltpu.VMEM((rows, cols), jnp.bfloat16),
            pltpu.VMEM((rows, cols), jnp.bfloat16),
            pltpu.SemaphoreType.DMA((2,)),
        ],
        compiler_params=pltpu.CompilerParams(vmem_limit_bytes=VMEM_BYTES),
        cost_estimate=pl.CostEstimate(
            flops=4 * rows * cols, bytes_accessed=16 * rows * cols, transcendentals=0
        ),
    )(first, second, high, low)


def per_device(root_inverse, root_row, coupling, pivot_variance):
    zh = lax.axis_index("zh")
    y = lax.axis_index("y")
    x = lax.axis_index("x")
    core = lax.axis_index("core")
    rows, cols = coupling.shape[1:]
    ranges = root_row.shape[1] // rows
    per_range = rows // BLOCK
    own_range = 2 * x + core
    device = (y * 4 + x) * 2 + core

    root = lax.all_gather(root_inverse, ("zh", "zl"), axis=0, tiled=False)

    pairs, holds = spread_plan()
    halves, found = piece_plan(holds)
    spots = lax.dynamic_slice(halves, (device, 0), (1, 8))[0]
    child = zh * 4 + jnp.concatenate([spots & 3, jnp.stack([y, (y + 1 - 2 * core) & 3])])
    ranged = jnp.concatenate([y + 4 * (spots >> 2), jnp.stack([own_range, own_range])])
    start_row = (child * ranges + ranged) * per_range
    block = (root_row[:, ::BLOCK] >> 7).reshape(-1, ranges, per_range)

    def blocks_of(r):
        return lax.dynamic_slice(block, (zh * 4, r, 0), (4, 1, per_range))[:, 0] & 7

    order = (y + jnp.stack([2, 3 - 2 * core, 1 + 2 * core, 0])) & 3
    table = jnp.concatenate(
        [
            blocks_of(own_range),
            blocks_of(y),
            blocks_of(y + 4) + 8,
            lax.dynamic_slice(found, (device, 0, 0), (1, 4, 2))[0],
            order[:, None],
        ],
        axis=1,
    ).astype(jnp.int32)
    own = lax.ppermute(coupling[0], ("y", "x", "core"), pairs)
    rows_of = root_row.reshape(-1, BLOCK)
    own, table, start_row, rows_of = lax.optimization_barrier((own, table, start_row, rows_of))
    along_x = opposite(4)
    beside = lax.ppermute(own, "core", CORES)
    near = lax.ppermute(own, ("x", "core"), along_x)
    near_beside = lax.ppermute(beside, ("x", "core"), along_x)
    far = lax.ppermute(near, ("x", "core"), along_x)
    pieces = [own, beside, near, near_beside, far]
    pieces += [lax.ppermute(p, "core", CORES) for p in (near, near_beside, far)]
    pieces += [coupling[0], lax.ppermute(coupling[0], ("y", "core"), opposite(4, -1))]
    high, low = spread(start_row, rows_of, pieces)

    root = root.reshape(-1, *root_inverse.shape)
    (far,) = product((0,), table, root, high, low)
    passed = lax.ppermute(far, ("y", "core"), opposite(4))
    second, first = product((2, 1), table, root, high, low)
    back = lax.ppermute(first, ("y", "core"), opposite(4, -1))
    last, last_sums = weigh(9, second, passed, high, low)
    last_sums = lax.ppermute(last_sums, ("y", "core"), opposite(4))
    table, last, last_sums = lax.optimization_barrier((table, last, last_sums))
    forth = lax.ppermute(last, ("y", "core"), opposite(4))
    (home,) = product((3,), table, root, high, low)
    kept, sums = weigh(8, home, back, high, low)
    sums = lax.all_to_all(
        jnp.broadcast_to(sums + last_sums, (8, cols)),
        ("x", "core"),
        split_axis=0,
        concat_axis=0,
        tiled=True,
    )
    marginal = pivot_variance + jnp.sum(sums, axis=0, keepdims=True)
    kept, marginal = lax.optimization_barrier((kept, marginal))
    summed = kept + forth

    own_place = lax.dynamic_slice(root_row, (zh * 4 + y, own_range * rows), (1, rows))[0]
    own_place = jnp.where(own_place >= 0, own_place & (BLOCK - 1), -1).reshape(per_range, BLOCK)
    hot = (own_place[:, :, None] == jnp.arange(BLOCK, dtype=jnp.int32)).astype(jnp.float32)
    result = -jnp.einsum(
        "iuo,ion->iun", hot, summed.reshape(per_range, BLOCK, cols), precision=lax.Precision.HIGHEST
    )

    return result.reshape(1, rows, cols), marginal


def solution(mesh):
    split = Mesh(mesh.devices.reshape(2, 4, 4, 2, 8), ("zh", "y", "x", "core", "zl"))
    leaf, row, col = ("zh", "y"), ("x", "core"), "zl"
    return jax.shard_map(
        per_device,
        mesh=split,
        in_specs=(P(row, ("zh", "y", "zl")), P(), P(leaf, row, col), P(leaf, col)),
        out_specs=(P(leaf, row, col), P(leaf, col)),
        check_vma=False,
    )
```

```python
import functools

import jax
import jax.numpy as jnp
from jax import lax
from jax.experimental import pallas as pl
from jax.experimental.pallas import tpu as pltpu
from jax.sharding import Mesh, PartitionSpec as P

BLOCK = 128
PART = 256
SLOTS = 4
VMEM_BYTES = 24 * 1024 * 1024
CORES = [(0, 1), (1, 0)]
SPREAD_X = (
    (3, 1, 0, 0),
    (0, 3, 0, 1),
    (1, 2, 0, 1),
    (2, 0, 1, 1),
    (2, 2, 1, 3),
    (3, 1, 2, 2),
    (3, 0, 2, 3),
    (3, 2, 3, 0),
)


def shift(size, step):
    return [(i, (i + step) % size) for i in range(size)]


def opposite(size, way=1):
    return [
        (2 * i + c, (i + way * (1 - 2 * c)) % size * 2 + c) for i in range(size) for c in range(2)
    ]


def spread_plan():
    pairs, holds, taken = [], {}, {}
    for y in range(4):
        for r in range(8):
            to = (SPREAD_X[r][y], r % 4)
            core = taken.get(to, 0)
            taken[to] = core + 1
            pairs.append(((y * 4 + r // 2) * 2 + r % 2, (to[1] * 4 + to[0]) * 2 + core))
            holds[(to[1], to[0], core)] = (r // 4, y)
    return pairs, holds


def piece_plan(holds):
    halves, found = [], []
    for y in range(4):
        for x in range(4):
            for c in range(2):
                d = 2 * c - 1
                at = [
                    (x, c),
                    (x, 1 - c),
                    (x + d, c),
                    (x + d, 1 - c),
                    (x + 2, c),
                    (x - d, 1 - c),
                    (x - d, c),
                    (x + 2, 1 - c),
                ]
                has = [holds[(y, px % 4, pc)] for px, pc in at]
                halves.append([h * 4 + k for h, k in has])
                found.append([[has.index((0, k)), has.index((1, k))] for k in range(4)])
    return [jnp.array(v, jnp.int32) for v in (halves, found)]


def spread_kernel(start_row, rows_ref, *rest):
    pieces = rest[:-7]
    high_hbm, low_hbm, z_f, z_h, z_l, in_sem, out_sem = rest[-7:]
    slots, rows = z_f.shape[:2]

    def fetch(i):
        return pltpu.make_async_copy(pieces[i], z_f.at[i % slots], in_sem.at[i])

    def store(i):
        return [
            pltpu.make_async_copy(z_h.at[i % slots], high_hbm.at[i], out_sem.at[2 * i]),
            pltpu.make_async_copy(z_l.at[i % slots], low_hbm.at[i], out_sem.at[2 * i + 1]),
        ]

    for i in range(slots):
        fetch(i).start()
    row = lax.broadcasted_iota(jnp.int32, (BLOCK, BLOCK), 0)
    for at in range(len(pieces)):
        fetch(at).wait()
        if at >= slots:
            for copy in store(at - slots):
                copy.wait()

        def one(i, carry, at=at):
            here = pl.ds(pl.multiple_of(i * BLOCK, BLOCK), BLOCK)
            value = z_f[at % slots, here, :]
            high = value.astype(jnp.bfloat16)
            low = (value - high.astype(jnp.float32)).astype(jnp.bfloat16)
            place = rows_ref[pl.ds(start_row[at] + i, 1), :]
            place = jnp.where(place >= 0, place & (BLOCK - 1), -1)
            hot = (place == row).astype(jnp.float32).astype(jnp.bfloat16)
            z_h[at % slots, here, :] = jnp.dot(
                hot, high, preferred_element_type=jnp.float32
            ).astype(jnp.bfloat16)
            z_l[at % slots, here, :] = jnp.dot(
                hot, low, preferred_element_type=jnp.float32
            ).astype(jnp.bfloat16)
            return carry

        lax.fori_loop(0, rows // BLOCK, one, 0, unroll=3)
        for copy in store(at):
            copy.start()
        if at + slots < len(pieces):
            fetch(at + slots).start()
    for at in range(len(pieces) - slots, len(pieces)):
        for copy in store(at):
            copy.wait()


def spread(start_row, root_row, pieces):
    rows, cols = pieces[0].shape
    any_spec = pl.BlockSpec(memory_space=pl.ANY)
    shape = (len(pieces), rows, cols)
    held = (SLOTS, rows, cols)
    return pl.pallas_call(
        spread_kernel,
        out_shape=[pltpu.HBM(shape, jnp.bfloat16)] * 2,
        in_specs=[
            pl.BlockSpec(memory_space=pltpu.SMEM),
            pl.BlockSpec(memory_space=pltpu.VMEM),
        ]
        + [any_spec] * len(pieces),
        out_specs=[pl.BlockSpec(memory_space=pltpu.HBM)] * 2,
        scratch_shapes=[
            pltpu.VMEM(held, jnp.float32),
            pltpu.VMEM(held, jnp.bfloat16),
            pltpu.VMEM(held, jnp.bfloat16),
            pltpu.SemaphoreType.DMA((len(pieces),)),
            pltpu.SemaphoreType.DMA((2 * len(pieces),)),
        ],
        compiler_params=pltpu.CompilerParams(vmem_limit_bytes=VMEM_BYTES),
        cost_estimate=pl.CostEstimate(
            flops=10 * 4 * rows * BLOCK * cols, bytes_accessed=80 * rows * cols, transcendentals=0
        ),
    )(start_row, root_row, *pieces)


def product_kernel(calls, table, root_hbm, high_hbm, low_hbm, *rest):
    outs = rest[: len(calls)]
    a_f, z_h, z_l, a_sem, z_sem = rest[len(calls) :]
    rows = outs[0].shape[0]
    per_range = rows // BLOCK
    per_part = PART // BLOCK
    parts = rows // PART
    children = [table[call, 3 * per_range + 2] for call in calls]

    def factor_copies(i, source, target, first):
        return [
            pltpu.make_async_copy(
                source.at[table[children[i], 3 * per_range + side]],
                target.at[i, pl.ds(side * rows, rows)],
                z_sem.at[i, first + side],
            )
            for side in range(2)
        ]

    def start_root(i, part):
        for m in range(per_part):
            mb = pl.multiple_of(table[children[i], part * per_part + m] * BLOCK, BLOCK)
            pltpu.make_async_copy(
                root_hbm.at[:, pl.ds(mb, BLOCK)],
                a_f.at[i, part, :, pl.ds(m * BLOCK, BLOCK)],
                a_sem.at[i, part],
            ).start()

    highs_in = [factor_copies(i, high_hbm, z_h, 0) for i in range(len(calls))]
    lows_in = [factor_copies(i, low_hbm, z_l, 2) for i in range(len(calls))]

    def begin(i):
        start_root(i, 0)
        for copy in highs_in[i] + lows_in[i]:
            copy.start()
        start_root(i, 1)

    begin(0)
    for i, out in enumerate(outs):
        for part in range(parts):
            pltpu.make_async_copy(a_f.at[i, part], a_f.at[i, part], a_sem.at[i, part]).wait()
            if part == 0:
                for copy in highs_in[i]:
                    copy.wait()
            if part + 2 < parts:
                start_root(i, part + 2)
            elif part + 2 == parts and i + 1 < len(calls):
                begin(i + 1)
            highs, lows = [], []
            for k in range(2 * per_range):
                value = a_f[i, part, table[children[i], per_range + k]]
                high = value.astype(jnp.bfloat16)
                highs.append(high)
                lows.append((value - high.astype(jnp.float32)).astype(jnp.bfloat16))
            high = jnp.concatenate(highs, axis=1)
            low = jnp.concatenate(lows, axis=1)
            value = jnp.dot(high, z_h[i], preferred_element_type=jnp.float32)
            value = value + jnp.dot(low, z_h[i], preferred_element_type=jnp.float32)
            if part == 0:
                for copy in lows_in[i]:
                    copy.wait()
            value = value + jnp.dot(high, z_l[i], preferred_element_type=jnp.float32)
            out[part * PART : (part + 1) * PART, :] = value


def product(calls, table, root, high, low):
    rows, cols = high.shape[1:]
    n = len(calls)
    any_spec = pl.BlockSpec(memory_space=pl.ANY)
    root, high, low = [pltpu.with_memory_space_constraint(v, pltpu.HBM) for v in (root, high, low)]
    return pl.pallas_call(
        functools.partial(product_kernel, calls),
        out_shape=[jax.ShapeDtypeStruct((rows, cols), jnp.float32)] * n,
        in_specs=[pl.BlockSpec(memory_space=pltpu.SMEM)] + [any_spec] * 3,
        out_specs=[pl.BlockSpec(memory_space=pltpu.VMEM)] * n,
        scratch_shapes=[
            pltpu.VMEM((n, rows // PART, root.shape[0], PART, BLOCK), jnp.float32),
            pltpu.VMEM((n, 2 * rows, cols), jnp.bfloat16),
            pltpu.VMEM((n, 2 * rows, cols), jnp.bfloat16),
            pltpu.SemaphoreType.DMA((n, rows // PART)),
            pltpu.SemaphoreType.DMA((n, 4)),
        ],
        compiler_params=pltpu.CompilerParams(vmem_limit_bytes=(12 + 14 * n) * 1024 * 1024),
        cost_estimate=pl.CostEstimate(
            flops=n * 3 * 2 * rows * 2 * rows * cols,
            bytes_accessed=n * 12 * rows * rows,
            transcendentals=0,
        ),
    )(table, root, high, low)


def weigh_kernel(piece, first, second, high_hbm, low_hbm, total, sums, high, low, sem):
    rows, cols = total.shape
    copies = [
        pltpu.make_async_copy(high_hbm.at[piece], high, sem.at[0]),
        pltpu.make_async_copy(low_hbm.at[piece], low, sem.at[1]),
    ]
    for copy in copies:
        copy.start()
    for copy in copies:
        copy.wait()

    def one(i, found):
        at = pl.ds(pl.multiple_of(i * 64, 64), 64)
        value = first[at, :] + second[at, :]
        total[at, :] = value
        factor = high[at, :].astype(jnp.float32) + low[at, :].astype(jnp.float32)
        return found + jnp.sum((factor * value).reshape(8, 8, cols), axis=0)

    found = lax.fori_loop(0, rows // 64, one, jnp.zeros((8, cols), jnp.float32))
    sums[...] = jnp.sum(found, axis=0, keepdims=True)


def weigh(piece, first, second, high, low):
    rows, cols = first.shape
    any_spec = pl.BlockSpec(memory_space=pl.ANY)
    vmem = pl.BlockSpec(memory_space=pltpu.VMEM)
    high, low = [pltpu.with_memory_space_constraint(v, pltpu.HBM) for v in (high, low)]
    return pl.pallas_call(
        functools.partial(weigh_kernel, piece),
        out_shape=[
            jax.ShapeDtypeStruct((rows, cols), jnp.float32),
            jax.ShapeDtypeStruct((1, cols), jnp.float32),
        ],
        in_specs=[vmem, vmem, any_spec, any_spec],
        out_specs=[vmem, vmem],
        scratch_shapes=[
            pltpu.VMEM((rows, cols), jnp.bfloat16),
            pltpu.VMEM((rows, cols), jnp.bfloat16),
            pltpu.SemaphoreType.DMA((2,)),
        ],
        compiler_params=pltpu.CompilerParams(vmem_limit_bytes=VMEM_BYTES),
        cost_estimate=pl.CostEstimate(
            flops=4 * rows * cols, bytes_accessed=16 * rows * cols, transcendentals=0
        ),
    )(first, second, high, low)


def per_device(root_inverse, root_row, coupling, pivot_variance):
    zh = lax.axis_index("zh")
    y = lax.axis_index("y")
    x = lax.axis_index("x")
    core = lax.axis_index("core")
    rows, cols = coupling.shape[1:]
    ranges = root_row.shape[1] // rows
    per_range = rows // BLOCK
    own_range = 2 * x + core
    device = (y * 4 + x) * 2 + core

    root = lax.all_gather(root_inverse, ("zh", "zl"), axis=0, tiled=False)

    pairs, holds = spread_plan()
    halves, found = piece_plan(holds)
    spots = lax.dynamic_slice(halves, (device, 0), (1, 8))[0]
    child = zh * 4 + jnp.concatenate([spots & 3, jnp.stack([y, (y + 1 - 2 * core) & 3])])
    ranged = jnp.concatenate([y + 4 * (spots >> 2), jnp.stack([own_range, own_range])])
    start_row = (child * ranges + ranged) * per_range
    block = (root_row[:, ::BLOCK] >> 7).reshape(-1, ranges, per_range)

    def blocks_of(r):
        return lax.dynamic_slice(block, (zh * 4, r, 0), (4, 1, per_range))[:, 0] & 7

    order = (y + jnp.stack([2, 3 - 2 * core, 1 + 2 * core, 0])) & 3
    table = jnp.concatenate(
        [
            blocks_of(own_range),
            blocks_of(y),
            blocks_of(y + 4) + 8,
            lax.dynamic_slice(found, (device, 0, 0), (1, 4, 2))[0],
            order[:, None],
        ],
        axis=1,
    ).astype(jnp.int32)
    own = lax.ppermute(coupling[0], ("y", "x", "core"), pairs)
    rows_of = root_row.reshape(-1, BLOCK)
    own, table, start_row, rows_of = lax.optimization_barrier((own, table, start_row, rows_of))
    along_x = opposite(4)
    beside = lax.ppermute(own, "core", CORES)
    near = lax.ppermute(own, ("x", "core"), along_x)
    near_beside = lax.ppermute(beside, ("x", "core"), along_x)
    far = lax.ppermute(near, ("x", "core"), along_x)
    pieces = [own, beside, near, near_beside, far]
    pieces += [lax.ppermute(p, "core", CORES) for p in (near, near_beside, far)]
    pieces += [coupling[0], lax.ppermute(coupling[0], ("y", "core"), opposite(4, -1))]
    high, low = spread(start_row, rows_of, pieces)

    root = root.reshape(-1, *root_inverse.shape)
    (far,) = product((0,), table, root, high, low)
    passed = lax.ppermute(far, ("y", "core"), opposite(4))
    second, first = product((2, 1), table, root, high, low)
    back = lax.ppermute(first, ("y", "core"), opposite(4, -1))
    last, last_sums = weigh(9, second, passed, high, low)
    table, last, last_sums = lax.optimization_barrier((table, last, last_sums))
    last_sums = lax.ppermute(last_sums, ("y", "core"), opposite(4))
    (home,) = product((3,), table, root, high, low)
    last, home, last_sums = lax.optimization_barrier((last, home, last_sums))
    forth = lax.ppermute(last, ("y", "core"), opposite(4))
    kept, sums = weigh(8, home, back, high, low)
    sums = jnp.broadcast_to(sums + last_sums, (8, cols))
    kept, sums = lax.optimization_barrier((kept, sums))
    sums = lax.all_to_all(sums, ("x", "core"), split_axis=0, concat_axis=0, tiled=True)
    marginal = pivot_variance + jnp.sum(sums, axis=0, keepdims=True)
    summed = kept + forth

    own_place = lax.dynamic_slice(root_row, (zh * 4 + y, own_range * rows), (1, rows))[0]
    own_place = jnp.where(own_place >= 0, own_place & (BLOCK - 1), -1).reshape(per_range, BLOCK)
    hot = (own_place[:, :, None] == jnp.arange(BLOCK, dtype=jnp.int32)).astype(jnp.float32)
    result = -jnp.einsum(
        "iuo,ion->iun", hot, summed.reshape(per_range, BLOCK, cols), precision=lax.Precision.HIGHEST
    )

    return result.reshape(1, rows, cols), marginal


def solution(mesh):
    split = Mesh(mesh.devices.reshape(2, 4, 4, 2, 8), ("zh", "y", "x", "core", "zl"))
    leaf, row, col = ("zh", "y"), ("x", "core"), "zl"
    return jax.shard_map(
        per_device,
        mesh=split,
        in_specs=(P(row, ("zh", "y", "zl")), P(), P(leaf, row, col), P(leaf, col)),
        out_specs=(P(leaf, row, col), P(leaf, col)),
        check_vma=False,
    )
```

```python
import functools

import jax
import jax.numpy as jnp
from jax import lax
from jax.experimental import pallas as pl
from jax.experimental.pallas import tpu as pltpu
from jax.sharding import Mesh, PartitionSpec as P

BLOCK = 128
PART = 256
SLOTS = 4
VMEM_BYTES = 24 * 1024 * 1024
CORES = [(0, 1), (1, 0)]
SPREAD_X = (
    (3, 1, 0, 0),
    (0, 3, 0, 1),
    (1, 2, 0, 1),
    (2, 0, 1, 1),
    (2, 2, 1, 3),
    (3, 1, 2, 2),
    (3, 0, 2, 3),
    (3, 2, 3, 0),
)


def shift(size, step):
    return [(i, (i + step) % size) for i in range(size)]


def opposite(size, way=1):
    return [
        (2 * i + c, (i + way * (1 - 2 * c)) % size * 2 + c) for i in range(size) for c in range(2)
    ]


def spread_plan():
    pairs, holds, taken = [], {}, {}
    for y in range(4):
        for r in range(8):
            to = (SPREAD_X[r][y], r % 4)
            core = taken.get(to, 0)
            taken[to] = core + 1
            pairs.append(((y * 4 + r // 2) * 2 + r % 2, (to[1] * 4 + to[0]) * 2 + core))
            holds[(to[1], to[0], core)] = (r // 4, y)
    return pairs, holds


def piece_plan(holds):
    halves, found = [], []
    for y in range(4):
        for x in range(4):
            for c in range(2):
                d = 2 * c - 1
                at = [
                    (x, c),
                    (x, 1 - c),
                    (x + d, c),
                    (x + d, 1 - c),
                    (x + 2, c),
                    (x - d, 1 - c),
                    (x - d, c),
                    (x + 2, 1 - c),
                ]
                has = [holds[(y, px % 4, pc)] for px, pc in at]
                halves.append([h * 4 + k for h, k in has])
                found.append([[has.index((0, k)), has.index((1, k))] for k in range(4)])
    return [jnp.array(v, jnp.int32) for v in (halves, found)]


def spread_kernel(start_row, rows_ref, *rest):
    pieces = rest[:-7]
    high_hbm, low_hbm, z_f, z_h, z_l, in_sem, out_sem = rest[-7:]
    slots, rows = z_f.shape[:2]

    def fetch(i):
        return pltpu.make_async_copy(pieces[i], z_f.at[i % slots], in_sem.at[i])

    def store(i):
        return [
            pltpu.make_async_copy(z_h.at[i % slots], high_hbm.at[i], out_sem.at[2 * i]),
            pltpu.make_async_copy(z_l.at[i % slots], low_hbm.at[i], out_sem.at[2 * i + 1]),
        ]

    for i in range(slots):
        fetch(i).start()
    row = lax.broadcasted_iota(jnp.int32, (BLOCK, BLOCK), 0)
    for at in range(len(pieces)):
        fetch(at).wait()
        if at >= slots:
            for copy in store(at - slots):
                copy.wait()

        def one(i, carry, at=at):
            here = pl.ds(pl.multiple_of(i * BLOCK, BLOCK), BLOCK)
            value = z_f[at % slots, here, :]
            high = value.astype(jnp.bfloat16)
            low = (value - high.astype(jnp.float32)).astype(jnp.bfloat16)
            place = rows_ref[pl.ds(start_row[at] + i, 1), :]
            place = jnp.where(place >= 0, place & (BLOCK - 1), -1)
            hot = (place == row).astype(jnp.float32).astype(jnp.bfloat16)
            z_h[at % slots, here, :] = jnp.dot(
                hot, high, preferred_element_type=jnp.float32
            ).astype(jnp.bfloat16)
            z_l[at % slots, here, :] = jnp.dot(
                hot, low, preferred_element_type=jnp.float32
            ).astype(jnp.bfloat16)
            return carry

        lax.fori_loop(0, rows // BLOCK, one, 0, unroll=3)
        for copy in store(at):
            copy.start()
        if at + slots < len(pieces):
            fetch(at + slots).start()
    for at in range(len(pieces) - slots, len(pieces)):
        for copy in store(at):
            copy.wait()


def spread(start_row, root_row, pieces):
    rows, cols = pieces[0].shape
    any_spec = pl.BlockSpec(memory_space=pl.ANY)
    shape = (len(pieces), rows, cols)
    held = (SLOTS, rows, cols)
    return pl.pallas_call(
        spread_kernel,
        out_shape=[pltpu.HBM(shape, jnp.bfloat16)] * 2,
        in_specs=[
            pl.BlockSpec(memory_space=pltpu.SMEM),
            pl.BlockSpec(memory_space=pltpu.VMEM),
        ]
        + [any_spec] * len(pieces),
        out_specs=[pl.BlockSpec(memory_space=pltpu.HBM)] * 2,
        scratch_shapes=[
            pltpu.VMEM(held, jnp.float32),
            pltpu.VMEM(held, jnp.bfloat16),
            pltpu.VMEM(held, jnp.bfloat16),
            pltpu.SemaphoreType.DMA((len(pieces),)),
            pltpu.SemaphoreType.DMA((2 * len(pieces),)),
        ],
        compiler_params=pltpu.CompilerParams(vmem_limit_bytes=VMEM_BYTES),
        cost_estimate=pl.CostEstimate(
            flops=10 * 4 * rows * BLOCK * cols, bytes_accessed=80 * rows * cols, transcendentals=0
        ),
    )(start_row, root_row, *pieces)


def product_kernel(calls, table, root_hbm, high_hbm, low_hbm, *rest):
    outs = rest[: len(calls)]
    a_f, z_h, z_l, a_sem, z_sem = rest[len(calls) :]
    rows = outs[0].shape[0]
    per_range = rows // BLOCK
    per_part = PART // BLOCK
    parts = rows // PART
    children = [table[call, 3 * per_range + 2] for call in calls]

    def factor_copies(i, source, target, first):
        return [
            pltpu.make_async_copy(
                source.at[table[children[i], 3 * per_range + side]],
                target.at[i, pl.ds(side * rows, rows)],
                z_sem.at[i, first + side],
            )
            for side in range(2)
        ]

    def start_root(i, part):
        for m in range(per_part):
            mb = pl.multiple_of(table[children[i], part * per_part + m] * BLOCK, BLOCK)
            pltpu.make_async_copy(
                root_hbm.at[:, pl.ds(mb, BLOCK)],
                a_f.at[i, part, :, pl.ds(m * BLOCK, BLOCK)],
                a_sem.at[i, part],
            ).start()

    highs_in = [factor_copies(i, high_hbm, z_h, 0) for i in range(len(calls))]
    lows_in = [factor_copies(i, low_hbm, z_l, 2) for i in range(len(calls))]

    def begin(i):
        start_root(i, 0)
        for copy in highs_in[i] + lows_in[i]:
            copy.start()
        start_root(i, 1)

    begin(0)
    for i, out in enumerate(outs):
        for part in range(parts):
            pltpu.make_async_copy(a_f.at[i, part], a_f.at[i, part], a_sem.at[i, part]).wait()
            if part == 0:
                for copy in highs_in[i]:
                    copy.wait()
            if part + 2 < parts:
                start_root(i, part + 2)
            elif part + 2 == parts and i + 1 < len(calls):
                begin(i + 1)
            highs, lows = [], []
            for k in range(2 * per_range):
                value = a_f[i, part, table[children[i], per_range + k]]
                high = value.astype(jnp.bfloat16)
                highs.append(high)
                lows.append((value - high.astype(jnp.float32)).astype(jnp.bfloat16))
            high = jnp.concatenate(highs, axis=1)
            low = jnp.concatenate(lows, axis=1)
            value = jnp.dot(high, z_h[i], preferred_element_type=jnp.float32)
            value = value + jnp.dot(low, z_h[i], preferred_element_type=jnp.float32)
            if part == 0:
                for copy in lows_in[i]:
                    copy.wait()
            value = value + jnp.dot(high, z_l[i], preferred_element_type=jnp.float32)
            out[part * PART : (part + 1) * PART, :] = value


def product(calls, table, root, high, low):
    rows, cols = high.shape[1:]
    n = len(calls)
    any_spec = pl.BlockSpec(memory_space=pl.ANY)
    root, high, low = [pltpu.with_memory_space_constraint(v, pltpu.HBM) for v in (root, high, low)]
    return pl.pallas_call(
        functools.partial(product_kernel, calls),
        out_shape=[jax.ShapeDtypeStruct((rows, cols), jnp.float32)] * n,
        in_specs=[pl.BlockSpec(memory_space=pltpu.SMEM)] + [any_spec] * 3,
        out_specs=[pl.BlockSpec(memory_space=pltpu.VMEM)] * n,
        scratch_shapes=[
            pltpu.VMEM((n, rows // PART, root.shape[0], PART, BLOCK), jnp.float32),
            pltpu.VMEM((n, 2 * rows, cols), jnp.bfloat16),
            pltpu.VMEM((n, 2 * rows, cols), jnp.bfloat16),
            pltpu.SemaphoreType.DMA((n, rows // PART)),
            pltpu.SemaphoreType.DMA((n, 4)),
        ],
        compiler_params=pltpu.CompilerParams(vmem_limit_bytes=(12 + 14 * n) * 1024 * 1024),
        cost_estimate=pl.CostEstimate(
            flops=n * 3 * 2 * rows * 2 * rows * cols,
            bytes_accessed=n * 12 * rows * rows,
            transcendentals=0,
        ),
    )(table, root, high, low)


def weigh_kernel(piece, first, second, high_hbm, low_hbm, total, sums, high, low, sem):
    rows, cols = total.shape
    copies = [
        pltpu.make_async_copy(high_hbm.at[piece], high, sem.at[0]),
        pltpu.make_async_copy(low_hbm.at[piece], low, sem.at[1]),
    ]
    for copy in copies:
        copy.start()
    for copy in copies:
        copy.wait()

    def one(i, found):
        at = pl.ds(pl.multiple_of(i * 64, 64), 64)
        value = first[at, :] + second[at, :]
        total[at, :] = value
        factor = high[at, :].astype(jnp.float32) + low[at, :].astype(jnp.float32)
        return found + jnp.sum((factor * value).reshape(8, 8, cols), axis=0)

    found = lax.fori_loop(0, rows // 64, one, jnp.zeros((8, cols), jnp.float32))
    sums[...] = jnp.sum(found, axis=0, keepdims=True)


def weigh(piece, first, second, high, low):
    rows, cols = first.shape
    any_spec = pl.BlockSpec(memory_space=pl.ANY)
    vmem = pl.BlockSpec(memory_space=pltpu.VMEM)
    high, low = [pltpu.with_memory_space_constraint(v, pltpu.HBM) for v in (high, low)]
    return pl.pallas_call(
        functools.partial(weigh_kernel, piece),
        out_shape=[
            jax.ShapeDtypeStruct((rows, cols), jnp.float32),
            jax.ShapeDtypeStruct((1, cols), jnp.float32),
        ],
        in_specs=[vmem, vmem, any_spec, any_spec],
        out_specs=[vmem, vmem],
        scratch_shapes=[
            pltpu.VMEM((rows, cols), jnp.bfloat16),
            pltpu.VMEM((rows, cols), jnp.bfloat16),
            pltpu.SemaphoreType.DMA((2,)),
        ],
        compiler_params=pltpu.CompilerParams(vmem_limit_bytes=VMEM_BYTES),
        cost_estimate=pl.CostEstimate(
            flops=4 * rows * cols, bytes_accessed=16 * rows * cols, transcendentals=0
        ),
    )(first, second, high, low)


def per_device(root_inverse, root_row, coupling, pivot_variance):
    zh = lax.axis_index("zh")
    y = lax.axis_index("y")
    x = lax.axis_index("x")
    core = lax.axis_index("core")
    rows, cols = coupling.shape[1:]
    ranges = root_row.shape[1] // rows
    per_range = rows // BLOCK
    own_range = 2 * x + core
    device = (y * 4 + x) * 2 + core

    root = lax.all_gather(root_inverse, ("zh", "zl"), axis=0, tiled=False)

    pairs, holds = spread_plan()
    halves, found = piece_plan(holds)
    spots = lax.dynamic_slice(halves, (device, 0), (1, 8))[0]
    child = zh * 4 + jnp.concatenate([spots & 3, jnp.stack([y, (y + 1 - 2 * core) & 3])])
    ranged = jnp.concatenate([y + 4 * (spots >> 2), jnp.stack([own_range, own_range])])
    start_row = (child * ranges + ranged) * per_range
    block = (root_row[:, ::BLOCK] >> 7).reshape(-1, ranges, per_range)

    def blocks_of(r):
        return lax.dynamic_slice(block, (zh * 4, r, 0), (4, 1, per_range))[:, 0] & 7

    order = (y + jnp.stack([2, 3 - 2 * core, 1 + 2 * core, 0])) & 3
    table = jnp.concatenate(
        [
            blocks_of(own_range),
            blocks_of(y),
            blocks_of(y + 4) + 8,
            lax.dynamic_slice(found, (device, 0, 0), (1, 4, 2))[0],
            order[:, None],
        ],
        axis=1,
    ).astype(jnp.int32)
    own = lax.ppermute(coupling[0], ("y", "x", "core"), pairs)
    rows_of = root_row.reshape(-1, BLOCK)
    own, table, start_row, rows_of = lax.optimization_barrier((own, table, start_row, rows_of))
    along_x = opposite(4)
    beside = lax.ppermute(own, "core", CORES)
    near = lax.ppermute(own, ("x", "core"), along_x)
    near_beside = lax.ppermute(beside, ("x", "core"), along_x)
    far = lax.ppermute(near, ("x", "core"), along_x)
    pieces = [own, beside, near, near_beside, far]
    pieces += [lax.ppermute(p, "core", CORES) for p in (near, near_beside, far)]
    pieces += [coupling[0], lax.ppermute(coupling[0], ("y", "core"), opposite(4, -1))]
    high, low = spread(start_row, rows_of, pieces)

    root = root.reshape(-1, *root_inverse.shape)
    (far,) = product((0,), table, root, high, low)
    passed = lax.ppermute(far, ("y", "core"), opposite(4))
    second, first = product((2, 1), table, root, high, low)
    back = lax.ppermute(first, ("y", "core"), opposite(4, -1))
    last, last_sums = weigh(9, second, passed, high, low)
    last_sums = lax.ppermute(last_sums, ("y", "core"), opposite(4))
    table, last, last_sums = lax.optimization_barrier((table, last, last_sums))
    forth = lax.ppermute(last, ("y", "core"), opposite(4))
    (home,) = product((3,), table, root, high, low)
    kept, sums = weigh(8, home, back, high, low)
    sums = jnp.broadcast_to(sums + last_sums, (8, cols))
    kept, sums = lax.optimization_barrier((kept, sums))
    sums = lax.all_to_all(sums, ("x", "core"), split_axis=0, concat_axis=0, tiled=True)
    summed = kept + forth

    own_place = lax.dynamic_slice(root_row, (zh * 4 + y, own_range * rows), (1, rows))[0]
    own_place = jnp.where(own_place >= 0, own_place & (BLOCK - 1), -1).reshape(per_range, BLOCK)
    hot = (own_place[:, :, None] == jnp.arange(BLOCK, dtype=jnp.int32)).astype(jnp.float32)
    result = -jnp.einsum(
        "iuo,ion->iun", hot, summed.reshape(per_range, BLOCK, cols), precision=lax.Precision.HIGHEST
    )
    result, sums = lax.optimization_barrier((result, sums))
    marginal = pivot_variance + jnp.sum(sums, axis=0, keepdims=True)
    return result.reshape(1, rows, cols), marginal


def solution(mesh):
    split = Mesh(mesh.devices.reshape(2, 4, 4, 2, 8), ("zh", "y", "x", "core", "zl"))
    leaf, row, col = ("zh", "y"), ("x", "core"), "zl"
    return jax.shard_map(
        per_device,
        mesh=split,
        in_specs=(P(row, ("zh", "y", "zl")), P(), P(leaf, row, col), P(leaf, col)),
        out_specs=(P(leaf, row, col), P(leaf, col)),
        check_vma=False,
    )
```

```python
import functools

import jax
import jax.numpy as jnp
from jax import lax
from jax.experimental import pallas as pl
from jax.experimental.pallas import tpu as pltpu
from jax.sharding import Mesh, PartitionSpec as P

BLOCK = 128
PART = 256
SLOTS = 4
VMEM_BYTES = 24 * 1024 * 1024
CORES = [(0, 1), (1, 0)]
SPREAD_X = (
    (3, 1, 0, 0),
    (0, 3, 0, 1),
    (1, 2, 0, 1),
    (2, 0, 1, 1),
    (2, 2, 1, 3),
    (3, 1, 2, 2),
    (3, 0, 2, 3),
    (3, 2, 3, 0),
)


def shift(size, step):
    return [(i, (i + step) % size) for i in range(size)]


def opposite(size, way=1):
    return [
        (2 * i + c, (i + way * (1 - 2 * c)) % size * 2 + c) for i in range(size) for c in range(2)
    ]


def spread_plan():
    pairs, holds, taken = [], {}, {}
    for y in range(4):
        for r in range(8):
            to = (SPREAD_X[r][y], r % 4)
            core = taken.get(to, 0)
            taken[to] = core + 1
            pairs.append(((y * 4 + r // 2) * 2 + r % 2, (to[1] * 4 + to[0]) * 2 + core))
            holds[(to[1], to[0], core)] = (r // 4, y)
    return pairs, holds


def piece_plan(holds):
    halves, found = [], []
    for y in range(4):
        for x in range(4):
            for c in range(2):
                d = 2 * c - 1
                at = [
                    (x, c),
                    (x, 1 - c),
                    (x + d, c),
                    (x + d, 1 - c),
                    (x + 2, c),
                    (x - d, 1 - c),
                    (x - d, c),
                    (x + 2, 1 - c),
                ]
                has = [holds[(y, px % 4, pc)] for px, pc in at]
                halves.append([h * 4 + k for h, k in has])
                found.append([[has.index((0, k)), has.index((1, k))] for k in range(4)])
    return [jnp.array(v, jnp.int32) for v in (halves, found)]


def spread_kernel(start_row, rows_ref, *rest):
    pieces = rest[:-7]
    high_hbm, low_hbm, z_f, z_h, z_l, in_sem, out_sem = rest[-7:]
    slots, rows = z_f.shape[:2]

    def fetch(i):
        return pltpu.make_async_copy(pieces[i], z_f.at[i % slots], in_sem.at[i])

    def store(i):
        return [
            pltpu.make_async_copy(z_h.at[i % slots], high_hbm.at[i], out_sem.at[2 * i]),
            pltpu.make_async_copy(z_l.at[i % slots], low_hbm.at[i], out_sem.at[2 * i + 1]),
        ]

    for i in range(slots):
        fetch(i).start()
    row = lax.broadcasted_iota(jnp.int32, (BLOCK, BLOCK), 0)
    for at in range(len(pieces)):
        fetch(at).wait()
        if at >= slots:
            for copy in store(at - slots):
                copy.wait()

        def one(i, carry, at=at):
            here = pl.ds(pl.multiple_of(i * BLOCK, BLOCK), BLOCK)
            value = z_f[at % slots, here, :]
            high = value.astype(jnp.bfloat16)
            low = (value - high.astype(jnp.float32)).astype(jnp.bfloat16)
            place = rows_ref[pl.ds(start_row[at] + i, 1), :]
            place = jnp.where(place >= 0, place & (BLOCK - 1), -1)
            hot = (place == row).astype(jnp.float32).astype(jnp.bfloat16)
            z_h[at % slots, here, :] = jnp.dot(
                hot, high, preferred_element_type=jnp.float32
            ).astype(jnp.bfloat16)
            z_l[at % slots, here, :] = jnp.dot(
                hot, low, preferred_element_type=jnp.float32
            ).astype(jnp.bfloat16)
            return carry

        lax.fori_loop(0, rows // BLOCK, one, 0, unroll=3)
        for copy in store(at):
            copy.start()
        if at + slots < len(pieces):
            fetch(at + slots).start()
    for at in range(len(pieces) - slots, len(pieces)):
        for copy in store(at):
            copy.wait()


def spread(start_row, root_row, pieces):
    rows, cols = pieces[0].shape
    any_spec = pl.BlockSpec(memory_space=pl.ANY)
    shape = (len(pieces), rows, cols)
    held = (SLOTS, rows, cols)
    return pl.pallas_call(
        spread_kernel,
        out_shape=[pltpu.HBM(shape, jnp.bfloat16)] * 2,
        in_specs=[
            pl.BlockSpec(memory_space=pltpu.SMEM),
            pl.BlockSpec(memory_space=pltpu.VMEM),
        ]
        + [any_spec] * len(pieces),
        out_specs=[pl.BlockSpec(memory_space=pltpu.HBM)] * 2,
        scratch_shapes=[
            pltpu.VMEM(held, jnp.float32),
            pltpu.VMEM(held, jnp.bfloat16),
            pltpu.VMEM(held, jnp.bfloat16),
            pltpu.SemaphoreType.DMA((len(pieces),)),
            pltpu.SemaphoreType.DMA((2 * len(pieces),)),
        ],
        compiler_params=pltpu.CompilerParams(vmem_limit_bytes=VMEM_BYTES),
        cost_estimate=pl.CostEstimate(
            flops=10 * 4 * rows * BLOCK * cols, bytes_accessed=80 * rows * cols, transcendentals=0
        ),
    )(start_row, root_row, *pieces)


def product_kernel(calls, table, root_hbm, high_hbm, low_hbm, *rest):
    outs = rest[: len(calls)]
    a_f, z_h, z_l, a_sem, z_sem = rest[len(calls) :]
    rows = outs[0].shape[0]
    per_range = rows // BLOCK
    per_part = PART // BLOCK
    parts = rows // PART
    children = [table[call, 3 * per_range + 2] for call in calls]

    def factor_copies(i, source, target, first):
        return [
            pltpu.make_async_copy(
                source.at[table[children[i], 3 * per_range + side]],
                target.at[i, pl.ds(side * rows, rows)],
                z_sem.at[i, first + side],
            )
            for side in range(2)
        ]

    def start_root(i, part):
        for m in range(per_part):
            mb = pl.multiple_of(table[children[i], part * per_part + m] * BLOCK, BLOCK)
            pltpu.make_async_copy(
                root_hbm.at[:, pl.ds(mb, BLOCK)],
                a_f.at[i, part, :, pl.ds(m * BLOCK, BLOCK)],
                a_sem.at[i, part],
            ).start()

    highs_in = [factor_copies(i, high_hbm, z_h, 0) for i in range(len(calls))]
    lows_in = [factor_copies(i, low_hbm, z_l, 2) for i in range(len(calls))]

    def begin(i):
        start_root(i, 0)
        for copy in highs_in[i] + lows_in[i]:
            copy.start()
        start_root(i, 1)

    begin(0)
    for i, out in enumerate(outs):
        for part in range(parts):
            pltpu.make_async_copy(a_f.at[i, part], a_f.at[i, part], a_sem.at[i, part]).wait()
            if part == 0:
                for copy in highs_in[i]:
                    copy.wait()
            if part + 2 < parts:
                start_root(i, part + 2)
            elif part + 2 == parts and i + 1 < len(calls):
                begin(i + 1)
            highs, lows = [], []
            for k in range(2 * per_range):
                value = a_f[i, part, table[children[i], per_range + k]]
                high = value.astype(jnp.bfloat16)
                highs.append(high)
                lows.append((value - high.astype(jnp.float32)).astype(jnp.bfloat16))
            high = jnp.concatenate(highs, axis=1)
            low = jnp.concatenate(lows, axis=1)
            value = jnp.dot(high, z_h[i], preferred_element_type=jnp.float32)
            value = value + jnp.dot(low, z_h[i], preferred_element_type=jnp.float32)
            if part == 0:
                for copy in lows_in[i]:
                    copy.wait()
            value = value + jnp.dot(high, z_l[i], preferred_element_type=jnp.float32)
            out[part * PART : (part + 1) * PART, :] = value


def product(calls, table, root, high, low):
    rows, cols = high.shape[1:]
    n = len(calls)
    any_spec = pl.BlockSpec(memory_space=pl.ANY)
    root, high, low = [pltpu.with_memory_space_constraint(v, pltpu.HBM) for v in (root, high, low)]
    return pl.pallas_call(
        functools.partial(product_kernel, calls),
        out_shape=[jax.ShapeDtypeStruct((rows, cols), jnp.float32)] * n,
        in_specs=[pl.BlockSpec(memory_space=pltpu.SMEM)] + [any_spec] * 3,
        out_specs=[pl.BlockSpec(memory_space=pltpu.VMEM)] * n,
        scratch_shapes=[
            pltpu.VMEM((n, rows // PART, root.shape[0], PART, BLOCK), jnp.float32),
            pltpu.VMEM((n, 2 * rows, cols), jnp.bfloat16),
            pltpu.VMEM((n, 2 * rows, cols), jnp.bfloat16),
            pltpu.SemaphoreType.DMA((n, rows // PART)),
            pltpu.SemaphoreType.DMA((n, 4)),
        ],
        compiler_params=pltpu.CompilerParams(vmem_limit_bytes=(12 + 14 * n) * 1024 * 1024),
        cost_estimate=pl.CostEstimate(
            flops=n * 3 * 2 * rows * 2 * rows * cols,
            bytes_accessed=n * 12 * rows * rows,
            transcendentals=0,
        ),
    )(table, root, high, low)


def weigh_kernel(piece, first, second, high_hbm, low_hbm, total, sums, high, low, sem):
    rows, cols = total.shape
    copies = [
        pltpu.make_async_copy(high_hbm.at[piece], high, sem.at[0]),
        pltpu.make_async_copy(low_hbm.at[piece], low, sem.at[1]),
    ]
    for copy in copies:
        copy.start()
    for copy in copies:
        copy.wait()

    def one(i, found):
        at = pl.ds(pl.multiple_of(i * 64, 64), 64)
        value = first[at, :] + second[at, :]
        total[at, :] = value
        factor = high[at, :].astype(jnp.float32) + low[at, :].astype(jnp.float32)
        return found + jnp.sum((factor * value).reshape(8, 8, cols), axis=0)

    found = lax.fori_loop(0, rows // 64, one, jnp.zeros((8, cols), jnp.float32))
    sums[...] = jnp.sum(found, axis=0, keepdims=True)


def weigh(piece, first, second, high, low):
    rows, cols = first.shape
    any_spec = pl.BlockSpec(memory_space=pl.ANY)
    vmem = pl.BlockSpec(memory_space=pltpu.VMEM)
    high, low = [pltpu.with_memory_space_constraint(v, pltpu.HBM) for v in (high, low)]
    return pl.pallas_call(
        functools.partial(weigh_kernel, piece),
        out_shape=[
            jax.ShapeDtypeStruct((rows, cols), jnp.float32),
            jax.ShapeDtypeStruct((1, cols), jnp.float32),
        ],
        in_specs=[vmem, vmem, any_spec, any_spec],
        out_specs=[vmem, vmem],
        scratch_shapes=[
            pltpu.VMEM((rows, cols), jnp.bfloat16),
            pltpu.VMEM((rows, cols), jnp.bfloat16),
            pltpu.SemaphoreType.DMA((2,)),
        ],
        compiler_params=pltpu.CompilerParams(vmem_limit_bytes=VMEM_BYTES),
        cost_estimate=pl.CostEstimate(
            flops=4 * rows * cols, bytes_accessed=16 * rows * cols, transcendentals=0
        ),
    )(first, second, high, low)


def select_kernel(place_ref, first, second, out):
    row = lax.broadcasted_iota(jnp.int32, (BLOCK, BLOCK), 0)
    for i in range(out.shape[0] // BLOCK):
        here = pl.ds(i * BLOCK, BLOCK)
        value = -(first[here, :] + second[here, :])
        high = value.astype(jnp.bfloat16)
        low = (value - high.astype(jnp.float32)).astype(jnp.bfloat16)
        hot = (place_ref[i : i + 1, :] == row).astype(jnp.float32).T.astype(jnp.bfloat16)
        found = jnp.dot(hot, low, preferred_element_type=jnp.float32)
        out[here, :] = found + jnp.dot(hot, high, preferred_element_type=jnp.float32)


def select(place, first, second):
    rows, cols = first.shape
    vmem = pl.BlockSpec(memory_space=pltpu.VMEM)
    return pl.pallas_call(
        select_kernel,
        out_shape=jax.ShapeDtypeStruct((rows, cols), jnp.float32),
        in_specs=[vmem] * 3,
        out_specs=vmem,
        compiler_params=pltpu.CompilerParams(vmem_limit_bytes=VMEM_BYTES),
        cost_estimate=pl.CostEstimate(
            flops=4 * rows * BLOCK * cols, bytes_accessed=12 * rows * cols, transcendentals=0
        ),
    )(place, first, second)


def per_device(root_inverse, root_row, coupling, pivot_variance):
    zh = lax.axis_index("zh")
    y = lax.axis_index("y")
    x = lax.axis_index("x")
    core = lax.axis_index("core")
    rows, cols = coupling.shape[1:]
    ranges = root_row.shape[1] // rows
    per_range = rows // BLOCK
    own_range = 2 * x + core
    device = (y * 4 + x) * 2 + core

    root = lax.all_gather(root_inverse, ("zh", "zl"), axis=0, tiled=False)

    pairs, holds = spread_plan()
    halves, found = piece_plan(holds)
    spots = lax.dynamic_slice(halves, (device, 0), (1, 8))[0]
    child = zh * 4 + jnp.concatenate([spots & 3, jnp.stack([y, (y + 1 - 2 * core) & 3])])
    ranged = jnp.concatenate([y + 4 * (spots >> 2), jnp.stack([own_range, own_range])])
    start_row = (child * ranges + ranged) * per_range
    block = (root_row[:, ::BLOCK] >> 7).reshape(-1, ranges, per_range)

    def blocks_of(r):
        return lax.dynamic_slice(block, (zh * 4, r, 0), (4, 1, per_range))[:, 0] & 7

    order = (y + jnp.stack([2, 3 - 2 * core, 1 + 2 * core, 0])) & 3
    table = jnp.concatenate(
        [
            blocks_of(own_range),
            blocks_of(y),
            blocks_of(y + 4) + 8,
            lax.dynamic_slice(found, (device, 0, 0), (1, 4, 2))[0],
            order[:, None],
        ],
        axis=1,
    ).astype(jnp.int32)
    own = lax.ppermute(coupling[0], ("y", "x", "core"), pairs)
    rows_of = root_row.reshape(-1, BLOCK)
    own, table, start_row, rows_of = lax.optimization_barrier((own, table, start_row, rows_of))
    along_x = opposite(4)
    beside = lax.ppermute(own, "core", CORES)
    near = lax.ppermute(own, ("x", "core"), along_x)
    near_beside = lax.ppermute(beside, ("x", "core"), along_x)
    far = lax.ppermute(near, ("x", "core"), along_x)
    pieces = [own, beside, near, near_beside, far]
    pieces += [lax.ppermute(p, "core", CORES) for p in (near, near_beside, far)]
    pieces += [coupling[0], lax.ppermute(coupling[0], ("y", "core"), opposite(4, -1))]
    high, low = spread(start_row, rows_of, pieces)

    root = root.reshape(-1, *root_inverse.shape)
    (far,) = product((0,), table, root, high, low)
    passed = lax.ppermute(far, ("y", "core"), opposite(4))
    second, first = product((2, 1), table, root, high, low)
    back = lax.ppermute(first, ("y", "core"), opposite(4, -1))
    last, last_sums = weigh(9, second, passed, high, low)
    last_sums = lax.ppermute(last_sums, ("y", "core"), opposite(4))
    table, last, last_sums = lax.optimization_barrier((table, last, last_sums))
    forth = lax.ppermute(last, ("y", "core"), opposite(4))
    (home,) = product((3,), table, root, high, low)
    kept, sums = weigh(8, home, back, high, low)
    sums = jnp.broadcast_to(sums + last_sums, (8, cols))
    kept, sums = lax.optimization_barrier((kept, sums))
    sums = lax.all_to_all(sums, ("x", "core"), split_axis=0, concat_axis=0, tiled=True)
    own_place = lax.dynamic_slice(root_row, (zh * 4 + y, own_range * rows), (1, rows))[0]
    own_place = jnp.where(own_place >= 0, own_place & (BLOCK - 1), -1).reshape(per_range, BLOCK)
    result = select(own_place, kept, forth)

    result, sums = lax.optimization_barrier((result, sums))
    marginal = pivot_variance + jnp.sum(sums, axis=0, keepdims=True)
    return result.reshape(1, rows, cols), marginal


def solution(mesh):
    split = Mesh(mesh.devices.reshape(2, 4, 4, 2, 8), ("zh", "y", "x", "core", "zl"))
    leaf, row, col = ("zh", "y"), ("x", "core"), "zl"
    return jax.shard_map(
        per_device,
        mesh=split,
        in_specs=(P(row, ("zh", "y", "zl")), P(), P(leaf, row, col), P(leaf, col)),
        out_specs=(P(leaf, row, col), P(leaf, col)),
        check_vma=False,
    )
```
